128 devices in a mesh: span: 16 (over x_lo, y, core), uly: 8 (over z, x_hi).
Axes of the slice: x: 4 (x_hi: 2, x_lo: 2; x = x_hi * 2 + x_lo), y: 4, z: 4, core: 2. Of those that a mesh axis runs over, the one named last changes fastest.
Arguments:
- hidden_in: bfloat16 [8192, 6144], P('span'), may hold values from -14 to 14
- span_ids: int32 [8192], replicated, may hold values from 0 to 15, as said below
- w_query: bfloat16 [6144, 6144], P('span', 'uly'), may hold values from -0.078125 to 0.078125
- w_keyval: bfloat16 [6144, 2, 1024], P('span', None, 'uly'), may hold values from -0.078125 to 0.078125
- w_out: bfloat16 [6144, 6144], P('uly', 'span'), may hold values from -0.078125 to 0.078125
Outputs:
- attended: bfloat16 [8192, 6144], P(('span', 'uly'))
The draws below stay inside these ranges and needn't reach their ends.
Inputs may be any that keep to these rules, and one draw needn't show every extreme that they name: `span_ids`: each aligned block of 512 tokens carries one span id, and the 16 blocks carry distinct ids.
All inputs are finite; a program needn't handle non-finite values.
Results may differ from the reference program's by a relative error of at most 0.02.
Values may be sent and summed in bfloat16 or wider, within the bound.
No kernel may reach another device: no remote copies, remote signals or barrier semaphores. Data moves between devices by JAX's collectives and lax.ppermute only.
A program may use at most 128 MiB of HBM per device.

```python
import math
import jax
import jax.numpy as jnp
from jax import lax

D = 6144
HEADS = 48
KV_HEADS = 8
HEAD = 128
TOK_SPAN = 512
SPANS = 16
TOKENS = 8192
GROUP_HEADS = 6
N_ULY = 8


def draw_hidden_in(key, part):
    key = jax.random.fold_in(key, 11)
    first_key = jax.random.fold_in(key, 0)
    values = jnp.clip(jax.random.normal(first_key, (TOKENS, D), jnp.float32), -6.0, 6.0)
    return values.astype(jnp.bfloat16)


def draw_span_ids(key, part):
    key = jax.random.fold_in(key, 5)
    order = jax.random.permutation(key, SPANS)
    return jnp.repeat(order, TOK_SPAN).astype(jnp.int32)


def level_of(stream_key, dims, cuts, smallest, high):
    def one(axis_at, blocks):
        heights = jax.random.uniform(jax.random.fold_in(jax.random.fold_in(stream_key, 6), axis_at), (blocks,), jnp.float32, smallest / len(cuts), high / len(cuts))
        return jnp.repeat(jnp.exp(heights), dims[axis_at] // blocks).reshape((-1,) + (1,) * (len(dims) - axis_at - 1))

    factor_of = one(*cuts[0])
    for cut in cuts[1:]:
        factor_of = factor_of * one(*cut)
    return factor_of


def scatter_about(rng, shape, scale, limit, cuts=(), kind=jnp.bfloat16):
    array = scale * jax.random.normal(rng, shape, jnp.float32)
    if cuts:
        array = array * level_of(rng, shape, cuts, -0.22, 0.18)
    return jnp.clip(array, -limit, limit).astype(kind)


def setup_inputs(seed: int = 0) -> dict:
    key_of = jax.random.split(jax.random.key(seed), 6)
    hidden_in = draw_hidden_in(jax.random.fold_in(key_of[5], 71), 0)
    span_ids = draw_span_ids(jax.random.fold_in(key_of[5], 71), 0)
    w_query = scatter_about(key_of[2], (D, HEADS * HEAD), D ** -0.5, 0.078125, ((0, 16), (1, 8)))
    w_keyval = scatter_about(key_of[3], (D, 2, KV_HEADS * HEAD), D ** -0.5, 0.078125, ((0, 16), (2, 8)))
    w_out = scatter_about(key_of[4], (HEADS * HEAD, D), (HEADS * HEAD) ** -0.5, 0.078125, ((0, 8), (1, 16)))
    return {"hidden_in": hidden_in, "span_ids": span_ids, "w_query": w_query, "w_keyval": w_keyval, "w_out": w_out}


NEG_LARGE = -1e+30

def reference(hidden_in, span_ids, w_query, w_keyval, w_out):
    group_size = HEADS // KV_HEADS
    scale_factor = 1.0 / math.sqrt(HEAD)
    queries = jnp.dot(hidden_in, w_query, preferred_element_type=jnp.float32).astype(jnp.bfloat16)
    flat_pair = w_keyval.reshape(D, 2 * KV_HEADS * HEAD)
    keyval = jnp.dot(hidden_in, flat_pair, preferred_element_type=jnp.float32).astype(jnp.bfloat16)
    keyval = keyval.reshape(TOKENS, 2, KV_HEADS, HEAD)
    keys = keyval[:, 0]
    values = keyval[:, 1]
    visible = span_ids[None, :] <= span_ids[:, None]

    def one_head(head):
        query_head = lax.dynamic_slice_in_dim(queries, head * HEAD, HEAD, 1)
        kv_index = head // group_size
        key_head = lax.dynamic_index_in_dim(keys, kv_index, 1, keepdims=False)
        value_head = lax.dynamic_index_in_dim(values, kv_index, 1, keepdims=False)
        scores = jnp.dot(query_head, key_head.T, preferred_element_type=jnp.float32) * scale_factor
        scores = jnp.where(visible, scores, NEG_LARGE)
        best = lax.optimization_barrier(jnp.max(scores, axis=-1, keepdims=True))
        probs = jnp.where(visible, jnp.exp(scores - best), 0.0)
        totals = lax.optimization_barrier(jnp.sum(probs, axis=-1, keepdims=True))
        mixed = jnp.dot(probs.astype(jnp.bfloat16), value_head, preferred_element_type=jnp.float32)
        return (mixed / totals).astype(jnp.bfloat16)
    attention = lax.map(one_head, jnp.arange(HEADS, dtype=jnp.int32))
    shaped_out = w_out.reshape(HEADS, HEAD, D)
    summed = jnp.zeros((TOKENS, D), jnp.float32)
    for group in range(N_ULY):
        lower = group * GROUP_HEADS
        group_term = jnp.einsum('htd,hdn->tn', attention[lower:lower + GROUP_HEADS].astype(jnp.float32), shaped_out[lower:lower + GROUP_HEADS].astype(jnp.float32))
        rounded = lax.optimization_barrier(group_term.astype(jnp.bfloat16))
        summed = summed + rounded.astype(jnp.float32)
    return summed.astype(jnp.bfloat16)
```

```python
import functools
import math

import jax
import jax.numpy as jnp
from jax import lax
from jax.experimental import pallas as pl
from jax.experimental.pallas import tpu as pltpu
from jax.sharding import PartitionSpec as P

HEADS = 48
HEAD = 128
D = 6144
SPANS = 16
TOK = 512
SHARD = D // SPANS
GROUP = 3
GCOLS = GROUP * HEAD
SCALE2 = math.log2(math.e) / math.sqrt(HEAD)
SAFE_EXPONENT = 90.0
NEG_LARGE = -1e30
BOTH = ("span", "uly")
F32 = jnp.float32
BF16 = jnp.bfloat16


def coords(index):
    span, uly = index // 8, index % 8
    return span // 8, (span // 2) % 4, span % 2, uly // 2, uly % 2


def index_of(xl, y, c, z, xh):
    return (xl * 8 + y * 2 + c) * 8 + z * 2 + xh


def move(array, dx=0, dy=0, dz=0, swap_xl=False, swap_xh=False, swap_c=False):
    pairs = []
    for source in range(128):
        xl, y, c, z, xh = coords(source)
        x = (xh * 2 + xl + dx) % 4
        xh, xl = x // 2, x % 2
        if swap_xl:
            xl = 1 - xl
        if swap_xh:
            xh = 1 - xh
        if swap_c:
            c = 1 - c
        pairs.append((source, index_of(xl, (y + dy) % 4, c, (z + dz) % 4, xh)))
    return lax.ppermute(array, BOTH, pairs)


def gather_x_first(own):
    half = own.shape[0] // 2
    side = move(own, swap_xl=True)
    up, down = move(own, dy=1), move(own, dy=-1)
    side_up, side_down = move(side, dy=1), move(side, dy=-1)
    far = move(up[:half], dy=1), move(down[half:], dy=-1)
    side_far = move(side_up[:half], dy=1), move(side_down[half:], dy=-1)
    return [own, side, up, side_up, down, side_down, *far, *side_far]


def gather_y_first(own):
    half = own.shape[0] // 2
    up, down = move(own, dy=1), move(own, dy=-1)
    side = move(own, swap_xl=True)
    far = move(up[:half], dy=1), move(down[half:], dy=-1)
    side_up, side_down = move(up, swap_xl=True), move(down, swap_xl=True)
    side_far = move(far[0], swap_xl=True), move(far[1], swap_xl=True)
    return [own, side, up, side_up, down, side_down, *far, *side_far]


def pick_kernel(which, hidden_ref, out_ref):
    out_ref[...] = hidden_ref[...]


def pick_columns(hidden, which):
    return pl.pallas_call(
        pick_kernel,
        grid_spec=pltpu.PrefetchScalarGridSpec(
            num_scalar_prefetch=1,
            grid=(8,),
            in_specs=[pl.BlockSpec((TOK, SHARD), lambda i, which: (0, which[i]))],
            out_specs=pl.BlockSpec((TOK, SHARD), lambda i, which: (0, i)),
        ),
        out_shape=jax.ShapeDtypeStruct((TOK, 8 * SHARD), BF16),
        cost_estimate=pl.CostEstimate(flops=0, bytes_accessed=4 * TOK * 8 * SHARD, transcendentals=0),
    )(which, hidden)


def project_kernel(which, own_ref, other_ref, *refs):
    pieces, (own_out, other_out, weight) = refs[:10], refs[10:]
    step = pl.program_id(0)
    half = SHARD // 2
    for at in range(6):
        @pl.when(step == at)
        def _():
            weight[...] = pieces[at][...]
    for at in range(2):
        @pl.when(step == 6 + at)
        def _():
            weight[:half] = pieces[6 + 2 * at][...]
            weight[half:] = pieces[7 + 2 * at][...]

    @pl.when(step == 0)
    def _():
        own_out[...] = jnp.zeros_like(own_out)
        other_out[...] = jnp.zeros_like(other_out)

    own_out[...] += jnp.dot(own_ref[...], weight[...], preferred_element_type=F32)
    other_out[...] += jnp.dot(other_ref[...], weight[...], preferred_element_type=F32)


def project(hidden, other, which, pieces):
    cols = pieces[0].shape[1]
    whole = lambda rows: pl.BlockSpec((rows, cols), lambda i, which: (0, 0))
    out = jax.ShapeDtypeStruct((TOK, cols), F32)
    return pl.pallas_call(
        project_kernel,
        grid_spec=pltpu.PrefetchScalarGridSpec(
            num_scalar_prefetch=1,
            grid=(8,),
            in_specs=[
                pl.BlockSpec((TOK, SHARD), lambda i, which: (0, which[i])),
                pl.BlockSpec((TOK, SHARD), lambda i, which: (0, which[8 + i])),
                *[whole(piece.shape[0]) for piece in pieces],
            ],
            out_specs=[whole(TOK), whole(TOK)],
            scratch_shapes=[pltpu.VMEM((SHARD, cols), BF16)],
        ),
        out_shape=[out, out],
        compiler_params=pltpu.CompilerParams(vmem_limit_bytes=40 * 2**20),
        cost_estimate=pl.CostEstimate(
            flops=4 * TOK * 8 * SHARD * cols, bytes_accessed=12 * 2**20, transcendentals=0
        ),
    )(which, hidden, other, *pieces)


def attend_kernel(flags, first_ref, second_ref, pair_ref, mine_ref, send_ref, query, value, accum, best):
    query[...] = (first_ref[...] + second_ref[...]).astype(BF16)
    value[:, HEAD:] = jnp.ones((SPANS * TOK, HEAD), BF16)
    accum[...] = jnp.zeros_like(accum)
    ones = jnp.ones((HEAD, HEAD), BF16)

    def prepare(block, largest):
        rows = pl.ds(pl.multiple_of(block * TOK, TOK), TOK)
        value[rows, :HEAD] = pair_ref[rows, HEAD:]
        key = pair_ref[rows, :HEAD]
        norms = jnp.dot(key * key, ones, preferred_element_type=F32)
        return jnp.maximum(largest, jnp.max(norms.reshape(TOK // 8, 8, HEAD), axis=0))

    key_norm = jnp.max(lax.fori_loop(0, SPANS, prepare, jnp.zeros((8, HEAD), F32)))
    query_norm = jnp.zeros((8, HEAD), F32)
    for head in range(GROUP):
        block = query[:, head * HEAD : (head + 1) * HEAD]
        norms = jnp.dot(block * block, ones, preferred_element_type=F32)
        query_norm = jnp.maximum(query_norm, jnp.max(norms.reshape(TOK // 8, 8, HEAD), axis=0))
    bound = key_norm * jnp.max(query_norm) * (1.03 * SCALE2 * SCALE2)
    small = bound <= SAFE_EXPONENT * SAFE_EXPONENT

    @pl.when(small)
    def _():
        def step(block, carry):
            @pl.when(flags[block] > 0)
            def _():
                rows = pl.ds(pl.multiple_of(block * TOK, TOK), TOK)
                key, extended = pair_ref[rows, :HEAD], value[rows, :]
                for head in range(GROUP):
                    scores = lax.dot_general(
                        query[:, head * HEAD : (head + 1) * HEAD],
                        key,
                        (((1,), (1,)), ((), ())),
                        preferred_element_type=F32,
                    )
                    probs = jnp.exp2(scores * SCALE2).astype(BF16)
                    accum[head] += jnp.dot(probs, extended, preferred_element_type=F32)

            return carry

        lax.fori_loop(0, SPANS, step, 0)

    @pl.when(jnp.logical_not(small))
    def _():
        best[...] = jnp.full_like(best, NEG_LARGE)

        def step(at, carry):
            block, head = at // GROUP, at % GROUP

            @pl.when(flags[block] > 0)
            def _():
                rows = pl.ds(pl.multiple_of(block * TOK, TOK), TOK)
                columns = pl.ds(pl.multiple_of(head * HEAD, HEAD), HEAD)
                scores = lax.dot_general(
                    query[:, columns],
                    pair_ref[rows, :HEAD],
                    (((1,), (1,)), ((), ())),
                    preferred_element_type=F32,
                )
                old = best[head]
                new = jnp.maximum(old, jnp.max(scores, axis=1, keepdims=True))
                best[head] = new
                probs = jnp.exp2((scores - new[:, :1]) * SCALE2).astype(BF16)
                factor = jnp.exp2((old - new) * SCALE2)
                accum[head] = accum[head] * factor[:, :1] + jnp.dot(
                    probs, value[rows, :], preferred_element_type=F32
                )

            return carry

        lax.fori_loop(0, SPANS * GROUP, step, 0)

    side = flags[SPANS]
    for head in range(GROUP):
        columns = slice(head * HEAD, (head + 1) * HEAD)
        for at in range(4):
            for out_ref, chosen in ((mine_ref, side), (send_ref, 1 - side)):
                rows = pl.ds(pl.multiple_of(at * 128 + chosen * 64, 64), 64)
                mixed = accum[head, rows, :]
                out_ref[at * 64 : at * 64 + 64, columns] = (mixed[:, :HEAD] / mixed[:, HEAD:]).astype(BF16)


def attend(flags, first, second, pair):
    out = jax.ShapeDtypeStruct((TOK // 2, GCOLS), BF16)
    return pl.pallas_call(
        attend_kernel,
        in_specs=[pl.BlockSpec(memory_space=pltpu.SMEM)] + [pl.BlockSpec(memory_space=pltpu.VMEM)] * 3,
        out_specs=[pl.BlockSpec(memory_space=pltpu.VMEM)] * 2,
        out_shape=[out, out],
        scratch_shapes=[
            pltpu.VMEM((TOK, GCOLS), BF16),
            pltpu.VMEM((SPANS * TOK, 2 * HEAD), BF16),
            pltpu.VMEM((GROUP, TOK, 2 * HEAD), F32),
            pltpu.VMEM((GROUP, TOK, HEAD), F32),
        ],
        compiler_params=pltpu.CompilerParams(vmem_limit_bytes=48 * 2**20),
        cost_estimate=pl.CostEstimate(
            flops=GROUP * 6 * TOK * SPANS * TOK * HEAD, bytes_accessed=6 * 2**20, transcendentals=0
        ),
    )(flags, first, second, pair)


Z_ORDER = (2, 1, 3, 0)


def output_kernel(place, *refs):
    own, other = refs[0:2], refs[2:4]
    weights = refs[4:20]
    far_a, far_b, up, down, stay, rows_of = refs[20:]
    core, z = place[0], place[1]
    for side in range(2):
        chosen = place[2 + side]
        for group in range(2):
            for at, step in enumerate(Z_ORDER):
                rows = pl.ds(pl.multiple_of(chosen * 256 + ((z + step) % 4) * 64, 64), 64)
                a, b = own[group][rows, :], other[group][rows, :]
                first = core == 0
                rows_of[side * 2 + group, at * 128 : at * 128 + 64, :] = jnp.where(first, a, b)
                rows_of[side * 2 + group, at * 128 + 64 : at * 128 + 128, :] = jnp.where(first, b, a)
    for dy in range(4):
        total = jnp.dot(rows_of[0], weights[dy * 4][...], preferred_element_type=F32)
        for at in range(1, 4):
            total += jnp.dot(rows_of[at], weights[dy * 4 + at][...], preferred_element_type=F32)
        total = total.astype(BF16)
        columns = slice(dy * SHARD, (dy + 1) * SHARD)
        far_a[:, columns] = total[:64]
        far_b[:, columns] = total[64:128]
        up[:, columns] = total[128:256]
        down[:, columns] = total[256:384]
        stay[:, columns] = total[384:]


def output_partial(place, own, other, weights):
    whole = pl.BlockSpec(memory_space=pltpu.VMEM)
    shapes = [jax.ShapeDtypeStruct((rows, 4 * SHARD), BF16) for rows in (64, 64, 128, 128, 128)]
    return pl.pallas_call(
        output_kernel,
        grid=(1,),
        in_specs=[pl.BlockSpec(memory_space=pltpu.SMEM)]
        + [whole] * 4
        + [pl.BlockSpec((SHARD, SHARD), lambda i, block=block: (block, 0)) for _, block in weights],
        out_specs=[whole] * 5,
        out_shape=shapes,
        scratch_shapes=[pltpu.VMEM((4, TOK, SHARD), BF16)],
        compiler_params=pltpu.CompilerParams(vmem_limit_bytes=40 * 2**20),
        cost_estimate=pl.CostEstimate(
            flops=2 * TOK * 4 * SHARD * 4 * SHARD, bytes_accessed=8 * 2**20, transcendentals=0
        ),
    )(place, *own, *other, *[array for array, _ in weights])


def assemble_kernel(place, same_ref, cross_ref, got_same, got_cross, out_ref):
    core = place[0]
    keep = pl.ds(pl.multiple_of(core * 64, 64), 64)
    for at, (mine, got) in enumerate(((same_ref, got_same), (cross_ref, got_cross))):
        for dy in range(4):
            span_pair = place[1 + at * 4 + dy]
            columns = slice(dy * SHARD, (dy + 1) * SHARD)
            to = pl.ds(pl.multiple_of((span_pair * 2 + core) * SHARD, 128), SHARD)
            out_ref[:, to] = mine[keep, columns]
            to = pl.ds(pl.multiple_of((span_pair * 2 + 1 - core) * SHARD, 128), SHARD)
            out_ref[:, to] = got[:, columns]


def assemble(place, same, cross, got_same, got_cross):
    whole = pl.BlockSpec(memory_space=pltpu.VMEM)
    return pl.pallas_call(
        assemble_kernel,
        in_specs=[pl.BlockSpec(memory_space=pltpu.SMEM)] + [whole] * 4,
        out_specs=whole,
        out_shape=jax.ShapeDtypeStruct((64, D), BF16),
    )(place, same, cross, got_same, got_cross)


def reduce_over_z(far_a, far_b, up, down, stay):
    got_a, got_b = move(far_a, dz=1), move(far_b, dz=-1)
    add = lambda a, b: (a.astype(F32) + b.astype(F32)).astype(BF16)
    up = jnp.concatenate([add(up[:64], got_a), up[64:]], axis=0)
    down = jnp.concatenate([down[:64], add(down[64:], got_b)], axis=0)
    below, above = move(up, dz=1), move(down, dz=-1)
    return (stay.astype(F32) + below.astype(F32) + above.astype(F32)).astype(BF16)


def per_device(hidden, span_ids, w_query, w_keyval, w_out):
    span, uly = lax.axis_index("span"), lax.axis_index("uly")
    xl, y, core = span // 8, (span // 2) % 4, span % 2
    z, xh = uly // 2, uly % 2
    as_int = lambda values: jnp.stack([jnp.asarray(v, jnp.int32) for v in values])

    everywhere = [j * 2 + 1 - core for j in range(8)]
    other_hidden = move(pick_columns(hidden, as_int(everywhere)), swap_c=True)
    chips = [x * 4 + (y + dy) % 4 for dy in (0, 3, 1, 2) for x in (xl, 1 - xl)]
    which = as_int([j * 2 + core for j in chips] + chips)

    pair_shard = jnp.concatenate([w_keyval[:, 0], w_keyval[:, 1]], axis=1)
    pair_own, pair_other = project(hidden, other_hidden, which, gather_x_first(pair_shard))
    keyval = (pair_own + move(pair_other, swap_c=True)).astype(BF16)
    keyval = lax.all_gather(keyval, "span", axis=0, tiled=True)

    query_parts = []
    for group, gather in enumerate((gather_y_first, gather_x_first)):
        shard = w_query[:, group * GCOLS : (group + 1) * GCOLS]
        own, other = project(hidden, other_hidden, which, gather(shard))
        query_parts.append((own, move(other, swap_c=True)))

    half, part = SHARD // 2, SHARD
    low, high = w_out[:part], w_out[part:]
    right, left = move(low, dx=1), move(low, dx=-1)
    opposite = move(right[:half], dx=1), move(left[half:], dx=-1)
    row = jnp.concatenate([low, right, left, *opposite], axis=0)
    row_up, row_down = move(row, dy=1), move(row, dy=-1)
    row_far = move(row_up[: 2 * part], dy=1), move(row_down[2 * part :], dy=-1)
    up, down = move(high, dy=1), move(high, dy=-1)
    far = move(up[:half], dy=1), move(down[half:], dy=-1)
    column = jnp.concatenate([high, up, down, *far], axis=0)
    column_right, column_left = move(column, dx=1), move(column, dx=-1)
    column_far = move(column_right[: 2 * part], dx=1), move(column_left[2 * part :], dx=-1)

    def low_block(at_x, at_y):
        if at_y < 3:
            return (row, row_up, row_down)[at_y], at_x
        return row_far[at_x // 2], at_x % 2

    def high_block(at_x, at_y):
        if at_x < 3:
            return (column, column_right, column_left)[at_x], at_y
        return column_far[at_y // 2], at_y % 2

    block_ids = span_ids.reshape(SPANS, TOK)[:, 0]
    own_id = lax.dynamic_index_in_dim(block_ids, span, keepdims=False)
    flags = jnp.concatenate([(block_ids <= own_id).astype(jnp.int32), as_int([xh])])
    mixed, mixed_other = [], []
    for first, second in query_parts:
        mine, send = attend(flags, first, second, keyval)
        both = jnp.concatenate([mine, move(send, swap_xh=True)], axis=0)
        mixed.append(both)
        mixed_other.append(move(both, swap_c=True))

    totals = []
    for pair, sides in (((0, 3), (0, 1)), ((2, 1), (xl, 1 - xl))):
        weights = []
        for at_y in range(4):
            for at_x in pair:
                weights += [low_block(at_x, at_y), high_block(at_x, at_y)]
        parts = output_partial(as_int([core, z, *sides]), mixed, mixed_other, weights)
        totals.append(reduce_over_z(*parts))
    same, cross = totals
    give = lambda total: lax.dynamic_slice_in_dim(total, (1 - core) * 64, 64)
    got_same, got_cross = move(give(same), swap_c=True), move(give(cross), swap_c=True)
    order = [x * 4 + (y + dy) % 4 for x in (xl, 1 - xl) for dy in (0, 3, 1, 2)]
    return assemble(as_int([core, *order]), same, cross, got_same, got_cross)


def solution(mesh):
    in_specs = (P("span", None), P(), P("span", "uly"), P("span", None, "uly"), P("uly", "span"))
    out_specs = P(("span", "uly"), None)
    return jax.shard_map(
        per_device, mesh=mesh, in_specs=in_specs, out_specs=out_specs, check_vma=False
    )
```

```python
import functools
import math

import jax
import jax.numpy as jnp
from jax import lax
from jax.experimental import pallas as pl
from jax.experimental.pallas import tpu as pltpu
from jax.sharding import PartitionSpec as P

HEADS = 48
HEAD = 128
D = 6144
SPANS = 16
TOK = 512
SHARD = D // SPANS
GROUP = 3
GCOLS = GROUP * HEAD
SCALE2 = math.log2(math.e) / math.sqrt(HEAD)
SAFE_EXPONENT = 90.0
NEG_LARGE = -1e30
VMEM_LIMIT = 60 * 2**20
BOTH = ("span", "uly")
F32 = jnp.float32
BF16 = jnp.bfloat16


def coords(index):
    span, uly = index // 8, index % 8
    return span // 8, (span // 2) % 4, span % 2, uly // 2, uly % 2


def index_of(xl, y, c, z, xh):
    return (xl * 8 + y * 2 + c) * 8 + z * 2 + xh


def move(array, dx=0, dy=0, dz=0, swap_xl=False, swap_xh=False, swap_c=False):
    pairs = []
    for source in range(128):
        xl, y, c, z, xh = coords(source)
        x = (xh * 2 + xl + dx) % 4
        xh, xl = x // 2, x % 2
        if swap_xl:
            xl = 1 - xl
        if swap_xh:
            xh = 1 - xh
        if swap_c:
            c = 1 - c
        pairs.append((source, index_of(xl, (y + dy) % 4, c, (z + dz) % 4, xh)))
    return lax.ppermute(array, BOTH, pairs)


def after(array, *results):
    return lax.optimization_barrier((array, *results))[0]


def project_kernel(which, own_ref, other_ref, *refs):
    pieces, (own_out, other_out, weight) = refs[:8], refs[8:]
    step = pl.program_id(0)
    for at in range(8):
        @pl.when(step == at)
        def _():
            weight[...] = pieces[at][...]

    @pl.when(step == 0)
    def _():
        own_out[...] = jnp.zeros_like(own_out)
        other_out[...] = jnp.zeros_like(other_out)

    own_out[...] += jnp.dot(own_ref[...], weight[...], preferred_element_type=F32)
    other_out[...] += jnp.dot(other_ref[...], weight[...], preferred_element_type=F32)


def project(hidden, other, which, pieces):
    cols = pieces[0].shape[1]
    whole = lambda rows: pl.BlockSpec((rows, cols), lambda i, which: (0, 0))
    out = jax.ShapeDtypeStruct((TOK, cols), F32)
    return pl.pallas_call(
        project_kernel,
        grid_spec=pltpu.PrefetchScalarGridSpec(
            num_scalar_prefetch=1,
            grid=(8,),
            in_specs=[
                pl.BlockSpec((TOK, SHARD), lambda i, which: (0, which[i])),
                pl.BlockSpec((TOK, SHARD), lambda i, which: (0, which[i])),
                *[whole(SHARD) for _ in pieces],
            ],
            out_specs=[whole(TOK), whole(TOK)],
            scratch_shapes=[pltpu.VMEM((SHARD, cols), BF16)],
        ),
        out_shape=[out, out],
        compiler_params=pltpu.CompilerParams(vmem_limit_bytes=VMEM_LIMIT),
        cost_estimate=pl.CostEstimate(
            flops=4 * TOK * 8 * SHARD * cols, bytes_accessed=12 * 2**20, transcendentals=0
        ),
    )(which, hidden, other, *pieces)


def attend_kernel(
    flags, first_ref, second_ref, pair_ref, other_ref, mine_ref, send_ref, query, keys, value, accum, best
):
    query[...] = (first_ref[...] + second_ref[...]).astype(BF16)
    value[:, HEAD:] = jnp.ones((SPANS * TOK, HEAD), BF16)
    accum[...] = jnp.zeros_like(accum)
    ones = jnp.ones((HEAD, HEAD), BF16)

    def prepare(block, largest):
        rows = pl.ds(pl.multiple_of(block * TOK, TOK), TOK)
        for at, ref in enumerate((pair_ref, other_ref)):
            to = pl.ds(pl.multiple_of(block * TOK, TOK) + at * SPANS // 2 * TOK, TOK)
            value[to, :HEAD] = ref[rows, HEAD:]
            key = ref[rows, :HEAD]
            keys[to, :] = key
            norms = jnp.dot(key * key, ones, preferred_element_type=F32)
            largest = jnp.maximum(largest, jnp.max(norms.reshape(TOK // 8, 8, HEAD), axis=0))
        return largest

    key_norm = jnp.max(lax.fori_loop(0, SPANS // 2, prepare, jnp.zeros((8, HEAD), F32)))
    query_norm = jnp.zeros((8, HEAD), F32)
    for head in range(GROUP):
        block = query[:, head * HEAD : (head + 1) * HEAD]
        norms = jnp.dot(block * block, ones, preferred_element_type=F32)
        query_norm = jnp.maximum(query_norm, jnp.max(norms.reshape(TOK // 8, 8, HEAD), axis=0))
    bound = key_norm * jnp.max(query_norm) * (1.03 * SCALE2 * SCALE2)
    small = bound <= SAFE_EXPONENT * SAFE_EXPONENT

    @pl.when(small)
    def _():
        def step(block, carry):
            @pl.when(flags[block] > 0)
            def _():
                rows = pl.ds(pl.multiple_of(block * TOK, TOK), TOK)
                key, extended = keys[rows, :], value[rows, :]
                for head in range(GROUP):
                    scores = lax.dot_general(
                        query[:, head * HEAD : (head + 1) * HEAD],
                        key,
                        (((1,), (1,)), ((), ())),
                        preferred_element_type=F32,
                    )
                    probs = jnp.exp2(scores * SCALE2).astype(BF16)
                    accum[head] += jnp.dot(probs, extended, preferred_element_type=F32)

            return carry

        lax.fori_loop(0, SPANS, step, 0)

    @pl.when(jnp.logical_not(small))
    def _():
        best[...] = jnp.full_like(best, NEG_LARGE)

        def step(at, carry):
            block, head = at // GROUP, at % GROUP

            @pl.when(flags[block] > 0)
            def _():
                rows = pl.ds(pl.multiple_of(block * TOK, TOK), TOK)
                columns = pl.ds(pl.multiple_of(head * HEAD, HEAD), HEAD)
                scores = lax.dot_general(
                    query[:, columns],
                    keys[rows, :],
                    (((1,), (1,)), ((), ())),
                    preferred_element_type=F32,
                )
                old = best[head]
                new = jnp.maximum(old, jnp.max(scores, axis=1, keepdims=True))
                best[head] = new
                probs = jnp.exp2((scores - new[:, :1]) * SCALE2).astype(BF16)
                factor = jnp.exp2((old - new) * SCALE2)
                accum[head] = accum[head] * factor[:, :1] + jnp.dot(
                    probs, value[rows, :], preferred_element_type=F32
                )

            return carry

        lax.fori_loop(0, SPANS * GROUP, step, 0)

    side = flags[SPANS]
    for head in range(GROUP):
        columns = slice(head * HEAD, (head + 1) * HEAD)
        for at in range(4):
            for out_ref, chosen in ((mine_ref, side), (send_ref, 1 - side)):
                rows = pl.ds(pl.multiple_of(at * 128 + chosen * 64, 64), 64)
                mixed = accum[head, rows, :]
                out_ref[at * 64 : at * 64 + 64, columns] = (mixed[:, :HEAD] / mixed[:, HEAD:]).astype(BF16)


def attend(flags, first, second, pair, other):
    out = jax.ShapeDtypeStruct((TOK // 2, GCOLS), BF16)
    return pl.pallas_call(
        attend_kernel,
        in_specs=[pl.BlockSpec(memory_space=pltpu.SMEM)] + [pl.BlockSpec(memory_space=pltpu.VMEM)] * 4,
        out_specs=[pl.BlockSpec(memory_space=pltpu.VMEM)] * 2,
        out_shape=[out, out],
        scratch_shapes=[
            pltpu.VMEM((TOK, GCOLS), BF16),
            pltpu.VMEM((SPANS * TOK, HEAD), BF16),
            pltpu.VMEM((SPANS * TOK, 2 * HEAD), BF16),
            pltpu.VMEM((GROUP, TOK, 2 * HEAD), F32),
            pltpu.VMEM((GROUP, TOK, HEAD), F32),
        ],
        compiler_params=pltpu.CompilerParams(vmem_limit_bytes=VMEM_LIMIT),
        cost_estimate=pl.CostEstimate(
            flops=GROUP * 6 * TOK * SPANS * TOK * HEAD, bytes_accessed=6 * 2**20, transcendentals=0
        ),
    )(flags, first, second, pair, other)


Z_ORDER = (2, 1, 3, 0)


def output_kernel(place, *refs):
    own, other = refs[0:2], refs[2:4]
    weights = refs[4:20]
    far_a, far_b, up, down, stay, rows_of = refs[20:]
    core, z = place[0], place[1]
    for side in range(2):
        chosen = place[2 + side]
        for group in range(2):
            for at, step in enumerate(Z_ORDER):
                rows = pl.ds(pl.multiple_of(chosen * 256 + ((z + step) % 4) * 64, 64), 64)
                a, b = own[group][rows, :], other[group][rows, :]
                first = core == 0
                rows_of[side * 2 + group, at * 128 : at * 128 + 64, :] = jnp.where(first, a, b)
                rows_of[side * 2 + group, at * 128 + 64 : at * 128 + 128, :] = jnp.where(first, b, a)
    for dy in range(4):
        total = jnp.dot(rows_of[0], weights[dy * 4][...], preferred_element_type=F32)
        for at in range(1, 4):
            total += jnp.dot(rows_of[at], weights[dy * 4 + at][...], preferred_element_type=F32)
        total = total.astype(BF16)
        columns = slice(dy * SHARD, (dy + 1) * SHARD)
        far_a[:, columns] = total[:64]
        far_b[:, columns] = total[64:128]
        up[:, columns] = total[128:256]
        down[:, columns] = total[256:384]
        stay[:, columns] = total[384:]


def output_partial(place, own, other, weights):
    whole = pl.BlockSpec(memory_space=pltpu.VMEM)
    shapes = [jax.ShapeDtypeStruct((rows, 4 * SHARD), BF16) for rows in (64, 64, 128, 128, 128)]
    return pl.pallas_call(
        output_kernel,
        grid=(1,),
        in_specs=[pl.BlockSpec(memory_space=pltpu.SMEM)]
        + [whole] * 4
        + [pl.BlockSpec((SHARD, SHARD), lambda i, block=block: (block, 0)) for _, block in weights],
        out_specs=[whole] * 5,
        out_shape=shapes,
        scratch_shapes=[pltpu.VMEM((4, TOK, SHARD), BF16)],
        compiler_params=pltpu.CompilerParams(vmem_limit_bytes=VMEM_LIMIT),
        cost_estimate=pl.CostEstimate(
            flops=2 * TOK * 4 * SHARD * 4 * SHARD, bytes_accessed=8 * 2**20, transcendentals=0
        ),
    )(place, *own, *other, *[array for array, _ in weights])


def assemble_kernel(place, same_ref, cross_ref, got_same, got_cross, out_ref):
    core = place[0]
    keep = pl.ds(pl.multiple_of(core * 64, 64), 64)
    for at, (mine, got) in enumerate(((same_ref, got_same), (cross_ref, got_cross))):
        for dy in range(4):
            span_pair = place[1 + at * 4 + dy]
            columns = slice(dy * SHARD, (dy + 1) * SHARD)
            to = pl.ds(pl.multiple_of((span_pair * 2 + core) * SHARD, 128), SHARD)
            out_ref[:, to] = mine[keep, columns]
            to = pl.ds(pl.multiple_of((span_pair * 2 + 1 - core) * SHARD, 128), SHARD)
            out_ref[:, to] = got[:, columns]


def assemble(place, same, cross, got_same, got_cross):
    whole = pl.BlockSpec(memory_space=pltpu.VMEM)
    return pl.pallas_call(
        assemble_kernel,
        in_specs=[pl.BlockSpec(memory_space=pltpu.SMEM)] + [whole] * 4,
        out_specs=whole,
        out_shape=jax.ShapeDtypeStruct((64, D), BF16),
    )(place, same, cross, got_same, got_cross)


def reduce_over_z(far_a, far_b, up, down, stay):
    got_a, got_b = move(far_a, dz=1), move(far_b, dz=-1)
    add = lambda a, b: (a.astype(F32) + b.astype(F32)).astype(BF16)
    up = jnp.concatenate([add(up[:64], got_a), up[64:]], axis=0)
    down = jnp.concatenate([down[:64], add(down[64:], got_b)], axis=0)
    below, above = move(up, dz=1), move(down, dz=-1)
    return (stay.astype(F32) + below.astype(F32) + above.astype(F32)).astype(BF16)


def per_device(hidden, span_ids, w_query, w_keyval, w_out):
    span, uly = lax.axis_index("span"), lax.axis_index("uly")
    xl, y, core = span // 8, (span // 2) % 4, span % 2
    z, xh = uly // 2, uly % 2
    as_int = lambda values: jnp.stack([jnp.asarray(v, jnp.int32) for v in values])

    chips = [x * 4 + (y + dy) % 4 for dy in (0, 3, 1, 2) for x in (xl, 1 - xl)]
    which = as_int([j * 2 + core for j in chips])
    other_which = as_int([j * 2 + 1 - core for j in chips])

    own = jnp.concatenate([w_keyval[:, 0], w_keyval[:, 1]], axis=1)
    side = move(own, swap_xl=True)
    up, down = move(own, dy=1), move(own, dy=-1)
    side_up, side_down = move(side, dy=1), move(side, dy=-1)
    far, side_far = move(up, dy=1), move(side_down, dy=-1)
    other_hidden = move(hidden, swap_c=True)

    one = after(w_query[:, :GCOLS], side_up, side_down)
    one_side = move(after(w_query[:, :GCOLS], side), swap_xl=True)
    one_up, one_down = move(one, dy=1), move(one, dy=-1)
    two_side = move(after(w_query[:, GCOLS:], one_side), swap_xl=True)
    one_side_up, one_side_down = move(one_up, swap_xl=True), move(one_down, swap_xl=True)
    two = after(w_query[:, GCOLS:], one_up, one_down)
    two_up, two_down = move(two, dy=1), move(two, dy=-1)
    one_far = move(one_up, dy=1)
    one_side_far = move(one_far, swap_xl=True)
    two_side = after(two_side, two_up, two_down)
    two_side_up, two_side_down = move(two_side, dy=1), move(two_side, dy=-1)
    two_far, two_side_far = move(two_down, dy=-1), move(two_side_up, dy=1)

    pieces = [own, side, up, side_up, down, side_down, far, side_far]
    pair_own, pair_other = project(hidden, other_hidden, which, pieces)
    pair = (pair_own + move(pair_other, swap_c=True)).astype(BF16)

    pair_side = move(pair, swap_xl=True)
    pair_up, pair_down = move(pair, dy=1), move(pair, dy=-1)
    pair_side_up, pair_side_down = move(pair_side, dy=1), move(pair_side, dy=-1)
    pair_far, pair_side_far = move(pair_down, dy=-1), move(pair_side_up, dy=1)
    pairs = [pair, pair_side, pair_up, pair_side_up, pair_down, pair_side_down, pair_far, pair_side_far]
    pairs = jnp.concatenate(pairs, axis=0)
    other_pairs = move(pairs, swap_c=True)

    query_parts = []
    for pieces in (
        [w_query[:, :GCOLS], one_side, one_up, one_side_up, one_down, one_side_down, one_far, one_side_far],
        [w_query[:, GCOLS:], two_side, two_up, two_side_up, two_down, two_side_down, two_far, two_side_far],
    ):
        part, other = project(hidden, other_hidden, which, pieces)
        query_parts.append((part, move(other, swap_c=True)))

    low, high = after(w_out[:SHARD], one_side_down), after(w_out[SHARD:], two_side_up, two_side_down)
    right, left = move(low, dx=1), move(low, dx=-1)
    opposite = move(right, dx=1)
    row = [jnp.concatenate([low, right], axis=0), jnp.concatenate([left, opposite], axis=0)]
    up, down = move(high, dy=1), move(high, dy=-1)
    far = move(down, dy=-1)
    column = [jnp.concatenate([high, up], axis=0), jnp.concatenate([down, far], axis=0)]
    row = [after(part, pair_side_up, pair_side_down) for part in row]
    row_up, row_down = [move(part, dy=1) for part in row], [move(part, dy=-1) for part in row]
    row_far = move(row_up[0], dy=1), move(row_down[1], dy=-1)
    column_right, column_left = [move(part, dx=1) for part in column], [move(part, dx=-1) for part in column]
    column_far = move(column_right[0], dx=1), move(column_left[1], dx=-1)

    def low_block(at_x, at_y):
        return (row, row_up, row_down, row_far)[at_y][at_x // 2], at_x % 2

    def high_block(at_x, at_y):
        return (column, column_right, column_left, column_far)[at_x][at_y // 2], at_y % 2

    block_ids = span_ids.reshape(SPANS, TOK)[:, 0]
    own_id = lax.dynamic_index_in_dim(block_ids, span, keepdims=False)
    seen = (block_ids <= own_id).astype(jnp.int32)
    flags = jnp.concatenate([seen[which], seen[other_which], as_int([xh])])
    mixed, mixed_other = [], []
    for first, second in query_parts:
        mine, send = attend(flags, first, second, pairs, other_pairs)
        both = jnp.concatenate([mine, move(send, swap_xh=True)], axis=0)
        mixed.append(both)
        mixed_other.append(move(both, swap_c=True))

    totals = []
    for pair, sides in (((0, 3), (0, 1)), ((2, 1), (xl, 1 - xl))):
        weights = []
        for at_y in range(4):
            for at_x in pair:
                weights += [low_block(at_x, at_y), high_block(at_x, at_y)]
        parts = output_partial(as_int([core, z, *sides]), mixed, mixed_other, weights)
        totals.append(reduce_over_z(*parts))
    same, cross = totals
    give = lambda total: lax.dynamic_slice_in_dim(total, (1 - core) * 64, 64)
    got_same, got_cross = move(give(same), swap_c=True), move(give(cross), swap_c=True)
    order = [x * 4 + (y + dy) % 4 for x in (xl, 1 - xl) for dy in (0, 3, 1, 2)]
    return assemble(as_int([core, *order]), same, cross, got_same, got_cross)


def solution(mesh):
    in_specs = (P("span", None), P(), P("span", "uly"), P("span", None, "uly"), P("uly", "span"))
    out_specs = P(("span", "uly"), None)
    return jax.shard_map(
        per_device, mesh=mesh, in_specs=in_specs, out_specs=out_specs, check_vma=False
    )
```

```python
import functools
import math

import jax
import jax.numpy as jnp
from jax import lax
from jax.experimental import pallas as pl
from jax.experimental.pallas import tpu as pltpu
from jax.sharding import PartitionSpec as P

HEADS = 48
HEAD = 128
D = 6144
SPANS = 16
TOK = 512
SHARD = D // SPANS
GROUP = 3
GCOLS = GROUP * HEAD
SCALE2 = math.log2(math.e) / math.sqrt(HEAD)
SAFE_EXPONENT = 90.0
NEG_LARGE = -1e30
VMEM_LIMIT = 60 * 2**20
BOTH = ("span", "uly")
F32 = jnp.float32
BF16 = jnp.bfloat16


def coords(index):
    span, uly = index // 8, index % 8
    return span // 8, (span // 2) % 4, span % 2, uly // 2, uly % 2


def index_of(xl, y, c, z, xh):
    return (xl * 8 + y * 2 + c) * 8 + z * 2 + xh


def move(array, dx=0, dy=0, dz=0, swap_xl=False, swap_xh=False, swap_c=False):
    pairs = []
    for source in range(128):
        xl, y, c, z, xh = coords(source)
        x = (xh * 2 + xl + dx) % 4
        xh, xl = x // 2, x % 2
        if swap_xl:
            xl = 1 - xl
        if swap_xh:
            xh = 1 - xh
        if swap_c:
            c = 1 - c
        pairs.append((source, index_of(xl, (y + dy) % 4, c, (z + dz) % 4, xh)))
    return lax.ppermute(array, BOTH, pairs)


def after(array, *results):
    return lax.optimization_barrier((array, *results))[0]


def project_kernel(which, own_ref, other_ref, *refs):
    pieces, (own_out, other_out, own_rows, other_rows, weight, arrived) = refs[:8], refs[8:]
    copies = []
    for at in range(8):
        columns = pl.ds(pl.multiple_of(which[at] * SHARD, 128), SHARD)
        to = slice(at * SHARD, (at + 1) * SHARD)
        copies.append(
            [
                pltpu.make_async_copy(pieces[at], weight.at[to, :], arrived.at[at, 0]),
                pltpu.make_async_copy(own_ref.at[:, columns], own_rows.at[:, to], arrived.at[at, 1]),
                pltpu.make_async_copy(other_ref.at[:, columns], other_rows.at[:, to], arrived.at[at, 2]),
            ]
        )
    for copy in copies:
        for one in copy:
            one.start()
    for at in range(4):
        for copy in copies[2 * at : 2 * at + 2]:
            for one in copy:
                one.wait()
        to = slice(2 * at * SHARD, (2 * at + 2) * SHARD)
        for rows, out in ((own_rows, own_out), (other_rows, other_out)):
            part = jnp.dot(rows[:, to], weight[to, :], preferred_element_type=F32)
            if at == 0:
                out[...] = part
            else:
                out[...] += part


def project(hidden, other, which, pieces):
    cols = pieces[0].shape[1]
    out = jax.ShapeDtypeStruct((TOK, cols), F32)
    return pl.pallas_call(
        project_kernel,
        in_specs=[pl.BlockSpec(memory_space=pltpu.SMEM)] + [pl.BlockSpec(memory_space=pl.ANY)] * 10,
        out_specs=[pl.BlockSpec(memory_space=pltpu.VMEM)] * 2,
        out_shape=[out, out],
        scratch_shapes=[
            pltpu.VMEM((TOK, 8 * SHARD), BF16),
            pltpu.VMEM((TOK, 8 * SHARD), BF16),
            pltpu.VMEM((8 * SHARD, cols), BF16),
            pltpu.SemaphoreType.DMA((8, 3)),
        ],
        compiler_params=pltpu.CompilerParams(vmem_limit_bytes=VMEM_LIMIT),
        cost_estimate=pl.CostEstimate(
            flops=4 * TOK * 8 * SHARD * cols, bytes_accessed=12 * 2**20, transcendentals=0
        ),
    )(which, hidden, other, *pieces)


def attend_kernel(
    flags, norms, one_a, one_b, two_a, two_b, pair_ref, other_ref,
    out_ref, parts, query, keys, value, accum, best, ready, arrived,
):
    side = flags[SPANS]
    heads = HEADS // 8
    loads = []
    for at in range(4):
        rows = pl.ds(pl.multiple_of(at * 128 + side * 64, 64), 64)
        for which, ref in enumerate((one_a, one_b, two_a, two_b)):
            to = parts.at[which, at * 64 : at * 64 + 64, :]
            loads.append(pltpu.make_async_copy(ref.at[rows, :], to, ready.at[which, at]))
    pairs = []
    for ref in (pair_ref, other_ref):
        for at in range(SPANS // 2):
            block, rows = len(pairs), slice(at * TOK, (at + 1) * TOK)
            pairs.append(
                (
                    pltpu.make_async_copy(ref.at[rows, :HEAD], keys.at[block], arrived.at[block, 0]),
                    pltpu.make_async_copy(ref.at[rows, HEAD:], value.at[block, :, :HEAD], arrived.at[block, 1]),
                )
            )
    for load in loads:
        load.start()
    for key, mixed in pairs:
        key.start()
        mixed.start()
    value[:, :, HEAD:] = jnp.ones((SPANS, TOK, HEAD), BF16)
    accum[...] = jnp.zeros_like(accum)
    for load in loads:
        load.wait()
    query[:, :GCOLS] = (parts[0] + parts[1]).astype(BF16)
    query[:, GCOLS:] = (parts[2] + parts[3]).astype(BF16)

    ones = jnp.ones((HEAD, HEAD), BF16)
    largest = jnp.zeros((8, HEAD), F32)
    for head in range(heads):
        block = query[:, head * HEAD : (head + 1) * HEAD]
        squares = jnp.dot(block * block, ones, preferred_element_type=F32)
        largest = jnp.maximum(largest, jnp.max(squares.reshape(TOK // 16, 8, HEAD), axis=0))
    bound = jnp.maximum(norms[0], norms[1]) * jnp.max(largest) * (1.03 * SCALE2 * SCALE2)
    small = bound <= SAFE_EXPONENT * SAFE_EXPONENT

    def step_small(block):
        key, extended = keys[block], value[block]
        for head in range(heads):
            scores = lax.dot_general(
                query[:, head * HEAD : (head + 1) * HEAD],
                key,
                (((1,), (1,)), ((), ())),
                preferred_element_type=F32,
            )
            probs = jnp.exp2(scores * SCALE2).astype(BF16)
            accum[head] += jnp.dot(probs, extended, preferred_element_type=F32)

    def step_any(block):
        def one(head, carry):
            scores = lax.dot_general(
                query[:, pl.ds(pl.multiple_of(head * HEAD, HEAD), HEAD)],
                keys[block],
                (((1,), (1,)), ((), ())),
                preferred_element_type=F32,
            )
            old = best[head]
            new = jnp.maximum(old, jnp.max(scores, axis=1, keepdims=True))
            best[head] = new
            probs = jnp.exp2((scores - new[:, :1]) * SCALE2).astype(BF16)
            factor = jnp.exp2((old - new) * SCALE2)
            accum[head] = accum[head] * factor[:, :1] + jnp.dot(
                probs, value[block], preferred_element_type=F32
            )
            return carry

        lax.fori_loop(0, heads, one, 0)

    @pl.when(jnp.logical_not(small))
    def _():
        best[...] = jnp.full_like(best, NEG_LARGE)

    def step(block, carry):
        for at, to in enumerate((keys.at[block], value.at[block, :, :HEAD])):
            pltpu.make_async_copy(pair_ref.at[:TOK, :HEAD], to, arrived.at[block, at]).wait()

        @pl.when((flags[block] > 0) & small)
        def _():
            step_small(block)

        @pl.when((flags[block] > 0) & jnp.logical_not(small))
        def _():
            step_any(block)

        return carry

    lax.fori_loop(0, SPANS, step, 0)
    for head in range(heads):
        mixed = accum[head]
        out_ref[:, head * HEAD : (head + 1) * HEAD] = (mixed[:, :HEAD] / mixed[:, HEAD:]).astype(BF16)


def attend(flags, norms, queries, pair, other):
    half, heads = TOK // 2, HEADS // 8
    return pl.pallas_call(
        attend_kernel,
        in_specs=[pl.BlockSpec(memory_space=pltpu.SMEM)] * 2 + [pl.BlockSpec(memory_space=pl.ANY)] * 6,
        out_specs=pl.BlockSpec(memory_space=pltpu.VMEM),
        out_shape=jax.ShapeDtypeStruct((half, 2 * GCOLS), BF16),
        scratch_shapes=[
            pltpu.VMEM((4, half, GCOLS), F32),
            pltpu.VMEM((half, 2 * GCOLS), BF16),
            pltpu.VMEM((SPANS, TOK, HEAD), BF16),
            pltpu.VMEM((SPANS, TOK, 2 * HEAD), BF16),
            pltpu.VMEM((heads, half, 2 * HEAD), F32),
            pltpu.VMEM((heads, half, HEAD), F32),
            pltpu.SemaphoreType.DMA((4, 4)),
            pltpu.SemaphoreType.DMA((SPANS, 2)),
        ],
        compiler_params=pltpu.CompilerParams(vmem_limit_bytes=VMEM_LIMIT),
        cost_estimate=pl.CostEstimate(
            flops=heads * 6 * half * SPANS * TOK * HEAD, bytes_accessed=6 * 2**20, transcendentals=0
        ),
    )(flags, norms, *queries, pair, other)


OUT_GROUPS = 4
OUT_COLS = D // OUT_GROUPS
Z_ORDER = (2, 1, 3, 0)


def output_kernel(place, mine_ref, got_ref, first_ref, second_ref, far, up, down, stay, rows_of):
    z = place[0]

    @pl.when(pl.program_id(0) == 0)
    def _():
        for at, step in enumerate(Z_ORDER):
            rows = pl.ds(pl.multiple_of(((z + step) % 4) * 64, 64), 64)
            rows_of[0, at * 64 : at * 64 + 64, :] = mine_ref[rows, :]
            rows_of[1, at * 64 : at * 64 + 64, :] = got_ref[rows, :]

    for at in range(2):
        block = slice(at * 2 * SHARD, (at + 1) * 2 * SHARD)
        total = jnp.dot(rows_of[0], first_ref[block, :], preferred_element_type=F32)
        total += jnp.dot(rows_of[1], second_ref[block, :], preferred_element_type=F32)
        total = total.astype(BF16)
        columns = slice(at * SHARD, (at + 1) * SHARD)
        for index, out in enumerate((far, up, down, stay)):
            out[:, columns] = total[index * 64 : index * 64 + 64]


def output_partial(group, place, mine, got, weights):
    steps = OUT_COLS // (2 * SHARD)
    whole = pl.BlockSpec((TOK // 2, 2 * GCOLS), lambda i, place: (0, 0))
    block = (4 * SHARD, SHARD)
    out = pl.BlockSpec((64, 2 * SHARD), lambda i, place: (0, i))
    return pl.pallas_call(
        output_kernel,
        grid_spec=pltpu.PrefetchScalarGridSpec(
            num_scalar_prefetch=1,
            grid=(steps,),
            in_specs=[
                whole,
                whole,
                pl.BlockSpec(block, lambda i, place: (place[1] * 8 + group * steps + i, 0)),
                pl.BlockSpec(block, lambda i, place: ((1 - place[1]) * 8 + group * steps + i, 0)),
            ],
            out_specs=[out] * 4,
            scratch_shapes=[pltpu.VMEM((2, TOK // 2, 2 * GCOLS), BF16)],
        ),
        out_shape=[jax.ShapeDtypeStruct((64, OUT_COLS), BF16)] * 4,
        compiler_params=pltpu.CompilerParams(vmem_limit_bytes=VMEM_LIMIT),
        cost_estimate=pl.CostEstimate(
            flops=2 * TOK // 2 * OUT_COLS * 4 * GCOLS, bytes_accessed=6 * 2**20, transcendentals=0
        ),
    )(place, mine, got, weights, weights)


def reduce_over_z(far, up, down, stay, sign):
    near, back = (up, down) if sign > 0 else (down, up)
    passed = move(far, dz=sign)
    behind = move(back, dz=-sign)
    near = (near.astype(F32) + passed.astype(F32)).astype(BF16)
    ahead = move(near, dz=sign)
    return (stay.astype(F32) + ahead.astype(F32) + behind.astype(F32)).astype(BF16)


def per_device(hidden, span_ids, w_query, w_keyval, w_out):
    span, uly = lax.axis_index("span"), lax.axis_index("uly")
    xl, y, core = span // 8, (span // 2) % 4, span % 2
    z, xh = uly // 2, uly % 2
    as_int = lambda values: jnp.stack([jnp.asarray(v, jnp.int32) for v in values])

    chips = [x * 4 + (y + dy) % 4 for dy in (0, 3, 1, 2) for x in (xl, 1 - xl)]
    which = as_int([j * 2 + core for j in chips])
    other_which = as_int([j * 2 + 1 - core for j in chips])

    own = jnp.concatenate([w_keyval[:, 0], w_keyval[:, 1]], axis=1)
    side = move(own, swap_xl=True)
    up, down = move(own, dy=1), move(own, dy=-1)
    side_up, side_down = move(side, dy=1), move(side, dy=-1)
    far, side_far = move(up, dy=1), move(side_down, dy=-1)
    other_hidden = move(hidden, swap_c=True)

    one = after(w_query[:, :GCOLS], side_up, side_down)
    one_side = move(after(w_query[:, :GCOLS], side), swap_xl=True)
    one_up, one_down = move(one, dy=1), move(one, dy=-1)
    two_side = move(after(w_query[:, GCOLS:], one_side), swap_xl=True)
    one_side_up, one_side_down = move(one_up, swap_xl=True), move(one_down, swap_xl=True)
    two = after(w_query[:, GCOLS:], one_up, one_down)
    two_up, two_down = move(two, dy=1), move(two, dy=-1)
    one_far = move(one_up, dy=1)
    one_side_far = move(one_far, swap_xl=True)
    two_side = after(two_side, two_up, two_down)
    two_side_up, two_side_down = move(two_side, dy=1), move(two_side, dy=-1)
    two_far, two_side_far = move(two_down, dy=-1), move(two_side_up, dy=1)

    pieces = [own, side, up, side_up, down, side_down, far, side_far]
    pair_own, pair_other = project(hidden, other_hidden, which, pieces)
    pair = (pair_own + move(pair_other, swap_c=True)).astype(BF16)

    pair_side = move(pair, swap_xl=True)
    pair_up, pair_down = move(pair, dy=1), move(pair, dy=-1)
    pair_side_up, pair_side_down = move(pair_side, dy=1), move(pair_side, dy=-1)
    pair_far, pair_side_far = move(pair_down, dy=-1), move(pair_side_up, dy=1)
    pairs = [pair, pair_side, pair_up, pair_side_up, pair_down, pair_side_down, pair_far, pair_side_far]
    pairs = jnp.concatenate(pairs, axis=0)
    other_pairs = move(pairs, swap_c=True)

    query_parts = []
    for pieces in (
        [w_query[:, :GCOLS], one_side, one_up, one_side_up, one_down, one_side_down, one_far, one_side_far],
        [w_query[:, GCOLS:], two_side, two_up, two_side_up, two_down, two_side_down, two_far, two_side_far],
    ):
        part, other = project(hidden, other_hidden, which, pieces)
        query_parts += [part, move(other, swap_c=True)]

    planes = [
        [index_of(span // 8, span // 2 % 4, span % 2, at, side) for side in range(2) for span in range(SPANS)]
        for at in range(4)
    ]
    weights = lax.all_gather(
        after(w_out, far, side_far), BOTH, axis=0, tiled=True, axis_index_groups=planes
    )

    block_ids = span_ids.reshape(SPANS, TOK)[:, 0]
    own_id = lax.dynamic_index_in_dim(block_ids, span, keepdims=False)
    seen = (block_ids <= own_id).astype(jnp.int32)
    seen = jnp.concatenate([seen[which], seen[other_which]])
    norm = lambda rows: jnp.max(jnp.sum(jnp.square(rows[:, :HEAD].astype(F32)), axis=1))
    norms = jnp.stack([norm(pairs), norm(other_pairs)])
    send = attend(jnp.concatenate([seen, as_int([1 - xh])]), norms, query_parts, pairs, other_pairs)
    got = move(send, swap_xh=True)
    flags = after(jnp.concatenate([seen, as_int([xh])]), send)
    mine = attend(flags, norms, query_parts, pairs, other_pairs)

    totals = []
    for group in range(OUT_GROUPS):
        parts = output_partial(group, as_int([z, xh]), mine, got, weights)
        totals.append(reduce_over_z(*parts, 1 if group % 2 == 0 else -1))
    return jnp.concatenate(totals, axis=1)


def solution(mesh):
    in_specs = (P("span", None), P(), P("span", "uly"), P("span", None, "uly"), P("uly", "span"))
    out_specs = P(("span", "uly"), None)
    return jax.shard_map(
        per_device, mesh=mesh, in_specs=in_specs, out_specs=out_specs, check_vma=False
    )
```

```python
import functools
import math

import jax
import jax.numpy as jnp
from jax import lax
from jax.experimental import pallas as pl
from jax.experimental.pallas import tpu as pltpu
from jax.sharding import PartitionSpec as P

HEADS = 48
HEAD = 128
D = 6144
SPANS = 16
TOK = 512
SHARD = D // SPANS
GROUP = 3
GCOLS = GROUP * HEAD
SCALE2 = math.log2(math.e) / math.sqrt(HEAD)
SAFE_EXPONENT = 90.0
NEG_LARGE = -1e30
VMEM_LIMIT = 60 * 2**20
BOTH = ("span", "uly")
F32 = jnp.float32
BF16 = jnp.bfloat16


def coords(index):
    span, uly = index // 8, index % 8
    return span // 8, (span // 2) % 4, span % 2, uly // 2, uly % 2


def index_of(xl, y, c, z, xh):
    return (xl * 8 + y * 2 + c) * 8 + z * 2 + xh


def move(array, dx=0, dy=0, dz=0, swap_xl=False, swap_xh=False, swap_c=False):
    pairs = []
    for source in range(128):
        xl, y, c, z, xh = coords(source)
        x = (xh * 2 + xl + dx) % 4
        xh, xl = x // 2, x % 2
        if swap_xl:
            xl = 1 - xl
        if swap_xh:
            xh = 1 - xh
        if swap_c:
            c = 1 - c
        pairs.append((source, index_of(xl, (y + dy) % 4, c, (z + dz) % 4, xh)))
    return lax.ppermute(array, BOTH, pairs)


def after(array, *results):
    return lax.optimization_barrier((array, *results))[0]


def project_kernel(which, own_ref, other_ref, *refs):
    pieces, (own_out, other_out, own_rows, other_rows, weight, arrived) = refs[:8], refs[8:]
    copies = []
    for at in range(8):
        columns = pl.ds(pl.multiple_of(which[at] * SHARD, 128), SHARD)
        to = slice(at * SHARD, (at + 1) * SHARD)
        copies.append(
            [
                pltpu.make_async_copy(pieces[at], weight.at[to, :], arrived.at[at, 0]),
                pltpu.make_async_copy(own_ref.at[:, columns], own_rows.at[:, to], arrived.at[at, 1]),
                pltpu.make_async_copy(other_ref.at[:, columns], other_rows.at[:, to], arrived.at[at, 2]),
            ]
        )
    for copy in copies:
        for one in copy:
            one.start()
    for at in range(4):
        for copy in copies[2 * at : 2 * at + 2]:
            for one in copy:
                one.wait()
        to = slice(2 * at * SHARD, (2 * at + 2) * SHARD)
        for rows, out in ((own_rows, own_out), (other_rows, other_out)):
            part = jnp.dot(rows[:, to], weight[to, :], preferred_element_type=F32)
            if at == 0:
                out[...] = part
            else:
                out[...] += part


def project(hidden, other, which, pieces):
    cols = pieces[0].shape[1]
    out = jax.ShapeDtypeStruct((TOK, cols), F32)
    return pl.pallas_call(
        project_kernel,
        in_specs=[pl.BlockSpec(memory_space=pltpu.SMEM)] + [pl.BlockSpec(memory_space=pl.ANY)] * 10,
        out_specs=[pl.BlockSpec(memory_space=pltpu.VMEM)] * 2,
        out_shape=[out, out],
        scratch_shapes=[
            pltpu.VMEM((TOK, 8 * SHARD), BF16),
            pltpu.VMEM((TOK, 8 * SHARD), BF16),
            pltpu.VMEM((8 * SHARD, cols), BF16),
            pltpu.SemaphoreType.DMA((8, 3)),
        ],
        compiler_params=pltpu.CompilerParams(vmem_limit_bytes=VMEM_LIMIT),
        cost_estimate=pl.CostEstimate(
            flops=4 * TOK * 8 * SHARD * cols, bytes_accessed=12 * 2**20, transcendentals=0
        ),
    )(which, hidden, other, *pieces)


QUERY_STEP = 768


def query_kernel(hidden_ref, weight_ref, out_ref, total):
    step = pl.program_id(0)
    part = jnp.dot(hidden_ref[...], weight_ref[...], preferred_element_type=F32)

    @pl.when(step == 0)
    def _():
        total[...] = part

    @pl.when(step > 0)
    def _():
        total[...] += part

    @pl.when(step == pl.num_programs(0) - 1)
    def _():
        out_ref[...] = total[...].astype(BF16)


def project_queries(hidden, weight):
    cols = weight.shape[1]
    return pl.pallas_call(
        query_kernel,
        grid=(D // QUERY_STEP,),
        in_specs=[
            pl.BlockSpec((TOK, QUERY_STEP), lambda i: (0, i)),
            pl.BlockSpec((QUERY_STEP, cols), lambda i: (i, 0)),
        ],
        out_specs=pl.BlockSpec((TOK, cols), lambda i: (0, 0)),
        out_shape=jax.ShapeDtypeStruct((TOK, cols), BF16),
        scratch_shapes=[pltpu.VMEM((TOK, cols), F32)],
        compiler_params=pltpu.CompilerParams(vmem_limit_bytes=VMEM_LIMIT),
        cost_estimate=pl.CostEstimate(
            flops=2 * TOK * D * cols, bytes_accessed=16 * 2**20, transcendentals=0
        ),
    )(hidden, weight)


def attend_kernel(
    flags, query_ref, *refs
):
    pair_refs, refs = refs[:4], refs[4:]
    out_ref, query, keys, value, accum, best, largest, ready, arrived = refs
    side = flags[SPANS]
    heads = HEADS // 8
    loads = []
    for at in range(4):
        rows = pl.ds(pl.multiple_of(at * 128 + side * 64, 64), 64)
        to = query.at[at * 64 : at * 64 + 64, :]
        loads.append(pltpu.make_async_copy(query_ref.at[rows, :], to, ready.at[at]))
    pairs = []
    for ref in pair_refs:
        for at in range(SPANS // 4):
            block, rows = len(pairs), slice(at * TOK, (at + 1) * TOK)
            pairs.append(
                (
                    pltpu.make_async_copy(ref.at[rows, :HEAD], keys.at[block], arrived.at[block, 0]),
                    pltpu.make_async_copy(ref.at[rows, HEAD:], value.at[block, :, :HEAD], arrived.at[block, 1]),
                )
            )
    for load in loads:
        load.start()
    for key, mixed in pairs:
        key.start()
        mixed.start()
    value[:, :, HEAD:] = jnp.ones((SPANS, TOK, HEAD), BF16)
    accum[...] = jnp.zeros_like(accum)
    largest[...] = jnp.zeros_like(largest)
    for load in loads:
        load.wait()
    ones = jnp.ones((HEAD, HEAD), BF16)

    def squares(rows):
        sums = jnp.dot(rows * rows, ones, preferred_element_type=F32)
        return jnp.max(sums.reshape(rows.shape[0] // 8, 8, HEAD), axis=0)

    for head in range(heads):
        largest[0] = jnp.maximum(largest[0], squares(query[:, head * HEAD : (head + 1) * HEAD]))

    def step_small(block):
        key, extended = keys[block], value[block]
        largest[1] = jnp.maximum(largest[1], squares(key))
        for head in range(heads):
            scores = lax.dot_general(
                query[:, head * HEAD : (head + 1) * HEAD],
                key,
                (((1,), (1,)), ((), ())),
                preferred_element_type=F32,
            )
            probs = jnp.exp2(scores * SCALE2).astype(BF16)
            accum[head] += jnp.dot(probs, extended, preferred_element_type=F32)

    def step_any(block):
        def one(head, carry):
            scores = lax.dot_general(
                query[:, pl.ds(pl.multiple_of(head * HEAD, HEAD), HEAD)],
                keys[block],
                (((1,), (1,)), ((), ())),
                preferred_element_type=F32,
            )
            old = best[head]
            new = jnp.maximum(old, jnp.max(scores, axis=1, keepdims=True))
            best[head] = new
            probs = jnp.exp2((scores - new[:, :1]) * SCALE2).astype(BF16)
            factor = jnp.exp2((old - new) * SCALE2)
            accum[head] = accum[head] * factor[:, :1] + jnp.dot(
                probs, value[block], preferred_element_type=F32
            )
            return carry

        lax.fori_loop(0, heads, one, 0)

    def step(block, carry):
        for at, to in enumerate((keys.at[block], value.at[block, :, :HEAD])):
            pltpu.make_async_copy(pair_refs[0].at[:TOK, :HEAD], to, arrived.at[block, at]).wait()

        @pl.when(flags[block] > 0)
        def _():
            step_small(block)

        return carry

    lax.fori_loop(0, SPANS, step, 0)
    bound = jnp.max(largest[0]) * jnp.max(largest[1]) * (1.03 * SCALE2 * SCALE2)

    @pl.when(jnp.logical_not(bound <= SAFE_EXPONENT * SAFE_EXPONENT))
    def _():
        accum[...] = jnp.zeros_like(accum)
        best[...] = jnp.full_like(best, NEG_LARGE)

        def again(block, carry):
            @pl.when(flags[block] > 0)
            def _():
                step_any(block)

            return carry

        lax.fori_loop(0, SPANS, again, 0)

    for head in range(heads):
        mixed = accum[head]
        out_ref[:, head * HEAD : (head + 1) * HEAD] = (mixed[:, :HEAD] / mixed[:, HEAD:]).astype(BF16)


def attend(flags, queries, pairs):
    half, heads = TOK // 2, HEADS // 8
    return pl.pallas_call(
        attend_kernel,
        in_specs=[pl.BlockSpec(memory_space=pltpu.SMEM)] + [pl.BlockSpec(memory_space=pl.ANY)] * 5,
        out_specs=pl.BlockSpec(memory_space=pltpu.VMEM),
        out_shape=jax.ShapeDtypeStruct((half, 2 * GCOLS), BF16),
        scratch_shapes=[
            pltpu.VMEM((half, 2 * GCOLS), BF16),
            pltpu.VMEM((SPANS, TOK, HEAD), BF16),
            pltpu.VMEM((SPANS, TOK, 2 * HEAD), BF16),
            pltpu.VMEM((heads, half, 2 * HEAD), F32),
            pltpu.VMEM((heads, half, HEAD), F32),
            pltpu.VMEM((2, 8, HEAD), F32),
            pltpu.SemaphoreType.DMA((4,)),
            pltpu.SemaphoreType.DMA((SPANS, 2)),
        ],
        compiler_params=pltpu.CompilerParams(vmem_limit_bytes=VMEM_LIMIT),
        cost_estimate=pl.CostEstimate(
            flops=heads * 6 * half * SPANS * TOK * HEAD, bytes_accessed=6 * 2**20, transcendentals=0
        ),
    )(flags, queries, *pairs)


OUT_GROUPS = 4
OUT_COLS = D // OUT_GROUPS
Z_ORDER = (2, 1, 3, 0)


def output_kernel(group, place, mine_ref, got_ref, weight_ref, far, up, down, stay, rows_of, wide, arrived):
    z, side = place[0], place[1]
    copies = []
    for at in range(SPANS // OUT_GROUPS):
        for which, chosen in enumerate((side, 1 - side)):
            start = (chosen * SPANS + group * (SPANS // OUT_GROUPS) + at) * 2 * SHARD
            source = weight_ref.at[pl.ds(pl.multiple_of(start, 2 * SHARD), 2 * SHARD), :]
            to = wide.at[which, :, at * SHARD : (at + 1) * SHARD]
            copies.append(pltpu.make_async_copy(source, to, arrived.at[at, which]))
    for copy in copies:
        copy.start()
    for at, step in enumerate(Z_ORDER):
        rows = pl.ds(pl.multiple_of(((z + step) % 4) * 64, 64), 64)
        rows_of[0, at * 64 : at * 64 + 64, :] = mine_ref[rows, :]
        rows_of[1, at * 64 : at * 64 + 64, :] = got_ref[rows, :]
    for part in range(2):
        for copy in copies[part * 4 : part * 4 + 4]:
            copy.wait()
        columns = slice(part * 2 * SHARD, (part + 1) * 2 * SHARD)
        total = jnp.dot(rows_of[0], wide[0, :, columns], preferred_element_type=F32)
        total += jnp.dot(rows_of[1], wide[1, :, columns], preferred_element_type=F32)
        total = total.astype(BF16)
        for index, out in enumerate((far, up, down, stay)):
            out[:, columns] = total[index * 64 : index * 64 + 64]


def output_partial(group, place, mine, got, weights):
    vmem = pl.BlockSpec(memory_space=pltpu.VMEM)
    return pl.pallas_call(
        functools.partial(output_kernel, group),
        in_specs=[pl.BlockSpec(memory_space=pltpu.SMEM), vmem, vmem, pl.BlockSpec(memory_space=pl.ANY)],
        out_specs=[vmem] * 4,
        out_shape=[jax.ShapeDtypeStruct((64, OUT_COLS), BF16)] * 4,
        scratch_shapes=[
            pltpu.VMEM((2, TOK // 2, 2 * GCOLS), BF16),
            pltpu.VMEM((2, 2 * SHARD, OUT_COLS), BF16),
            pltpu.SemaphoreType.DMA((SPANS // OUT_GROUPS, 2)),
        ],
        compiler_params=pltpu.CompilerParams(vmem_limit_bytes=VMEM_LIMIT),
        cost_estimate=pl.CostEstimate(
            flops=2 * TOK // 2 * OUT_COLS * 4 * GCOLS, bytes_accessed=6 * 2**20, transcendentals=0
        ),
    )(place, mine, got, weights)


def reduce_over_z(far, up, down, stay, sign):
    near, back = (up, down) if sign > 0 else (down, up)
    passed = move(far, dz=sign)
    behind = move(back, dz=-sign)
    near = (near.astype(F32) + passed.astype(F32)).astype(BF16)
    ahead = move(near, dz=sign)
    return (stay.astype(F32) + ahead.astype(F32) + behind.astype(F32)).astype(BF16), passed


def per_device(hidden, span_ids, w_query, w_keyval, w_out):
    span, uly = lax.axis_index("span"), lax.axis_index("uly")
    xl, y, core = span // 8, (span // 2) % 4, span % 2
    z, xh = uly // 2, uly % 2
    as_int = lambda values: jnp.stack([jnp.asarray(v, jnp.int32) for v in values])

    chips = [x * 4 + (y + dy) % 4 for dy in (0, 3, 1, 2) for x in (xl, 1 - xl)]
    which = as_int([j * 2 + core for j in chips])
    place = as_int([z, xh])
    block_ids = span_ids.reshape(SPANS, TOK)[:, 0]
    seen = (block_ids <= block_ids[span]).astype(jnp.int32)
    order = [chips[at] * 2 + core for at in (0, 1, 2, 4, 3, 5, 6, 7)]
    seen = seen[as_int(order + [at + 1 - 2 * core for at in order])]
    send_flags = jnp.concatenate([seen, as_int([1 - xh])])
    mine_flags = jnp.concatenate([seen, as_int([xh])])

    query_weight = lax.all_gather(w_query, "span", axis=0, tiled=True)
    planes = [
        [index_of(span // 8, span // 2 % 4, span % 2, at, side) for side in range(2) for span in range(SPANS)]
        for at in range(4)
    ]
    weights = lax.all_gather(
        after(w_out, query_weight), BOTH, axis=0, tiled=True, axis_index_groups=planes
    )

    own = jnp.concatenate([w_keyval[:, 0], w_keyval[:, 1]], axis=1)
    side = move(own, swap_xl=True)
    up, down = move(own, dy=1), move(own, dy=-1)
    other_hidden = move(hidden, swap_c=True)
    side, up, down, which, place, send_flags, mine_flags = lax.optimization_barrier(
        (side, up, down, which, place, send_flags, mine_flags)
    )
    side_up, side_down = move(side, dy=1), move(side, dy=-1)
    up, side_up, side_down = lax.optimization_barrier((up, side_up, side_down))
    far, side_far = move(up, dy=1), move(side_down, dy=-1)
    pieces = [own, side, up, side_up, down, side_down, far, side_far]
    pair_own, pair_other = project(hidden, other_hidden, which, pieces)
    pair = (pair_own + move(pair_other, swap_c=True)).astype(BF16)

    pair_side = move(pair, swap_xl=True)
    pair_up, pair_down = move(pair, dy=1), move(pair, dy=-1)
    pair_side, pair_up, pair_down = lax.optimization_barrier((pair_side, pair_up, pair_down))
    pair_side_up, pair_side_down = move(pair_side, dy=1), move(pair_side, dy=-1)
    pairs = jnp.concatenate([pair, pair_side, pair_up, pair_down], axis=0)
    other_pairs = move(pairs, swap_c=True)
    pair_down, pair_side_up, pair_side_down = lax.optimization_barrier((pair_down, pair_side_up, pair_side_down))
    pair_far, pair_side_far = move(pair_down, dy=-1), move(pair_side_up, dy=1)
    more_pairs = jnp.concatenate([pair_side_up, pair_side_down, pair_far, pair_side_far], axis=0)
    pairs = [pairs, more_pairs, other_pairs, move(more_pairs, swap_c=True)]

    queries = project_queries(hidden, query_weight)
    send = attend(send_flags, queries, pairs)
    got = move(send, swap_xh=True)
    mine = attend(after(mine_flags, send), queries, pairs)

    totals, passed = [], []
    for group in range(OUT_GROUPS):
        if group > 1:
            place = after(place, passed[group - 2])
        parts = output_partial(group, place, mine, got, weights)
        total, through = reduce_over_z(*parts, 1 if group % 2 == 0 else -1)
        totals.append(total)
        passed.append(through)
    return jnp.concatenate(totals, axis=1)


def solution(mesh):
    in_specs = (P("span", None), P(), P("span", "uly"), P("span", None, "uly"), P("uly", "span"))
    out_specs = P(("span", "uly"), None)
    return jax.shard_map(
        per_device, mesh=mesh, in_specs=in_specs, out_specs=out_specs, check_vma=False
    )
```

```python
import functools
import math

import jax
import jax.numpy as jnp
from jax import lax
from jax.experimental import pallas as pl
from jax.experimental.pallas import tpu as pltpu
from jax.sharding import PartitionSpec as P

HEADS = 48
HEAD = 128
D = 6144
SPANS = 16
TOK = 512
SHARD = D // SPANS
GROUP = 3
GCOLS = GROUP * HEAD
SCALE2 = math.log2(math.e) / math.sqrt(HEAD)
SAFE_EXPONENT = 90.0
NEG_LARGE = -1e30
VMEM_LIMIT = 60 * 2**20
BOTH = ("span", "uly")
F32 = jnp.float32
BF16 = jnp.bfloat16


def coords(index):
    span, uly = index // 8, index % 8
    return span // 8, (span // 2) % 4, span % 2, uly // 2, uly % 2


def index_of(xl, y, c, z, xh):
    return (xl * 8 + y * 2 + c) * 8 + z * 2 + xh


def move(array, dx=0, dy=0, dz=0, swap_xl=False, swap_xh=False, swap_c=False):
    pairs = []
    for source in range(128):
        xl, y, c, z, xh = coords(source)
        x = (xh * 2 + xl + dx) % 4
        xh, xl = x // 2, x % 2
        if swap_xl:
            xl = 1 - xl
        if swap_xh:
            xh = 1 - xh
        if swap_c:
            c = 1 - c
        pairs.append((source, index_of(xl, (y + dy) % 4, c, (z + dz) % 4, xh)))
    return lax.ppermute(array, BOTH, pairs)


def after(array, *results):
    return lax.optimization_barrier((array, *results))[0]


def project_kernel(which, own_ref, other_ref, *refs):
    pieces, (own_out, other_out, own_rows, other_rows, weight, arrived) = refs[:8], refs[8:]
    copies = []
    for at in range(8):
        columns = pl.ds(pl.multiple_of(which[at] * SHARD, 128), SHARD)
        to = slice(at * SHARD, (at + 1) * SHARD)
        copies.append(
            [
                pltpu.make_async_copy(pieces[at], weight.at[to, :], arrived.at[at, 0]),
                pltpu.make_async_copy(own_ref.at[:, columns], own_rows.at[:, to], arrived.at[at, 1]),
                pltpu.make_async_copy(other_ref.at[:, columns], other_rows.at[:, to], arrived.at[at, 2]),
            ]
        )
    for copy in copies:
        for one in copy:
            one.start()
    for at in range(4):
        for copy in copies[2 * at : 2 * at + 2]:
            for one in copy:
                one.wait()
        to = slice(2 * at * SHARD, (2 * at + 2) * SHARD)
        for rows, out in ((own_rows, own_out), (other_rows, other_out)):
            part = jnp.dot(rows[:, to], weight[to, :], preferred_element_type=F32)
            if at == 0:
                out[...] = part
            else:
                out[...] += part


def project(hidden, other, which, pieces):
    cols = pieces[0].shape[1]
    out = jax.ShapeDtypeStruct((TOK, cols), F32)
    return pl.pallas_call(
        project_kernel,
        in_specs=[pl.BlockSpec(memory_space=pltpu.SMEM)] + [pl.BlockSpec(memory_space=pl.ANY)] * 10,
        out_specs=[pl.BlockSpec(memory_space=pltpu.VMEM)] * 2,
        out_shape=[out, out],
        scratch_shapes=[
            pltpu.VMEM((TOK, 8 * SHARD), BF16),
            pltpu.VMEM((TOK, 8 * SHARD), BF16),
            pltpu.VMEM((8 * SHARD, cols), BF16),
            pltpu.SemaphoreType.DMA((8, 3)),
        ],
        compiler_params=pltpu.CompilerParams(vmem_limit_bytes=VMEM_LIMIT),
        cost_estimate=pl.CostEstimate(
            flops=4 * TOK * 8 * SHARD * cols, bytes_accessed=12 * 2**20, transcendentals=0
        ),
    )(which, hidden, other, *pieces)


QUERY_STEP = 768


def query_kernel(hidden_ref, weight_ref, out_ref, total):
    step = pl.program_id(0)
    part = jnp.dot(hidden_ref[...], weight_ref[...], preferred_element_type=F32)

    @pl.when(step == 0)
    def _():
        total[...] = part

    @pl.when(step > 0)
    def _():
        total[...] += part

    @pl.when(step == pl.num_programs(0) - 1)
    def _():
        out_ref[...] = total[...].astype(BF16)


def project_queries(hidden, weight):
    cols = weight.shape[1]
    return pl.pallas_call(
        query_kernel,
        grid=(D // QUERY_STEP,),
        in_specs=[
            pl.BlockSpec((TOK, QUERY_STEP), lambda i: (0, i)),
            pl.BlockSpec((QUERY_STEP, cols), lambda i: (i, 0)),
        ],
        out_specs=pl.BlockSpec((TOK, cols), lambda i: (0, 0)),
        out_shape=jax.ShapeDtypeStruct((TOK, cols), BF16),
        scratch_shapes=[pltpu.VMEM((TOK, cols), F32)],
        compiler_params=pltpu.CompilerParams(vmem_limit_bytes=VMEM_LIMIT),
        cost_estimate=pl.CostEstimate(
            flops=2 * TOK * D * cols, bytes_accessed=16 * 2**20, transcendentals=0
        ),
    )(hidden, weight)


def attend_kernel(
    flags, query_ref, *refs
):
    pair_refs, refs = refs[:4], refs[4:]
    out_ref, query, keys, value, accum, best, largest, ready, arrived = refs
    side = flags[SPANS]
    heads = HEADS // 8
    loads = []
    for at in range(4):
        rows = pl.ds(pl.multiple_of(at * 128 + side * 64, 64), 64)
        to = query.at[at * 64 : at * 64 + 64, :]
        loads.append(pltpu.make_async_copy(query_ref.at[rows, :], to, ready.at[at]))
    pairs = []
    for ref in pair_refs:
        for at in range(SPANS // 4):
            block, rows = len(pairs), slice(at * TOK, (at + 1) * TOK)
            pairs.append(
                (
                    pltpu.make_async_copy(ref.at[rows, :HEAD], keys.at[block], arrived.at[block, 0]),
                    pltpu.make_async_copy(ref.at[rows, HEAD:], value.at[block, :, :HEAD], arrived.at[block, 1]),
                )
            )
    for load in loads:
        load.start()
    for key, mixed in pairs:
        key.start()
        mixed.start()
    value[:, :, HEAD:] = jnp.ones((SPANS, TOK, HEAD), BF16)
    accum[...] = jnp.zeros_like(accum)
    largest[...] = jnp.zeros_like(largest)
    for load in loads:
        load.wait()
    ones = jnp.ones((HEAD, HEAD), BF16)

    def squares(rows):
        sums = jnp.dot(rows * rows, ones, preferred_element_type=F32)
        return jnp.max(sums.reshape(rows.shape[0] // 8, 8, HEAD), axis=0)

    for head in range(heads):
        largest[0] = jnp.maximum(largest[0], squares(query[:, head * HEAD : (head + 1) * HEAD]))

    def step_small(block):
        key, extended = keys[block], value[block]
        largest[1] = jnp.maximum(largest[1], squares(key))
        for head in range(heads):
            scores = lax.dot_general(
                query[:, head * HEAD : (head + 1) * HEAD],
                key,
                (((1,), (1,)), ((), ())),
                preferred_element_type=F32,
            )
            probs = jnp.exp2(scores * SCALE2).astype(BF16)
            accum[head] += jnp.dot(probs, extended, preferred_element_type=F32)

    def step_any(block):
        def one(head, carry):
            scores = lax.dot_general(
                query[:, pl.ds(pl.multiple_of(head * HEAD, HEAD), HEAD)],
                keys[block],
                (((1,), (1,)), ((), ())),
                preferred_element_type=F32,
            )
            old = best[head]
            new = jnp.maximum(old, jnp.max(scores, axis=1, keepdims=True))
            best[head] = new
            probs = jnp.exp2((scores - new[:, :1]) * SCALE2).astype(BF16)
            factor = jnp.exp2((old - new) * SCALE2)
            accum[head] = accum[head] * factor[:, :1] + jnp.dot(
                probs, value[block], preferred_element_type=F32
            )
            return carry

        lax.fori_loop(0, heads, one, 0)

    def step(block, carry):
        for at, to in enumerate((keys.at[block], value.at[block, :, :HEAD])):
            pltpu.make_async_copy(pair_refs[0].at[:TOK, :HEAD], to, arrived.at[block, at]).wait()

        @pl.when(flags[block] > 0)
        def _():
            step_small(block)

        return carry

    lax.fori_loop(0, SPANS, step, 0)
    bound = jnp.max(largest[0]) * jnp.max(largest[1]) * (1.03 * SCALE2 * SCALE2)

    @pl.when(jnp.logical_not(bound <= SAFE_EXPONENT * SAFE_EXPONENT))
    def _():
        accum[...] = jnp.zeros_like(accum)
        best[...] = jnp.full_like(best, NEG_LARGE)

        def again(block, carry):
            @pl.when(flags[block] > 0)
            def _():
                step_any(block)

            return carry

        lax.fori_loop(0, SPANS, again, 0)

    for head in range(heads):
        mixed = accum[head]
        out_ref[:, head * HEAD : (head + 1) * HEAD] = (mixed[:, :HEAD] / mixed[:, HEAD:]).astype(BF16)


def attend(flags, queries, pairs):
    half, heads = TOK // 2, HEADS // 8
    return pl.pallas_call(
        attend_kernel,
        in_specs=[pl.BlockSpec(memory_space=pltpu.SMEM)] + [pl.BlockSpec(memory_space=pl.ANY)] * 5,
        out_specs=pl.BlockSpec(memory_space=pltpu.VMEM),
        out_shape=jax.ShapeDtypeStruct((half, 2 * GCOLS), BF16),
        scratch_shapes=[
            pltpu.VMEM((half, 2 * GCOLS), BF16),
            pltpu.VMEM((SPANS, TOK, HEAD), BF16),
            pltpu.VMEM((SPANS, TOK, 2 * HEAD), BF16),
            pltpu.VMEM((heads, half, 2 * HEAD), F32),
            pltpu.VMEM((heads, half, HEAD), F32),
            pltpu.VMEM((2, 8, HEAD), F32),
            pltpu.SemaphoreType.DMA((4,)),
            pltpu.SemaphoreType.DMA((SPANS, 2)),
        ],
        compiler_params=pltpu.CompilerParams(vmem_limit_bytes=VMEM_LIMIT),
        cost_estimate=pl.CostEstimate(
            flops=heads * 6 * half * SPANS * TOK * HEAD, bytes_accessed=6 * 2**20, transcendentals=0
        ),
    )(flags, queries, *pairs)


OUT_GROUPS = 4
OUT_COLS = D // OUT_GROUPS
Z_ORDER = (2, 1, 3, 0)


def output_kernel(group, place, mine_ref, got_ref, weight_ref, far, up, down, stay, rows_of, wide, arrived):
    z, side = place[0], place[1]
    copies = []
    for at in range(SPANS // OUT_GROUPS):
        for which, chosen in enumerate((side, 1 - side)):
            start = (chosen * SPANS + group * (SPANS // OUT_GROUPS) + at) * 2 * SHARD
            source = weight_ref.at[pl.ds(pl.multiple_of(start, 2 * SHARD), 2 * SHARD), :]
            to = wide.at[which, :, at * SHARD : (at + 1) * SHARD]
            copies.append(pltpu.make_async_copy(source, to, arrived.at[at, which]))
    for copy in copies:
        copy.start()
    for at, step in enumerate(Z_ORDER):
        rows = pl.ds(pl.multiple_of(((z + step) % 4) * 64, 64), 64)
        rows_of[0, at * 64 : at * 64 + 64, :] = mine_ref[rows, :]
        rows_of[1, at * 64 : at * 64 + 64, :] = got_ref[rows, :]
    for part in range(2):
        for copy in copies[part * 4 : part * 4 + 4]:
            copy.wait()
        columns = slice(part * 2 * SHARD, (part + 1) * 2 * SHARD)
        total = jnp.dot(rows_of[0], wide[0, :, columns], preferred_element_type=F32)
        total += jnp.dot(rows_of[1], wide[1, :, columns], preferred_element_type=F32)
        total = total.astype(BF16)
        for index, out in enumerate((far, up, down, stay)):
            out[:, columns] = total[index * 64 : index * 64 + 64]


def output_partial(group, place, mine, got, weights):
    vmem = pl.BlockSpec(memory_space=pltpu.VMEM)
    return pl.pallas_call(
        functools.partial(output_kernel, group),
        in_specs=[pl.BlockSpec(memory_space=pltpu.SMEM), vmem, vmem, pl.BlockSpec(memory_space=pl.ANY)],
        out_specs=[vmem] * 4,
        out_shape=[jax.ShapeDtypeStruct((64, OUT_COLS), BF16)] * 4,
        scratch_shapes=[
            pltpu.VMEM((2, TOK // 2, 2 * GCOLS), BF16),
            pltpu.VMEM((2, 2 * SHARD, OUT_COLS), BF16),
            pltpu.SemaphoreType.DMA((SPANS // OUT_GROUPS, 2)),
        ],
        compiler_params=pltpu.CompilerParams(vmem_limit_bytes=VMEM_LIMIT),
        cost_estimate=pl.CostEstimate(
            flops=2 * TOK // 2 * OUT_COLS * 4 * GCOLS, bytes_accessed=6 * 2**20, transcendentals=0
        ),
    )(place, mine, got, weights)


def reduce_over_z(far, up, down, stay, sign):
    near, back = (up, down) if sign > 0 else (down, up)
    passed = move(far, dz=sign)
    behind = move(back, dz=-sign)
    near = (near.astype(F32) + passed.astype(F32)).astype(BF16)
    ahead = move(near, dz=sign)
    return (stay.astype(F32) + ahead.astype(F32) + behind.astype(F32)).astype(BF16), passed


def per_device(hidden, span_ids, w_query, w_keyval, w_out):
    span, uly = lax.axis_index("span"), lax.axis_index("uly")
    xl, y, core = span // 8, (span // 2) % 4, span % 2
    z, xh = uly // 2, uly % 2
    as_int = lambda values: jnp.stack([jnp.asarray(v, jnp.int32) for v in values])

    chips = [x * 4 + (y + dy) % 4 for dy in (0, 3, 1, 2) for x in (xl, 1 - xl)]
    which = as_int([j * 2 + core for j in chips])
    place = as_int([z, xh])
    block_ids = span_ids.reshape(SPANS, TOK)[:, 0]
    seen = (block_ids <= block_ids[span]).astype(jnp.int32)
    order = [chips[at] * 2 + core for at in (0, 1, 2, 4, 3, 5, 6, 7)]
    seen = seen[as_int(order + [at + 1 - 2 * core for at in order])]
    send_flags = jnp.concatenate([seen, as_int([1 - xh])])
    mine_flags = jnp.concatenate([seen, as_int([xh])])

    query_weight = lax.all_gather(w_query, "span", axis=0, tiled=True)
    planes = [
        [index_of(span // 8, span // 2 % 4, span % 2, at, side) for side in range(2) for span in range(SPANS)]
        for at in range(4)
    ]

    own = jnp.concatenate([w_keyval[:, 0], w_keyval[:, 1]], axis=1)
    side = move(own, swap_xl=True)
    up, down = move(own, dy=1), move(own, dy=-1)
    other_hidden = move(hidden, swap_c=True)
    side, up, down, which, place, send_flags, mine_flags = lax.optimization_barrier(
        (side, up, down, which, place, send_flags, mine_flags)
    )
    side_up, side_down = move(side, dy=1), move(side, dy=-1)
    up, side_up, side_down = lax.optimization_barrier((up, side_up, side_down))
    far, side_far = move(up, dy=1), move(side_down, dy=-1)
    weights = lax.all_gather(
        after(w_out, far, side_far), BOTH, axis=0, tiled=True, axis_index_groups=planes
    )
    pieces = [own, side, up, side_up, down, side_down, far, side_far]
    pair_own, pair_other = project(hidden, other_hidden, which, pieces)
    pair = (pair_own + move(pair_other, swap_c=True)).astype(BF16)

    pair_side = move(pair, swap_xl=True)
    pair_up, pair_down = move(pair, dy=1), move(pair, dy=-1)
    pair_side, pair_up, pair_down = lax.optimization_barrier((pair_side, pair_up, pair_down))
    pair_side_up, pair_side_down = move(pair_side, dy=1), move(pair_side, dy=-1)
    pairs = jnp.concatenate([pair, pair_side, pair_up, pair_down], axis=0)
    other_pairs = move(pairs, swap_c=True)
    pair_down, pair_side_up, pair_side_down = lax.optimization_barrier((pair_down, pair_side_up, pair_side_down))
    pair_far, pair_side_far = move(pair_down, dy=-1), move(pair_side_up, dy=1)
    more_pairs = jnp.concatenate([pair_side_up, pair_side_down, pair_far, pair_side_far], axis=0)
    pairs = [pairs, more_pairs, other_pairs, move(more_pairs, swap_c=True)]

    queries = project_queries(hidden, query_weight)
    send = attend(send_flags, queries, pairs)
    got = move(send, swap_xh=True)
    mine = attend(after(mine_flags, send), queries, pairs)

    totals, passed = [], []
    for group in range(OUT_GROUPS):
        if group > 1:
            place = after(place, passed[group - 2])
        parts = output_partial(group, place, mine, got, weights)
        total, through = reduce_over_z(*parts, 1 if group % 2 == 0 else -1)
        totals.append(total)
        passed.append(through)
    return jnp.concatenate(totals, axis=1)


def solution(mesh):
    in_specs = (P("span", None), P(), P("span", "uly"), P("span", None, "uly"), P("uly", "span"))
    out_specs = P(("span", "uly"), None)
    return jax.shard_map(
        per_device, mesh=mesh, in_specs=in_specs, out_specs=out_specs, check_vma=False
    )
```

```python
import functools
import math

import jax
import jax.numpy as jnp
from jax import lax
from jax.experimental import pallas as pl
from jax.experimental.pallas import tpu as pltpu
from jax.sharding import PartitionSpec as P

HEADS = 48
HEAD = 128
D = 6144
SPANS = 16
TOK = 512
SHARD = D // SPANS
GROUP = 3
GCOLS = GROUP * HEAD
SCALE2 = math.log2(math.e) / math.sqrt(HEAD)
SAFE_EXPONENT = 90.0
NEG_LARGE = -1e30
VMEM_LIMIT = 60 * 2**20
BOTH = ("span", "uly")
F32 = jnp.float32
BF16 = jnp.bfloat16


def coords(index):
    span, uly = index // 8, index % 8
    return span // 8, (span // 2) % 4, span % 2, uly // 2, uly % 2


def index_of(xl, y, c, z, xh):
    return (xl * 8 + y * 2 + c) * 8 + z * 2 + xh


def move(array, dx=0, dy=0, dz=0, swap_xl=False, swap_xh=False, swap_c=False):
    pairs = []
    for source in range(128):
        xl, y, c, z, xh = coords(source)
        x = (xh * 2 + xl + dx) % 4
        xh, xl = x // 2, x % 2
        if swap_xl:
            xl = 1 - xl
        if swap_xh:
            xh = 1 - xh
        if swap_c:
            c = 1 - c
        pairs.append((source, index_of(xl, (y + dy) % 4, c, (z + dz) % 4, xh)))
    return lax.ppermute(array, BOTH, pairs)


def after(array, *results):
    return lax.optimization_barrier((array, *results))[0]


def pick_kernel(which, hidden_ref, out_ref, arrived):
    copies = []
    for at in range(8):
        columns = pl.ds(pl.multiple_of(which[at] * SHARD, 128), SHARD)
        to = out_ref.at[:, at * SHARD : (at + 1) * SHARD]
        copies.append(pltpu.make_async_copy(hidden_ref.at[:, columns], to, arrived.at[at]))
    for copy in copies:
        copy.start()
    for copy in copies:
        copy.wait()


def pick_columns(hidden, which):
    return pl.pallas_call(
        pick_kernel,
        in_specs=[pl.BlockSpec(memory_space=pltpu.SMEM), pl.BlockSpec(memory_space=pl.ANY)],
        out_specs=pl.BlockSpec(memory_space=pltpu.VMEM),
        out_shape=jax.ShapeDtypeStruct((TOK, 8 * SHARD), BF16),
        scratch_shapes=[pltpu.SemaphoreType.DMA((8,))],
        compiler_params=pltpu.CompilerParams(vmem_limit_bytes=VMEM_LIMIT),
        cost_estimate=pl.CostEstimate(flops=0, bytes_accessed=4 * TOK * 8 * SHARD, transcendentals=0),
    )(which, hidden)


def project_kernel(which, own_ref, other_ref, *refs):
    pieces, (own_out, other_out, own_rows, other_rows, weight, arrived) = refs[:8], refs[8:]
    copies = []
    for at in range(8):
        columns = pl.ds(pl.multiple_of(which[at] * SHARD, 128), SHARD)
        other = pl.ds(pl.multiple_of(which[8 + at] * SHARD, 128), SHARD)
        to = slice(at * SHARD, (at + 1) * SHARD)
        copies.append(
            [
                pltpu.make_async_copy(pieces[at], weight.at[to, :], arrived.at[at, 0]),
                pltpu.make_async_copy(own_ref.at[:, columns], own_rows.at[:, to], arrived.at[at, 1]),
                pltpu.make_async_copy(other_ref.at[:, other], other_rows.at[:, to], arrived.at[at, 2]),
            ]
        )
    for copy in copies:
        for one in copy:
            one.start()
    for at in range(4):
        for copy in copies[2 * at : 2 * at + 2]:
            for one in copy:
                one.wait()
        to = slice(2 * at * SHARD, (2 * at + 2) * SHARD)
        for rows, out in ((own_rows, own_out), (other_rows, other_out)):
            part = jnp.dot(rows[:, to], weight[to, :], preferred_element_type=F32)
            if at == 0:
                out[...] = part
            else:
                out[...] += part


def project(hidden, other, which, pieces):
    cols = pieces[0].shape[1]
    out = jax.ShapeDtypeStruct((TOK, cols), F32)
    return pl.pallas_call(
        project_kernel,
        in_specs=[pl.BlockSpec(memory_space=pltpu.SMEM)] + [pl.BlockSpec(memory_space=pl.ANY)] * 10,
        out_specs=[pl.BlockSpec(memory_space=pltpu.VMEM)] * 2,
        out_shape=[out, out],
        scratch_shapes=[
            pltpu.VMEM((TOK, 8 * SHARD), BF16),
            pltpu.VMEM((TOK, 8 * SHARD), BF16),
            pltpu.VMEM((8 * SHARD, cols), BF16),
            pltpu.SemaphoreType.DMA((8, 3)),
        ],
        compiler_params=pltpu.CompilerParams(vmem_limit_bytes=VMEM_LIMIT),
        cost_estimate=pl.CostEstimate(
            flops=4 * TOK * 8 * SHARD * cols, bytes_accessed=12 * 2**20, transcendentals=0
        ),
    )(which, hidden, other, *pieces)


QUERY_STEP = 768


def query_kernel(hidden_ref, weight_ref, out_ref, total):
    step = pl.program_id(0)
    part = jnp.dot(hidden_ref[...], weight_ref[...], preferred_element_type=F32)

    @pl.when(step == 0)
    def _():
        total[...] = part

    @pl.when(step > 0)
    def _():
        total[...] += part

    @pl.when(step == pl.num_programs(0) - 1)
    def _():
        out_ref[...] = total[...].astype(BF16)


def project_queries(hidden, weight):
    cols = weight.shape[1]
    return pl.pallas_call(
        query_kernel,
        grid=(D // QUERY_STEP,),
        in_specs=[
            pl.BlockSpec((TOK, QUERY_STEP), lambda i: (0, i)),
            pl.BlockSpec((QUERY_STEP, cols), lambda i: (i, 0)),
        ],
        out_specs=pl.BlockSpec((TOK, cols), lambda i: (0, 0)),
        out_shape=jax.ShapeDtypeStruct((TOK, cols), BF16),
        scratch_shapes=[pltpu.VMEM((TOK, cols), F32)],
        compiler_params=pltpu.CompilerParams(vmem_limit_bytes=VMEM_LIMIT),
        cost_estimate=pl.CostEstimate(
            flops=2 * TOK * D * cols, bytes_accessed=16 * 2**20, transcendentals=0
        ),
    )(hidden, weight)


def attend_kernel(
    flags, query_ref, *refs
):
    pair_refs, refs = refs[:4], refs[4:]
    out_ref, query, keys, value, accum, best, largest, ready, arrived = refs
    side = flags[SPANS]
    heads = HEADS // 8
    loads = []
    for at in range(4):
        rows = pl.ds(pl.multiple_of(at * 128 + side * 64, 64), 64)
        to = query.at[at * 64 : at * 64 + 64, :]
        loads.append(pltpu.make_async_copy(query_ref.at[rows, :], to, ready.at[at]))
    pairs = []
    for ref in pair_refs:
        for at in range(SPANS // 4):
            block, rows = len(pairs), slice(at * TOK, (at + 1) * TOK)
            pairs.append(
                (
                    pltpu.make_async_copy(ref.at[rows, :HEAD], keys.at[block], arrived.at[block, 0]),
                    pltpu.make_async_copy(ref.at[rows, HEAD:], value.at[block, :, :HEAD], arrived.at[block, 1]),
                )
            )
    for load in loads:
        load.start()
    for key, mixed in pairs:
        key.start()
        mixed.start()
    value[:, :, HEAD:] = jnp.ones((SPANS, TOK, HEAD), BF16)
    accum[...] = jnp.zeros_like(accum)
    largest[...] = jnp.zeros_like(largest)
    for load in loads:
        load.wait()
    ones = jnp.ones((HEAD, HEAD), BF16)

    def squares(rows):
        sums = jnp.dot(rows * rows, ones, preferred_element_type=F32)
        return jnp.max(sums.reshape(rows.shape[0] // 8, 8, HEAD), axis=0)

    for head in range(heads):
        largest[0] = jnp.maximum(largest[0], squares(query[:, head * HEAD : (head + 1) * HEAD]))

    def step_small(block):
        key, extended = keys[block], value[block]
        largest[1] = jnp.maximum(largest[1], squares(key))
        for head in range(heads):
            scores = lax.dot_general(
                query[:, head * HEAD : (head + 1) * HEAD],
                key,
                (((1,), (1,)), ((), ())),
                preferred_element_type=F32,
            )
            probs = jnp.exp2(scores * SCALE2).astype(BF16)
            accum[head] += jnp.dot(probs, extended, preferred_element_type=F32)

    def step_any(block):
        def one(head, carry):
            scores = lax.dot_general(
                query[:, pl.ds(pl.multiple_of(head * HEAD, HEAD), HEAD)],
                keys[block],
                (((1,), (1,)), ((), ())),
                preferred_element_type=F32,
            )
            old = best[head]
            new = jnp.maximum(old, jnp.max(scores, axis=1, keepdims=True))
            best[head] = new
            probs = jnp.exp2((scores - new[:, :1]) * SCALE2).astype(BF16)
            factor = jnp.exp2((old - new) * SCALE2)
            accum[head] = accum[head] * factor[:, :1] + jnp.dot(
                probs, value[block], preferred_element_type=F32
            )
            return carry

        lax.fori_loop(0, heads, one, 0)

    def step(block, carry):
        for at, to in enumerate((keys.at[block], value.at[block, :, :HEAD])):
            pltpu.make_async_copy(pair_refs[0].at[:TOK, :HEAD], to, arrived.at[block, at]).wait()

        @pl.when(flags[block] > 0)
        def _():
            step_small(block)

        return carry

    lax.fori_loop(0, SPANS, step, 0)
    bound = jnp.max(largest[0]) * jnp.max(largest[1]) * (1.03 * SCALE2 * SCALE2)

    @pl.when(jnp.logical_not(bound <= SAFE_EXPONENT * SAFE_EXPONENT))
    def _():
        accum[...] = jnp.zeros_like(accum)
        best[...] = jnp.full_like(best, NEG_LARGE)

        def again(block, carry):
            @pl.when(flags[block] > 0)
            def _():
                step_any(block)

            return carry

        lax.fori_loop(0, SPANS, again, 0)

    for head in range(heads):
        mixed = accum[head]
        out_ref[:, head * HEAD : (head + 1) * HEAD] = (mixed[:, :HEAD] / mixed[:, HEAD:]).astype(BF16)


def attend(flags, queries, pairs):
    half, heads = TOK // 2, HEADS // 8
    return pl.pallas_call(
        attend_kernel,
        in_specs=[pl.BlockSpec(memory_space=pltpu.SMEM)] + [pl.BlockSpec(memory_space=pl.ANY)] * 5,
        out_specs=pl.BlockSpec(memory_space=pltpu.VMEM),
        out_shape=jax.ShapeDtypeStruct((half, 2 * GCOLS), BF16),
        scratch_shapes=[
            pltpu.VMEM((half, 2 * GCOLS), BF16),
            pltpu.VMEM((SPANS, TOK, HEAD), BF16),
            pltpu.VMEM((SPANS, TOK, 2 * HEAD), BF16),
            pltpu.VMEM((heads, half, 2 * HEAD), F32),
            pltpu.VMEM((heads, half, HEAD), F32),
            pltpu.VMEM((2, 8, HEAD), F32),
            pltpu.SemaphoreType.DMA((4,)),
            pltpu.SemaphoreType.DMA((SPANS, 2)),
        ],
        compiler_params=pltpu.CompilerParams(vmem_limit_bytes=VMEM_LIMIT),
        cost_estimate=pl.CostEstimate(
            flops=heads * 6 * half * SPANS * TOK * HEAD, bytes_accessed=6 * 2**20, transcendentals=0
        ),
    )(flags, queries, *pairs)


OUT_GROUPS = 4
OUT_COLS = D // OUT_GROUPS
Z_ORDER = (2, 1, 3, 0)


def output_kernel(group, place, mine_ref, got_ref, weight_ref, *refs):
    outs, (mine, got, rows_of, wide, result, loaded, arrived, stored) = refs[:4], refs[4:]
    z, side = place[0], place[1]
    loads = [
        pltpu.make_async_copy(mine_ref, mine, loaded.at[0]),
        pltpu.make_async_copy(got_ref, got, loaded.at[1]),
    ]
    copies = []
    for at in range(SPANS // OUT_GROUPS):
        for which, chosen in enumerate((side, 1 - side)):
            start = (chosen * SPANS + group * (SPANS // OUT_GROUPS) + at) * 2 * SHARD
            source = weight_ref.at[pl.ds(pl.multiple_of(start, 2 * SHARD), 2 * SHARD), :]
            to = wide.at[which, :, at * SHARD : (at + 1) * SHARD]
            copies.append(pltpu.make_async_copy(source, to, arrived.at[at, which]))
    for copy in loads + copies:
        copy.start()
    for copy in loads:
        copy.wait()
    for at, step in enumerate(Z_ORDER):
        rows = pl.ds(pl.multiple_of(((z + step) % 4) * 64, 64), 64)
        rows_of[0, at * 64 : at * 64 + 64, :] = mine[rows, :]
        rows_of[1, at * 64 : at * 64 + 64, :] = got[rows, :]
    stores = []
    for part in range(2):
        for copy in copies[part * 4 : part * 4 + 4]:
            copy.wait()
        columns = slice(part * 2 * SHARD, (part + 1) * 2 * SHARD)
        total = jnp.dot(rows_of[0], wide[0, :, columns], preferred_element_type=F32)
        total += jnp.dot(rows_of[1], wide[1, :, columns], preferred_element_type=F32)
        result[part] = total.astype(BF16)
        for index, out in enumerate(outs):
            source = result.at[part, index * 64 : index * 64 + 64, :]
            stores.append(pltpu.make_async_copy(source, out.at[:, columns], stored.at[part, index]))
            stores[-1].start()
    for store in stores:
        store.wait()


def output_partial(group, place, mine, got, weights):
    anywhere = pl.BlockSpec(memory_space=pl.ANY)
    half = TOK // 2
    return pl.pallas_call(
        functools.partial(output_kernel, group),
        in_specs=[pl.BlockSpec(memory_space=pltpu.SMEM)] + [anywhere] * 3,
        out_specs=[anywhere] * 4,
        out_shape=[jax.ShapeDtypeStruct((64, OUT_COLS), BF16)] * 4,
        scratch_shapes=[
            pltpu.VMEM((half, 2 * GCOLS), BF16),
            pltpu.VMEM((half, 2 * GCOLS), BF16),
            pltpu.VMEM((2, half, 2 * GCOLS), BF16),
            pltpu.VMEM((2, 2 * SHARD, OUT_COLS), BF16),
            pltpu.VMEM((2, half, OUT_COLS // 2), BF16),
            pltpu.SemaphoreType.DMA((2,)),
            pltpu.SemaphoreType.DMA((SPANS // OUT_GROUPS, 2)),
            pltpu.SemaphoreType.DMA((2, 4)),
        ],
        compiler_params=pltpu.CompilerParams(vmem_limit_bytes=VMEM_LIMIT),
        cost_estimate=pl.CostEstimate(
            flops=2 * TOK // 2 * OUT_COLS * 4 * GCOLS, bytes_accessed=6 * 2**20, transcendentals=0
        ),
    )(place, mine, got, weights)


def reduce_over_z(far, up, down, stay, sign):
    near, back = (up, down) if sign > 0 else (down, up)
    passed = move(far, dz=sign)
    behind = move(back, dz=-sign)
    near = (near.astype(F32) + passed.astype(F32)).astype(BF16)
    ahead = move(near, dz=sign)
    return (stay.astype(F32) + ahead.astype(F32) + behind.astype(F32)).astype(BF16), passed


def per_device(hidden, span_ids, w_query, w_keyval, w_out):
    span, uly = lax.axis_index("span"), lax.axis_index("uly")
    xl, y, core = span // 8, (span // 2) % 4, span % 2
    z, xh = uly // 2, uly % 2
    as_int = lambda values: jnp.stack([jnp.asarray(v, jnp.int32) for v in values])

    chips = [x * 4 + (y + dy) % 4 for dy in (0, 3, 1, 2) for x in (xl, 1 - xl)]
    which = as_int([j * 2 + core for j in chips] + chips)
    place = as_int([z, xh])
    block_ids = span_ids.reshape(SPANS, TOK)[:, 0]
    seen = (block_ids <= block_ids[span]).astype(jnp.int32)
    order = [chips[at] * 2 + core for at in (0, 1, 2, 4, 3, 5, 6, 7)]
    seen = seen[as_int(order + [at + 1 - 2 * core for at in order])]
    send_flags = jnp.concatenate([seen, as_int([1 - xh])])
    mine_flags = jnp.concatenate([seen, as_int([xh])])

    query_weight = lax.all_gather(w_query, "span", axis=0, tiled=True)
    planes = [
        [index_of(span // 8, span // 2 % 4, span % 2, at, side) for side in range(2) for span in range(SPANS)]
        for at in range(4)
    ]

    own = jnp.concatenate([w_keyval[:, 0], w_keyval[:, 1]], axis=1)
    side = move(own, swap_xl=True)
    up, down = move(own, dy=1), move(own, dy=-1)
    elsewhere = after(as_int([j * 2 + 1 - core for j in range(8)]), side)
    other_hidden = move(pick_columns(hidden, elsewhere), swap_c=True)
    side, up, down, which, place, send_flags, mine_flags = lax.optimization_barrier(
        (side, up, down, which, place, send_flags, mine_flags)
    )
    side_up, side_down = move(side, dy=1), move(side, dy=-1)
    up, side_up, side_down = lax.optimization_barrier((up, side_up, side_down))
    far, side_far = move(up, dy=1), move(side_down, dy=-1)
    weights = lax.all_gather(
        after(w_out, far, side_far), BOTH, axis=0, tiled=True, axis_index_groups=planes
    )
    pieces = [own, side, up, side_up, down, side_down, far, side_far]
    pair_own, pair_other = project(hidden, other_hidden, which, pieces)
    pair = (pair_own + move(pair_other, swap_c=True)).astype(BF16)

    pair_side = move(pair, swap_xl=True)
    pair_up, pair_down = move(pair, dy=1), move(pair, dy=-1)
    pair_side, pair_up, pair_down = lax.optimization_barrier((pair_side, pair_up, pair_down))
    pair_side_up, pair_side_down = move(pair_side, dy=1), move(pair_side, dy=-1)
    pairs = jnp.concatenate([pair, pair_side, pair_up, pair_down], axis=0)
    other_pairs = move(pairs, swap_c=True)
    pair_down, pair_side_up, pair_side_down = lax.optimization_barrier((pair_down, pair_side_up, pair_side_down))
    pair_far, pair_side_far = move(pair_down, dy=-1), move(pair_side_up, dy=1)
    more_pairs = jnp.concatenate([pair_side_up, pair_side_down, pair_far, pair_side_far], axis=0)
    pairs = [pairs, more_pairs, other_pairs, move(more_pairs, swap_c=True)]

    queries = project_queries(hidden, query_weight)
    send = attend(send_flags, queries, pairs)
    got = move(send, swap_xh=True)
    mine = attend(after(mine_flags, send), queries, pairs)

    totals, passed = [], []
    for group in range(OUT_GROUPS):
        if group == OUT_GROUPS - 1:
            place = after(place, *passed[:2])
        parts = output_partial(group, place, mine, got, weights)
        total, through = reduce_over_z(*parts, 1 if group % 2 == 0 else -1)
        totals.append(total)
        passed.append(through)
    return jnp.concatenate(totals, axis=1)


def solution(mesh):
    in_specs = (P("span", None), P(), P("span", "uly"), P("span", None, "uly"), P("uly", "span"))
    out_specs = P(("span", "uly"), None)
    return jax.shard_map(
        per_device, mesh=mesh, in_specs=in_specs, out_specs=out_specs, check_vma=False
    )
```

```python
import functools
import math

import jax
import jax.numpy as jnp
from jax import lax
from jax.experimental import pallas as pl
from jax.experimental.pallas import tpu as pltpu
from jax.sharding import PartitionSpec as P

HEADS = 48
HEAD = 128
D = 6144
SPANS = 16
TOK = 512
SHARD = D // SPANS
GROUP = 3
GCOLS = GROUP * HEAD
SCALE2 = math.log2(math.e) / math.sqrt(HEAD)
SAFE_EXPONENT = 90.0
NEG_LARGE = -1e30
VMEM_LIMIT = 60 * 2**20
BOTH = ("span", "uly")
F32 = jnp.float32
BF16 = jnp.bfloat16


def coords(index):
    span, uly = index // 8, index % 8
    return span // 8, (span // 2) % 4, span % 2, uly // 2, uly % 2


def index_of(xl, y, c, z, xh):
    return (xl * 8 + y * 2 + c) * 8 + z * 2 + xh


def move(array, dx=0, dy=0, dz=0, swap_xl=False, swap_xh=False, swap_c=False):
    pairs = []
    for source in range(128):
        xl, y, c, z, xh = coords(source)
        x = (xh * 2 + xl + dx) % 4
        xh, xl = x // 2, x % 2
        if swap_xl:
            xl = 1 - xl
        if swap_xh:
            xh = 1 - xh
        if swap_c:
            c = 1 - c
        pairs.append((source, index_of(xl, (y + dy) % 4, c, (z + dz) % 4, xh)))
    return lax.ppermute(array, BOTH, pairs)


def after(array, *results):
    return lax.optimization_barrier((array, *results))[0]


def pick_kernel(which, hidden_ref, out_ref, arrived):
    copies = []
    for at in range(8):
        columns = pl.ds(pl.multiple_of(which[at] * SHARD, 128), SHARD)
        to = out_ref.at[:, at * SHARD : (at + 1) * SHARD]
        copies.append(pltpu.make_async_copy(hidden_ref.at[:, columns], to, arrived.at[at]))
    for copy in copies:
        copy.start()
    for copy in copies:
        copy.wait()


def pick_columns(hidden, which):
    return pl.pallas_call(
        pick_kernel,
        in_specs=[pl.BlockSpec(memory_space=pltpu.SMEM), pl.BlockSpec(memory_space=pl.ANY)],
        out_specs=pl.BlockSpec(memory_space=pltpu.VMEM),
        out_shape=jax.ShapeDtypeStruct((TOK, 8 * SHARD), BF16),
        scratch_shapes=[pltpu.SemaphoreType.DMA((8,))],
        compiler_params=pltpu.CompilerParams(vmem_limit_bytes=VMEM_LIMIT),
        cost_estimate=pl.CostEstimate(flops=0, bytes_accessed=4 * TOK * 8 * SHARD, transcendentals=0),
    )(which, hidden)


def project_kernel(which, own_ref, other_ref, *refs):
    pieces, (own_out, other_out, own_rows, other_rows, weight, arrived) = refs[:8], refs[8:]
    copies = []
    for at in range(8):
        columns = pl.ds(pl.multiple_of(which[at] * SHARD, 128), SHARD)
        other = pl.ds(pl.multiple_of(which[8 + at] * SHARD, 128), SHARD)
        to = slice(at * SHARD, (at + 1) * SHARD)
        copies.append(
            [
                pltpu.make_async_copy(pieces[at], weight.at[to, :], arrived.at[at, 0]),
                pltpu.make_async_copy(own_ref.at[:, columns], own_rows.at[:, to], arrived.at[at, 1]),
                pltpu.make_async_copy(other_ref.at[:, other], other_rows.at[:, to], arrived.at[at, 2]),
            ]
        )
    for copy in copies:
        for one in copy:
            one.start()
    for at in range(4):
        for copy in copies[2 * at : 2 * at + 2]:
            for one in copy:
                one.wait()
        to = slice(2 * at * SHARD, (2 * at + 2) * SHARD)
        for rows, out in ((own_rows, own_out), (other_rows, other_out)):
            part = jnp.dot(rows[:, to], weight[to, :], preferred_element_type=F32)
            if at == 0:
                out[...] = part
            else:
                out[...] += part


def project(hidden, other, which, pieces):
    cols = pieces[0].shape[1]
    out = jax.ShapeDtypeStruct((TOK, cols), F32)
    return pl.pallas_call(
        project_kernel,
        in_specs=[pl.BlockSpec(memory_space=pltpu.SMEM)] + [pl.BlockSpec(memory_space=pl.ANY)] * 10,
        out_specs=[pl.BlockSpec(memory_space=pltpu.VMEM)] * 2,
        out_shape=[out, out],
        scratch_shapes=[
            pltpu.VMEM((TOK, 8 * SHARD), BF16),
            pltpu.VMEM((TOK, 8 * SHARD), BF16),
            pltpu.VMEM((8 * SHARD, cols), BF16),
            pltpu.SemaphoreType.DMA((8, 3)),
        ],
        compiler_params=pltpu.CompilerParams(vmem_limit_bytes=VMEM_LIMIT),
        cost_estimate=pl.CostEstimate(
            flops=4 * TOK * 8 * SHARD * cols, bytes_accessed=12 * 2**20, transcendentals=0
        ),
    )(which, hidden, other, *pieces)


def attend_kernel(
    flags, query_ref, *refs
):
    pair_refs, refs = refs[:4], refs[4:]
    out_ref, query, keys, value, accum, best, largest, ready, arrived = refs
    side = flags[SPANS]
    heads = HEADS // 8
    loads = []
    for at in range(4):
        rows = pl.ds(pl.multiple_of(at * 128 + side * 64, 64), 64)
        to = query.at[at * 64 : at * 64 + 64, :]
        loads.append(pltpu.make_async_copy(query_ref.at[rows, :], to, ready.at[at]))
    pairs = []
    for ref in pair_refs:
        for at in range(SPANS // 4):
            block, rows = len(pairs), slice(at * TOK, (at + 1) * TOK)
            pairs.append(
                (
                    pltpu.make_async_copy(ref.at[rows, :HEAD], keys.at[block], arrived.at[block, 0]),
                    pltpu.make_async_copy(ref.at[rows, HEAD:], value.at[block, :, :HEAD], arrived.at[block, 1]),
                )
            )
    for load in loads:
        load.start()
    for key, mixed in pairs:
        key.start()
        mixed.start()
    value[:, :, HEAD:] = jnp.ones((SPANS, TOK, HEAD), BF16)
    accum[...] = jnp.zeros_like(accum)
    largest[...] = jnp.zeros_like(largest)
    for load in loads:
        load.wait()
    ones = jnp.ones((HEAD, HEAD), BF16)

    def squares(rows):
        sums = jnp.dot(rows * rows, ones, preferred_element_type=F32)
        return jnp.max(sums.reshape(rows.shape[0] // 8, 8, HEAD), axis=0)

    for head in range(heads):
        largest[0] = jnp.maximum(largest[0], squares(query[:, head * HEAD : (head + 1) * HEAD]))

    def step_small(block):
        key, extended = keys[block], value[block]
        largest[1] = jnp.maximum(largest[1], squares(key))
        for head in range(heads):
            scores = lax.dot_general(
                query[:, head * HEAD : (head + 1) * HEAD],
                key,
                (((1,), (1,)), ((), ())),
                preferred_element_type=F32,
            )
            probs = jnp.exp2(scores * SCALE2).astype(BF16)
            accum[head] += jnp.dot(probs, extended, preferred_element_type=F32)

    def step_any(block):
        def one(head, carry):
            scores = lax.dot_general(
                query[:, pl.ds(pl.multiple_of(head * HEAD, HEAD), HEAD)],
                keys[block],
                (((1,), (1,)), ((), ())),
                preferred_element_type=F32,
            )
            old = best[head]
            new = jnp.maximum(old, jnp.max(scores, axis=1, keepdims=True))
            best[head] = new
            probs = jnp.exp2((scores - new[:, :1]) * SCALE2).astype(BF16)
            factor = jnp.exp2((old - new) * SCALE2)
            accum[head] = accum[head] * factor[:, :1] + jnp.dot(
                probs, value[block], preferred_element_type=F32
            )
            return carry

        lax.fori_loop(0, heads, one, 0)

    def step(block, carry):
        for at, to in enumerate((keys.at[block], value.at[block, :, :HEAD])):
            pltpu.make_async_copy(pair_refs[0].at[:TOK, :HEAD], to, arrived.at[block, at]).wait()

        @pl.when(flags[block] > 0)
        def _():
            step_small(block)

        return carry

    lax.fori_loop(0, SPANS, step, 0)
    bound = jnp.max(largest[0]) * jnp.max(largest[1]) * (1.03 * SCALE2 * SCALE2)

    @pl.when(jnp.logical_not(bound <= SAFE_EXPONENT * SAFE_EXPONENT))
    def _():
        accum[...] = jnp.zeros_like(accum)
        best[...] = jnp.full_like(best, NEG_LARGE)

        def again(block, carry):
            @pl.when(flags[block] > 0)
            def _():
                step_any(block)

            return carry

        lax.fori_loop(0, SPANS, again, 0)

    for head in range(heads):
        mixed = accum[head]
        out_ref[:, head * HEAD : (head + 1) * HEAD] = (mixed[:, :HEAD] / mixed[:, HEAD:]).astype(BF16)


def attend(flags, queries, pairs):
    half, heads = TOK // 2, HEADS // 8
    return pl.pallas_call(
        attend_kernel,
        in_specs=[pl.BlockSpec(memory_space=pltpu.SMEM)] + [pl.BlockSpec(memory_space=pl.ANY)] * 5,
        out_specs=pl.BlockSpec(memory_space=pltpu.VMEM),
        out_shape=jax.ShapeDtypeStruct((half, 2 * GCOLS), BF16),
        scratch_shapes=[
            pltpu.VMEM((half, 2 * GCOLS), BF16),
            pltpu.VMEM((SPANS, TOK, HEAD), BF16),
            pltpu.VMEM((SPANS, TOK, 2 * HEAD), BF16),
            pltpu.VMEM((heads, half, 2 * HEAD), F32),
            pltpu.VMEM((heads, half, HEAD), F32),
            pltpu.VMEM((2, 8, HEAD), F32),
            pltpu.SemaphoreType.DMA((4,)),
            pltpu.SemaphoreType.DMA((SPANS, 2)),
        ],
        compiler_params=pltpu.CompilerParams(vmem_limit_bytes=VMEM_LIMIT),
        cost_estimate=pl.CostEstimate(
            flops=heads * 6 * half * SPANS * TOK * HEAD, bytes_accessed=6 * 2**20, transcendentals=0
        ),
    )(flags, queries, *pairs)


OUT_GROUPS = 2
OUT_PARTS = 8 // OUT_GROUPS
OUT_COLS = D // OUT_GROUPS
Z_ORDER = (2, 1, 3, 0)


def output_kernel(group, place, mine_ref, got_ref, weight_ref, *refs):
    outs, (mine, got, rows_of, wide, result, loaded, arrived, stored) = refs[:4], refs[4:]
    z, side = place[0], place[1]
    loads = [
        pltpu.make_async_copy(mine_ref, mine, loaded.at[0]),
        pltpu.make_async_copy(got_ref, got, loaded.at[1]),
    ]
    copies = []
    for at in range(SPANS // OUT_GROUPS):
        for which, chosen in enumerate((side, 1 - side)):
            start = (chosen * SPANS + group * (SPANS // OUT_GROUPS) + at) * 2 * SHARD
            source = weight_ref.at[pl.ds(pl.multiple_of(start, 2 * SHARD), 2 * SHARD), :]
            to = wide.at[which, :, at * SHARD : (at + 1) * SHARD]
            copies.append(pltpu.make_async_copy(source, to, arrived.at[at, which]))
    for copy in loads + copies[:8]:
        copy.start()
    for copy in loads:
        copy.wait()
    for at, step in enumerate(Z_ORDER):
        rows = pl.ds(pl.multiple_of(((z + step) % 4) * 64, 64), 64)
        rows_of[0, at * 64 : at * 64 + 64, :] = mine[rows, :]
        rows_of[1, at * 64 : at * 64 + 64, :] = got[rows, :]
    stores = []
    for part in range(OUT_PARTS):
        for copy in copies[part * 4 : part * 4 + 4]:
            copy.wait()
        for copy in copies[part * 4 + 8 : part * 4 + 12]:
            copy.start()
        columns = slice(part * 2 * SHARD, (part + 1) * 2 * SHARD)
        total = jnp.dot(rows_of[0], wide[0, :, columns], preferred_element_type=F32)
        total += jnp.dot(rows_of[1], wide[1, :, columns], preferred_element_type=F32)
        result[part] = total.astype(BF16)
        for index, out in enumerate(outs):
            source = result.at[part, index * 64 : index * 64 + 64, :]
            stores.append(pltpu.make_async_copy(source, out.at[:, columns], stored.at[part, index]))
            stores[-1].start()
    for store in stores:
        store.wait()


def output_partial(group, place, mine, got, weights):
    anywhere = pl.BlockSpec(memory_space=pl.ANY)
    half = TOK // 2
    return pl.pallas_call(
        functools.partial(output_kernel, group),
        in_specs=[pl.BlockSpec(memory_space=pltpu.SMEM)] + [anywhere] * 3,
        out_specs=[anywhere] * 4,
        out_shape=[jax.ShapeDtypeStruct((64, OUT_COLS), BF16)] * 4,
        scratch_shapes=[
            pltpu.VMEM((half, 2 * GCOLS), BF16),
            pltpu.VMEM((half, 2 * GCOLS), BF16),
            pltpu.VMEM((2, half, 2 * GCOLS), BF16),
            pltpu.VMEM((2, 2 * SHARD, OUT_COLS), BF16),
            pltpu.VMEM((OUT_PARTS, half, 2 * SHARD), BF16),
            pltpu.SemaphoreType.DMA((2,)),
            pltpu.SemaphoreType.DMA((SPANS // OUT_GROUPS, 2)),
            pltpu.SemaphoreType.DMA((OUT_PARTS, 4)),
        ],
        compiler_params=pltpu.CompilerParams(vmem_limit_bytes=VMEM_LIMIT),
        cost_estimate=pl.CostEstimate(
            flops=2 * TOK // 2 * OUT_COLS * 4 * GCOLS, bytes_accessed=6 * 2**20, transcendentals=0
        ),
    )(place, mine, got, weights)


def reduce_over_z(far, up, down, stay, sign):
    near, back = (up, down) if sign > 0 else (down, up)
    passed = move(far, dz=sign)
    behind = move(back, dz=-sign)
    near = (near.astype(F32) + passed.astype(F32)).astype(BF16)
    ahead = move(near, dz=sign)
    return (stay.astype(F32) + ahead.astype(F32) + behind.astype(F32)).astype(BF16)


def per_device(hidden, span_ids, w_query, w_keyval, w_out):
    span, uly = lax.axis_index("span"), lax.axis_index("uly")
    xl, y, core = span // 8, (span // 2) % 4, span % 2
    z, xh = uly // 2, uly % 2
    as_int = lambda values: jnp.stack([jnp.asarray(v, jnp.int32) for v in values])

    chips = [x * 4 + (y + dy) % 4 for dy in (0, 3, 1, 2) for x in (xl, 1 - xl)]
    which = as_int([j * 2 + core for j in chips] + chips)
    place = as_int([z, xh])
    block_ids = span_ids.reshape(SPANS, TOK)[:, 0]
    seen = (block_ids <= block_ids[span]).astype(jnp.int32)
    order = [chips[at] * 2 + core for at in (0, 1, 2, 4, 3, 5, 6, 7)]
    seen = seen[as_int(order + [at + 1 - 2 * core for at in order])]
    send_flags = jnp.concatenate([seen, as_int([1 - xh])])
    mine_flags = jnp.concatenate([seen, as_int([xh])])

    own = jnp.concatenate([w_keyval[:, 0], w_keyval[:, 1]], axis=1)
    side = move(own, swap_xl=True)
    up, down = move(own, dy=1), move(own, dy=-1)
    elsewhere = after(as_int([j * 2 + 1 - core for j in range(8)]), own)
    picked = pick_columns(hidden, elsewhere)
    side, up, down, picked, which, place, send_flags, mine_flags = lax.optimization_barrier(
        (side, up, down, picked, which, place, send_flags, mine_flags)
    )
    other_hidden = move(picked, swap_c=True)
    side_up, side_down = move(side, dy=1), move(side, dy=-1)
    query_side = move(after(w_query, side), swap_xl=True)
    up, side_up, side_down, other_hidden, query_own = lax.optimization_barrier(
        (up, side_up, side_down, other_hidden, w_query)
    )
    far, side_far = move(up, dy=1), move(side_down, dy=-1)
    query_up, query_down = move(query_own, dy=1), move(query_own, dy=-1)
    pieces = [own, side, up, side_up, down, side_down, far, side_far]
    pair_own, pair_other = project(hidden, other_hidden, which, pieces)
    pair = (pair_own + move(pair_other, swap_c=True)).astype(BF16)

    pair, query_up, query_down, query_side, out_shard = lax.optimization_barrier(
        (pair, query_up, query_down, query_side, w_out)
    )
    pair_side = move(pair, swap_xl=True)
    pair_up, pair_down = move(pair, dy=1), move(pair, dy=-1)

    planes = [
        [index_of(span // 8, span // 2 % 4, span % 2, at, side) for side in range(2) for span in range(SPANS)]
        for at in range(4)
    ]
    weights = lax.all_gather(out_shard, BOTH, axis=0, tiled=True, axis_index_groups=planes)

    pair_side, pair_up, pair_down, query_side = lax.optimization_barrier((pair_side, pair_up, pair_down, query_side))
    pair_side_up, pair_side_down = move(pair_side, dy=1), move(pair_side, dy=-1)
    query_side_up, query_side_down = move(query_side, dy=1), move(query_side, dy=-1)
    pairs = jnp.concatenate([pair, pair_side, pair_up, pair_down], axis=0)
    other_pairs = move(pairs, swap_c=True)
    pair_down, pair_side_up, pair_side_down = lax.optimization_barrier((pair_down, pair_side_up, pair_side_down))
    pair_far, pair_side_far = move(pair_down, dy=-1), move(pair_side_up, dy=1)
    query_far = move(after(query_up, query_side_up, query_side_down), dy=1)
    query_side_far = move(query_side_down, dy=-1)
    more_pairs = jnp.concatenate([pair_side_up, pair_side_down, pair_far, pair_side_far], axis=0)
    pairs = [pairs, more_pairs, other_pairs, move(more_pairs, swap_c=True)]

    pieces = [
        w_query, query_side, query_up, query_side_up, query_down, query_side_down, query_far, query_side_far
    ]
    query_own, query_other = project(hidden, other_hidden, which, pieces)
    queries = (query_own + move(query_other, swap_c=True)).astype(BF16)

    send = attend(send_flags, queries, pairs)
    got = move(send, swap_xh=True)
    mine = attend(after(mine_flags, send), queries, pairs)

    totals = []
    for group in range(OUT_GROUPS):
        parts = output_partial(group, place, mine, got, weights)
        totals.append(reduce_over_z(*parts, 1 if group % 2 == 0 else -1))
    return jnp.concatenate(totals, axis=1)


def solution(mesh):
    in_specs = (P("span", None), P(), P("span", "uly"), P("span", None, "uly"), P("uly", "span"))
    out_specs = P(("span", "uly"), None)
    return jax.shard_map(
        per_device, mesh=mesh, in_specs=in_specs, out_specs=out_specs, check_vma=False
    )
```

```python
import functools
import math

import jax
import jax.numpy as jnp
from jax import lax
from jax.experimental import pallas as pl
from jax.experimental.pallas import tpu as pltpu
from jax.sharding import PartitionSpec as P

HEADS = 48
HEAD = 128
D = 6144
SPANS = 16
TOK = 512
SHARD = D // SPANS
GROUP = 3
GCOLS = GROUP * HEAD
SCALE2 = math.log2(math.e) / math.sqrt(HEAD)
SAFE_EXPONENT = 90.0
NEG_LARGE = -1e30
VMEM_LIMIT = 60 * 2**20
BOTH = ("span", "uly")
F32 = jnp.float32
BF16 = jnp.bfloat16


def coords(index):
    span, uly = index // 8, index % 8
    return span // 8, (span // 2) % 4, span % 2, uly // 2, uly % 2


def index_of(xl, y, c, z, xh):
    return (xl * 8 + y * 2 + c) * 8 + z * 2 + xh


def move(array, dx=0, dy=0, dz=0, swap_xl=False, swap_xh=False, swap_c=False):
    pairs = []
    for source in range(128):
        xl, y, c, z, xh = coords(source)
        x = (xh * 2 + xl + dx) % 4
        xh, xl = x // 2, x % 2
        if swap_xl:
            xl = 1 - xl
        if swap_xh:
            xh = 1 - xh
        if swap_c:
            c = 1 - c
        pairs.append((source, index_of(xl, (y + dy) % 4, c, (z + dz) % 4, xh)))
    return lax.ppermute(array, BOTH, pairs)


def after(array, *results):
    return lax.optimization_barrier((array, *results))[0]


def pick_kernel(which, hidden_ref, out_ref, arrived):
    copies = []
    for at in range(8):
        columns = pl.ds(pl.multiple_of(which[at] * SHARD, 128), SHARD)
        to = out_ref.at[:, at * SHARD : (at + 1) * SHARD]
        copies.append(pltpu.make_async_copy(hidden_ref.at[:, columns], to, arrived.at[at]))
    for copy in copies:
        copy.start()
    for copy in copies:
        copy.wait()


def pick_columns(hidden, which):
    return pl.pallas_call(
        pick_kernel,
        in_specs=[pl.BlockSpec(memory_space=pltpu.SMEM), pl.BlockSpec(memory_space=pl.ANY)],
        out_specs=pl.BlockSpec(memory_space=pltpu.VMEM),
        out_shape=jax.ShapeDtypeStruct((TOK, 8 * SHARD), BF16),
        scratch_shapes=[pltpu.SemaphoreType.DMA((8,))],
        compiler_params=pltpu.CompilerParams(vmem_limit_bytes=VMEM_LIMIT),
        cost_estimate=pl.CostEstimate(flops=0, bytes_accessed=4 * TOK * 8 * SHARD, transcendentals=0),
    )(which, hidden)


def project_kernel(which, own_ref, other_ref, *refs):
    pieces, (own_out, other_out, own_rows, other_rows, weight, arrived) = refs[:8], refs[8:]
    copies = []
    for at in range(8):
        columns = pl.ds(pl.multiple_of(which[at] * SHARD, 128), SHARD)
        other = pl.ds(pl.multiple_of(which[8 + at] * SHARD, 128), SHARD)
        to = slice(at * SHARD, (at + 1) * SHARD)
        copies.append(
            [
                pltpu.make_async_copy(pieces[at], weight.at[to, :], arrived.at[at, 0]),
                pltpu.make_async_copy(own_ref.at[:, columns], own_rows.at[:, to], arrived.at[at, 1]),
                pltpu.make_async_copy(other_ref.at[:, other], other_rows.at[:, to], arrived.at[at, 2]),
            ]
        )
    for copy in copies:
        for one in copy:
            one.start()
    for at in range(4):
        for copy in copies[2 * at : 2 * at + 2]:
            for one in copy:
                one.wait()
        to = slice(2 * at * SHARD, (2 * at + 2) * SHARD)
        for rows, out in ((own_rows, own_out), (other_rows, other_out)):
            part = jnp.dot(rows[:, to], weight[to, :], preferred_element_type=F32)
            if at == 0:
                out[...] = part
            else:
                out[...] += part


def project(hidden, other, which, pieces):
    cols = pieces[0].shape[1]
    out = jax.ShapeDtypeStruct((TOK, cols), F32)
    return pl.pallas_call(
        project_kernel,
        in_specs=[pl.BlockSpec(memory_space=pltpu.SMEM)] + [pl.BlockSpec(memory_space=pl.ANY)] * 10,
        out_specs=[pl.BlockSpec(memory_space=pltpu.VMEM)] * 2,
        out_shape=[out, out],
        scratch_shapes=[
            pltpu.VMEM((TOK, 8 * SHARD), BF16),
            pltpu.VMEM((TOK, 8 * SHARD), BF16),
            pltpu.VMEM((8 * SHARD, cols), BF16),
            pltpu.SemaphoreType.DMA((8, 3)),
        ],
        compiler_params=pltpu.CompilerParams(vmem_limit_bytes=VMEM_LIMIT),
        cost_estimate=pl.CostEstimate(
            flops=4 * TOK * 8 * SHARD * cols, bytes_accessed=12 * 2**20, transcendentals=0
        ),
    )(which, hidden, other, *pieces)


QUERY_STEP = 768


def query_kernel(hidden_ref, weight_ref, out_ref, total):
    step = pl.program_id(0)
    part = jnp.dot(hidden_ref[...], weight_ref[...], preferred_element_type=F32)

    @pl.when(step == 0)
    def _():
        total[...] = part

    @pl.when(step > 0)
    def _():
        total[...] += part

    @pl.when(step == pl.num_programs(0) - 1)
    def _():
        out_ref[...] = total[...].astype(BF16)


def project_queries(hidden, weight):
    cols = weight.shape[1]
    return pl.pallas_call(
        query_kernel,
        grid=(D // QUERY_STEP,),
        in_specs=[
            pl.BlockSpec((TOK, QUERY_STEP), lambda i: (0, i)),
            pl.BlockSpec((QUERY_STEP, cols), lambda i: (i, 0)),
        ],
        out_specs=pl.BlockSpec((TOK, cols), lambda i: (0, 0)),
        out_shape=jax.ShapeDtypeStruct((TOK, cols), BF16),
        scratch_shapes=[pltpu.VMEM((TOK, cols), F32)],
        compiler_params=pltpu.CompilerParams(vmem_limit_bytes=VMEM_LIMIT),
        cost_estimate=pl.CostEstimate(
            flops=2 * TOK * D * cols, bytes_accessed=16 * 2**20, transcendentals=0
        ),
    )(hidden, weight)


def attend_kernel(
    flags, query_ref, *refs
):
    pair_refs, refs = refs[:4], refs[4:]
    out_ref, query, keys, value, accum, best, largest, ready, arrived = refs
    side = flags[SPANS]
    heads = HEADS // 8
    loads = []
    for at in range(4):
        rows = pl.ds(pl.multiple_of(at * 128 + side * 64, 64), 64)
        to = query.at[at * 64 : at * 64 + 64, :]
        loads.append(pltpu.make_async_copy(query_ref.at[rows, :], to, ready.at[at]))
    pairs = []
    for ref in pair_refs:
        for at in range(SPANS // 4):
            block, rows = len(pairs), slice(at * TOK, (at + 1) * TOK)
            pairs.append(
                (
                    pltpu.make_async_copy(ref.at[rows, :HEAD], keys.at[block], arrived.at[block, 0]),
                    pltpu.make_async_copy(ref.at[rows, HEAD:], value.at[block, :, :HEAD], arrived.at[block, 1]),
                )
            )
    for load in loads:
        load.start()
    for key, mixed in pairs:
        key.start()
        mixed.start()
    value[:, :, HEAD:] = jnp.ones((SPANS, TOK, HEAD), BF16)
    accum[...] = jnp.zeros_like(accum)
    largest[...] = jnp.zeros_like(largest)
    for load in loads:
        load.wait()
    ones = jnp.ones((HEAD, HEAD), BF16)

    def squares(rows):
        sums = jnp.dot(rows * rows, ones, preferred_element_type=F32)
        return jnp.max(sums.reshape(rows.shape[0] // 8, 8, HEAD), axis=0)

    for head in range(heads):
        largest[0] = jnp.maximum(largest[0], squares(query[:, head * HEAD : (head + 1) * HEAD]))

    def step_small(block):
        key, extended = keys[block], value[block]
        largest[1] = jnp.maximum(largest[1], squares(key))
        for head in range(heads):
            scores = lax.dot_general(
                query[:, head * HEAD : (head + 1) * HEAD],
                key,
                (((1,), (1,)), ((), ())),
                preferred_element_type=F32,
            )
            probs = jnp.exp2(scores * SCALE2).astype(BF16)
            accum[head] += jnp.dot(probs, extended, preferred_element_type=F32)

    def step_any(block):
        def one(head, carry):
            scores = lax.dot_general(
                query[:, pl.ds(pl.multiple_of(head * HEAD, HEAD), HEAD)],
                keys[block],
                (((1,), (1,)), ((), ())),
                preferred_element_type=F32,
            )
            old = best[head]
            new = jnp.maximum(old, jnp.max(scores, axis=1, keepdims=True))
            best[head] = new
            probs = jnp.exp2((scores - new[:, :1]) * SCALE2).astype(BF16)
            factor = jnp.exp2((old - new) * SCALE2)
            accum[head] = accum[head] * factor[:, :1] + jnp.dot(
                probs, value[block], preferred_element_type=F32
            )
            return carry

        lax.fori_loop(0, heads, one, 0)

    def step(block, carry):
        for at, to in enumerate((keys.at[block], value.at[block, :, :HEAD])):
            pltpu.make_async_copy(pair_refs[0].at[:TOK, :HEAD], to, arrived.at[block, at]).wait()

        @pl.when(flags[block] > 0)
        def _():
            step_small(block)

        return carry

    lax.fori_loop(0, SPANS, step, 0)
    bound = jnp.max(largest[0]) * jnp.max(largest[1]) * (1.03 * SCALE2 * SCALE2)

    @pl.when(jnp.logical_not(bound <= SAFE_EXPONENT * SAFE_EXPONENT))
    def _():
        accum[...] = jnp.zeros_like(accum)
        best[...] = jnp.full_like(best, NEG_LARGE)

        def again(block, carry):
            @pl.when(flags[block] > 0)
            def _():
                step_any(block)

            return carry

        lax.fori_loop(0, SPANS, again, 0)

    for head in range(heads):
        mixed = accum[head]
        out_ref[:, head * HEAD : (head + 1) * HEAD] = (mixed[:, :HEAD] / mixed[:, HEAD:]).astype(BF16)


def attend(flags, queries, pairs):
    half, heads = TOK // 2, HEADS // 8
    return pl.pallas_call(
        attend_kernel,
        in_specs=[pl.BlockSpec(memory_space=pltpu.SMEM)] + [pl.BlockSpec(memory_space=pl.ANY)] * 5,
        out_specs=pl.BlockSpec(memory_space=pltpu.VMEM),
        out_shape=jax.ShapeDtypeStruct((half, 2 * GCOLS), BF16),
        scratch_shapes=[
            pltpu.VMEM((half, 2 * GCOLS), BF16),
            pltpu.VMEM((SPANS, TOK, HEAD), BF16),
            pltpu.VMEM((SPANS, TOK, 2 * HEAD), BF16),
            pltpu.VMEM((heads, half, 2 * HEAD), F32),
            pltpu.VMEM((heads, half, HEAD), F32),
            pltpu.VMEM((2, 8, HEAD), F32),
            pltpu.SemaphoreType.DMA((4,)),
            pltpu.SemaphoreType.DMA((SPANS, 2)),
        ],
        compiler_params=pltpu.CompilerParams(vmem_limit_bytes=VMEM_LIMIT),
        cost_estimate=pl.CostEstimate(
            flops=heads * 6 * half * SPANS * TOK * HEAD, bytes_accessed=6 * 2**20, transcendentals=0
        ),
    )(flags, queries, *pairs)


OUT_GROUPS = 2
OUT_PARTS = 8 // OUT_GROUPS
OUT_COLS = D // OUT_GROUPS
Z_ORDER = (2, 1, 3, 0)


def output_kernel(group, place, mine_ref, got_ref, weight_ref, *refs):
    outs, (mine, got, rows_of, wide, result, loaded, arrived, stored) = refs[:4], refs[4:]
    z, side = place[0], place[1]
    loads = [
        pltpu.make_async_copy(mine_ref, mine, loaded.at[0]),
        pltpu.make_async_copy(got_ref, got, loaded.at[1]),
    ]
    copies = []
    for at in range(SPANS // OUT_GROUPS):
        for which, chosen in enumerate((side, 1 - side)):
            start = (chosen * SPANS + group * (SPANS // OUT_GROUPS) + at) * 2 * SHARD
            source = weight_ref.at[pl.ds(pl.multiple_of(start, 2 * SHARD), 2 * SHARD), :]
            to = wide.at[which, :, at * SHARD : (at + 1) * SHARD]
            copies.append(pltpu.make_async_copy(source, to, arrived.at[at, which]))
    for copy in loads + copies[:8]:
        copy.start()
    for copy in loads:
        copy.wait()
    for at, step in enumerate(Z_ORDER):
        rows = pl.ds(pl.multiple_of(((z + step) % 4) * 64, 64), 64)
        rows_of[0, at * 64 : at * 64 + 64, :] = mine[rows, :]
        rows_of[1, at * 64 : at * 64 + 64, :] = got[rows, :]
    stores = []
    for part in range(OUT_PARTS):
        for copy in copies[part * 4 : part * 4 + 4]:
            copy.wait()
        for copy in copies[part * 4 + 8 : part * 4 + 12]:
            copy.start()
        columns = slice(part * 2 * SHARD, (part + 1) * 2 * SHARD)
        total = jnp.dot(rows_of[0], wide[0, :, columns], preferred_element_type=F32)
        total += jnp.dot(rows_of[1], wide[1, :, columns], preferred_element_type=F32)
        result[part] = total.astype(BF16)
        for index, out in enumerate(outs):
            source = result.at[part, index * 64 : index * 64 + 64, :]
            stores.append(pltpu.make_async_copy(source, out.at[:, columns], stored.at[part, index]))
            stores[-1].start()
    for store in stores:
        store.wait()


def output_partial(group, place, mine, got, weights):
    anywhere = pl.BlockSpec(memory_space=pl.ANY)
    half = TOK // 2
    return pl.pallas_call(
        functools.partial(output_kernel, group),
        in_specs=[pl.BlockSpec(memory_space=pltpu.SMEM)] + [anywhere] * 3,
        out_specs=[anywhere] * 4,
        out_shape=[jax.ShapeDtypeStruct((64, OUT_COLS), BF16)] * 4,
        scratch_shapes=[
            pltpu.VMEM((half, 2 * GCOLS), BF16),
            pltpu.VMEM((half, 2 * GCOLS), BF16),
            pltpu.VMEM((2, half, 2 * GCOLS), BF16),
            pltpu.VMEM((2, 2 * SHARD, OUT_COLS), BF16),
            pltpu.VMEM((OUT_PARTS, half, 2 * SHARD), BF16),
            pltpu.SemaphoreType.DMA((2,)),
            pltpu.SemaphoreType.DMA((SPANS // OUT_GROUPS, 2)),
            pltpu.SemaphoreType.DMA((OUT_PARTS, 4)),
        ],
        compiler_params=pltpu.CompilerParams(vmem_limit_bytes=VMEM_LIMIT),
        cost_estimate=pl.CostEstimate(
            flops=2 * TOK // 2 * OUT_COLS * 4 * GCOLS, bytes_accessed=6 * 2**20, transcendentals=0
        ),
    )(place, mine, got, weights)


def reduce_over_z(far, up, down, stay, sign):
    near, back = (up, down) if sign > 0 else (down, up)
    passed = move(far, dz=sign)
    behind = move(back, dz=-sign)
    near = (near.astype(F32) + passed.astype(F32)).astype(BF16)
    ahead = move(near, dz=sign)
    return (stay.astype(F32) + ahead.astype(F32) + behind.astype(F32)).astype(BF16)


def per_device(hidden, span_ids, w_query, w_keyval, w_out):
    span, uly = lax.axis_index("span"), lax.axis_index("uly")
    xl, y, core = span // 8, (span // 2) % 4, span % 2
    z, xh = uly // 2, uly % 2
    as_int = lambda values: jnp.stack([jnp.asarray(v, jnp.int32) for v in values])

    chips = [x * 4 + (y + dy) % 4 for dy in (0, 3, 1, 2) for x in (xl, 1 - xl)]
    which = as_int([j * 2 + core for j in chips] + chips)
    place = as_int([z, xh])
    block_ids = span_ids.reshape(SPANS, TOK)[:, 0]
    seen = (block_ids <= block_ids[span]).astype(jnp.int32)
    order = [chips[at] * 2 + core for at in (0, 1, 2, 4, 3, 5, 6, 7)]
    seen = seen[as_int(order + [at + 1 - 2 * core for at in order])]
    send_flags = jnp.concatenate([seen, as_int([1 - xh])])
    mine_flags = jnp.concatenate([seen, as_int([xh])])

    query_weight = lax.all_gather(w_query, "span", axis=0, tiled=True)

    own = jnp.concatenate([w_keyval[:, 0], w_keyval[:, 1]], axis=1)
    side = move(own, swap_xl=True)
    up, down = move(own, dy=1), move(own, dy=-1)
    elsewhere = after(as_int([j * 2 + 1 - core for j in range(8)]), own)
    picked = pick_columns(hidden, elsewhere)
    side, up, down, picked, which, place, send_flags, mine_flags = lax.optimization_barrier(
        (side, up, down, picked, which, place, send_flags, mine_flags)
    )
    other_hidden = move(picked, swap_c=True)
    side_up, side_down = move(side, dy=1), move(side, dy=-1)
    up, side_up, side_down, other_hidden = lax.optimization_barrier((up, side_up, side_down, other_hidden))
    far, side_far = move(up, dy=1), move(side_down, dy=-1)

    planes = [
        [index_of(span // 8, span // 2 % 4, span % 2, at, side) for side in range(2) for span in range(SPANS)]
        for at in range(4)
    ]
    weights = lax.all_gather(
        after(w_out, far, side_far), BOTH, axis=0, tiled=True, axis_index_groups=planes
    )
    pieces = [own, side, up, side_up, down, side_down, far, side_far]
    pair_own, pair_other = project(hidden, other_hidden, which, pieces)
    pair = (pair_own + move(pair_other, swap_c=True)).astype(BF16)

    pair_side = move(pair, swap_xl=True)
    pair_up, pair_down = move(pair, dy=1), move(pair, dy=-1)
    pair_side, pair_up, pair_down = lax.optimization_barrier((pair_side, pair_up, pair_down))
    pair_side_up, pair_side_down = move(pair_side, dy=1), move(pair_side, dy=-1)
    pairs = jnp.concatenate([pair, pair_side, pair_up, pair_down], axis=0)
    other_pairs = move(pairs, swap_c=True)
    pair_down, pair_side_up, pair_side_down = lax.optimization_barrier((pair_down, pair_side_up, pair_side_down))
    pair_far, pair_side_far = move(pair_down, dy=-1), move(pair_side_up, dy=1)
    more_pairs = jnp.concatenate([pair_side_up, pair_side_down, pair_far, pair_side_far], axis=0)
    pairs = [pairs, more_pairs, other_pairs, move(more_pairs, swap_c=True)]

    queries = project_queries(hidden, query_weight)
    send = attend(send_flags, queries, pairs)
    got = move(send, swap_xh=True)
    mine = attend(after(mine_flags, send), queries, pairs)

    totals = []
    for group in range(OUT_GROUPS):
        parts = output_partial(group, place, mine, got, weights)
        totals.append(reduce_over_z(*parts, 1 if group % 2 == 0 else -1))
    return jnp.concatenate(totals, axis=1)


def solution(mesh):
    in_specs = (P("span", None), P(), P("span", "uly"), P("span", None, "uly"), P("uly", "span"))
    out_specs = P(("span", "uly"), None)
    return jax.shard_map(
        per_device, mesh=mesh, in_specs=in_specs, out_specs=out_specs, check_vma=False
    )
```

```python
import functools
import math

import jax
import jax.numpy as jnp
from jax import lax
from jax.experimental import pallas as pl
from jax.experimental.pallas import tpu as pltpu
from jax.sharding import PartitionSpec as P

HEADS = 48
HEAD = 128
D = 6144
SPANS = 16
TOK = 512
SHARD = D // SPANS
GROUP = 3
GCOLS = GROUP * HEAD
SCALE2 = math.log2(math.e) / math.sqrt(HEAD)
SAFE_EXPONENT = 90.0
NEG_LARGE = -1e30
VMEM_LIMIT = 60 * 2**20
BOTH = ("span", "uly")
F32 = jnp.float32
BF16 = jnp.bfloat16


def coords(index):
    span, uly = index // 8, index % 8
    return span // 8, (span // 2) % 4, span % 2, uly // 2, uly % 2


def index_of(xl, y, c, z, xh):
    return (xl * 8 + y * 2 + c) * 8 + z * 2 + xh


def move(array, dx=0, dy=0, dz=0, swap_xl=False, swap_xh=False, swap_c=False):
    pairs = []
    for source in range(128):
        xl, y, c, z, xh = coords(source)
        x = (xh * 2 + xl + dx) % 4
        xh, xl = x // 2, x % 2
        if swap_xl:
            xl = 1 - xl
        if swap_xh:
            xh = 1 - xh
        if swap_c:
            c = 1 - c
        pairs.append((source, index_of(xl, (y + dy) % 4, c, (z + dz) % 4, xh)))
    return lax.ppermute(array, BOTH, pairs)


def after(array, *results):
    return lax.optimization_barrier((array, *results))[0]


def pick_kernel(which, hidden_ref, out_ref, arrived):
    copies = []
    for at in range(8):
        columns = pl.ds(pl.multiple_of(which[at] * SHARD, 128), SHARD)
        to = out_ref.at[:, at * SHARD : (at + 1) * SHARD]
        copies.append(pltpu.make_async_copy(hidden_ref.at[:, columns], to, arrived.at[at]))
    for copy in copies:
        copy.start()
    for copy in copies:
        copy.wait()


def pick_columns(hidden, which):
    return pl.pallas_call(
        pick_kernel,
        in_specs=[pl.BlockSpec(memory_space=pltpu.SMEM), pl.BlockSpec(memory_space=pl.ANY)],
        out_specs=pl.BlockSpec(memory_space=pltpu.VMEM),
        out_shape=jax.ShapeDtypeStruct((TOK, 8 * SHARD), BF16),
        scratch_shapes=[pltpu.SemaphoreType.DMA((8,))],
        compiler_params=pltpu.CompilerParams(vmem_limit_bytes=VMEM_LIMIT),
        cost_estimate=pl.CostEstimate(flops=0, bytes_accessed=4 * TOK * 8 * SHARD, transcendentals=0),
    )(which, hidden)


def project_kernel(which, own_ref, other_ref, *refs):
    pieces, (own_out, other_out, own_rows, other_rows, weight, arrived) = refs[:8], refs[8:]
    copies = []
    for at in range(8):
        columns = pl.ds(pl.multiple_of(which[at] * SHARD, 128), SHARD)
        other = pl.ds(pl.multiple_of(which[8 + at] * SHARD, 128), SHARD)
        to = slice(at * SHARD, (at + 1) * SHARD)
        copies.append(
            [
                pltpu.make_async_copy(pieces[at], weight.at[to, :], arrived.at[at, 0]),
                pltpu.make_async_copy(own_ref.at[:, columns], own_rows.at[:, to], arrived.at[at, 1]),
                pltpu.make_async_copy(other_ref.at[:, other], other_rows.at[:, to], arrived.at[at, 2]),
            ]
        )
    for copy in copies:
        for one in copy:
            one.start()
    for at in range(4):
        for copy in copies[2 * at : 2 * at + 2]:
            for one in copy:
                one.wait()
        to = slice(2 * at * SHARD, (2 * at + 2) * SHARD)
        for rows, out in ((own_rows, own_out), (other_rows, other_out)):
            part = jnp.dot(rows[:, to], weight[to, :], preferred_element_type=F32)
            if at == 0:
                out[...] = part
            else:
                out[...] += part


def project(hidden, other, which, pieces):
    cols = pieces[0].shape[1]
    out = jax.ShapeDtypeStruct((TOK, cols), F32)
    return pl.pallas_call(
        project_kernel,
        in_specs=[pl.BlockSpec(memory_space=pltpu.SMEM)] + [pl.BlockSpec(memory_space=pl.ANY)] * 10,
        out_specs=[pl.BlockSpec(memory_space=pltpu.VMEM)] * 2,
        out_shape=[out, out],
        scratch_shapes=[
            pltpu.VMEM((TOK, 8 * SHARD), BF16),
            pltpu.VMEM((TOK, 8 * SHARD), BF16),
            pltpu.VMEM((8 * SHARD, cols), BF16),
            pltpu.SemaphoreType.DMA((8, 3)),
        ],
        compiler_params=pltpu.CompilerParams(vmem_limit_bytes=VMEM_LIMIT),
        cost_estimate=pl.CostEstimate(
            flops=4 * TOK * 8 * SHARD * cols, bytes_accessed=12 * 2**20, transcendentals=0
        ),
    )(which, hidden, other, *pieces)


QUERY_STEP = 768


def query_kernel(hidden_ref, weight_ref, out_ref, total):
    step = pl.program_id(0)
    part = jnp.dot(hidden_ref[...], weight_ref[...], preferred_element_type=F32)

    @pl.when(step == 0)
    def _():
        total[...] = part

    @pl.when(step > 0)
    def _():
        total[...] += part

    @pl.when(step == pl.num_programs(0) - 1)
    def _():
        out_ref[...] = total[...].astype(BF16)


def project_queries(hidden, weight):
    cols = weight.shape[1]
    return pl.pallas_call(
        query_kernel,
        grid=(D // QUERY_STEP,),
        in_specs=[
            pl.BlockSpec((TOK, QUERY_STEP), lambda i: (0, i)),
            pl.BlockSpec((QUERY_STEP, cols), lambda i: (i, 0)),
        ],
        out_specs=pl.BlockSpec((TOK, cols), lambda i: (0, 0)),
        out_shape=jax.ShapeDtypeStruct((TOK, cols), BF16),
        scratch_shapes=[pltpu.VMEM((TOK, cols), F32)],
        compiler_params=pltpu.CompilerParams(vmem_limit_bytes=VMEM_LIMIT),
        cost_estimate=pl.CostEstimate(
            flops=2 * TOK * D * cols, bytes_accessed=16 * 2**20, transcendentals=0
        ),
    )(hidden, weight)


def attend_kernel(
    flags, query_ref, *refs
):
    pair_refs, refs = refs[:4], refs[4:]
    out_ref, query, keys, value, accum, best, largest, ready, arrived = refs
    side = flags[SPANS]
    heads = HEADS // 8
    loads = []
    for at in range(4):
        rows = pl.ds(pl.multiple_of(at * 128 + side * 64, 64), 64)
        to = query.at[at * 64 : at * 64 + 64, :]
        loads.append(pltpu.make_async_copy(query_ref.at[rows, :], to, ready.at[at]))
    pairs = []
    for ref in pair_refs:
        for at in range(SPANS // 4):
            block, rows = len(pairs), slice(at * TOK, (at + 1) * TOK)
            pairs.append(
                (
                    pltpu.make_async_copy(ref.at[rows, :HEAD], keys.at[block], arrived.at[block, 0]),
                    pltpu.make_async_copy(ref.at[rows, HEAD:], value.at[block, :, :HEAD], arrived.at[block, 1]),
                )
            )
    for load in loads:
        load.start()
    for key, mixed in pairs:
        key.start()
        mixed.start()
    value[:, :, HEAD:] = jnp.ones((SPANS, TOK, HEAD), BF16)
    accum[...] = jnp.zeros_like(accum)
    largest[...] = jnp.zeros_like(largest)
    for load in loads:
        load.wait()
    ones = jnp.ones((HEAD, HEAD), BF16)

    def squares(rows):
        sums = jnp.dot(rows * rows, ones, preferred_element_type=F32)
        return jnp.max(sums.reshape(rows.shape[0] // 8, 8, HEAD), axis=0)

    for head in range(heads):
        largest[0] = jnp.maximum(largest[0], squares(query[:, head * HEAD : (head + 1) * HEAD]))

    def step_small(block):
        key, extended = keys[block], value[block]
        largest[1] = jnp.maximum(largest[1], squares(key))
        for head in range(heads):
            scores = lax.dot_general(
                query[:, head * HEAD : (head + 1) * HEAD],
                key,
                (((1,), (1,)), ((), ())),
                preferred_element_type=F32,
            )
            probs = jnp.exp2(scores * SCALE2).astype(BF16)
            accum[head] += jnp.dot(probs, extended, preferred_element_type=F32)

    def step_any(block):
        def one(head, carry):
            scores = lax.dot_general(
                query[:, pl.ds(pl.multiple_of(head * HEAD, HEAD), HEAD)],
                keys[block],
                (((1,), (1,)), ((), ())),
                preferred_element_type=F32,
            )
            old = best[head]
            new = jnp.maximum(old, jnp.max(scores, axis=1, keepdims=True))
            best[head] = new
            probs = jnp.exp2((scores - new[:, :1]) * SCALE2).astype(BF16)
            factor = jnp.exp2((old - new) * SCALE2)
            accum[head] = accum[head] * factor[:, :1] + jnp.dot(
                probs, value[block], preferred_element_type=F32
            )
            return carry

        lax.fori_loop(0, heads, one, 0)

    def step(block, carry):
        for at, to in enumerate((keys.at[block], value.at[block, :, :HEAD])):
            pltpu.make_async_copy(pair_refs[0].at[:TOK, :HEAD], to, arrived.at[block, at]).wait()

        @pl.when(flags[block] > 0)
        def _():
            step_small(block)

        return carry

    lax.fori_loop(0, SPANS, step, 0)
    bound = jnp.max(largest[0]) * jnp.max(largest[1]) * (1.03 * SCALE2 * SCALE2)

    @pl.when(jnp.logical_not(bound <= SAFE_EXPONENT * SAFE_EXPONENT))
    def _():
        accum[...] = jnp.zeros_like(accum)
        best[...] = jnp.full_like(best, NEG_LARGE)

        def again(block, carry):
            @pl.when(flags[block] > 0)
            def _():
                step_any(block)

            return carry

        lax.fori_loop(0, SPANS, again, 0)

    for head in range(heads):
        mixed = accum[head]
        out_ref[:, head * HEAD : (head + 1) * HEAD] = (mixed[:, :HEAD] / mixed[:, HEAD:]).astype(BF16)


def attend(flags, queries, pairs):
    half, heads = TOK // 2, HEADS // 8
    return pl.pallas_call(
        attend_kernel,
        in_specs=[pl.BlockSpec(memory_space=pltpu.SMEM)] + [pl.BlockSpec(memory_space=pl.ANY)] * 5,
        out_specs=pl.BlockSpec(memory_space=pltpu.VMEM),
        out_shape=jax.ShapeDtypeStruct((half, 2 * GCOLS), BF16),
        scratch_shapes=[
            pltpu.VMEM((half, 2 * GCOLS), BF16),
            pltpu.VMEM((SPANS, TOK, HEAD), BF16),
            pltpu.VMEM((SPANS, TOK, 2 * HEAD), BF16),
            pltpu.VMEM((heads, half, 2 * HEAD), F32),
            pltpu.VMEM((heads, half, HEAD), F32),
            pltpu.VMEM((2, 8, HEAD), F32),
            pltpu.SemaphoreType.DMA((4,)),
            pltpu.SemaphoreType.DMA((SPANS, 2)),
        ],
        compiler_params=pltpu.CompilerParams(vmem_limit_bytes=VMEM_LIMIT),
        cost_estimate=pl.CostEstimate(
            flops=heads * 6 * half * SPANS * TOK * HEAD, bytes_accessed=6 * 2**20, transcendentals=0
        ),
    )(flags, queries, *pairs)


OUT_GROUPS = 2
OUT_PARTS = 8 // OUT_GROUPS
OUT_COLS = D // OUT_GROUPS
Z_ORDER = (2, 1, 3, 0)


def output_kernel(group, place, mine_ref, got_ref, weight_ref, *refs):
    outs, (mine, got, rows_of, wide, result, loaded, arrived, stored) = refs[:4], refs[4:]
    z, side = place[0], place[1]
    loads = [
        pltpu.make_async_copy(mine_ref, mine, loaded.at[0]),
        pltpu.make_async_copy(got_ref, got, loaded.at[1]),
    ]
    copies = []
    for at in range(SPANS // OUT_GROUPS):
        for which, chosen in enumerate((side, 1 - side)):
            start = (chosen * SPANS + group * (SPANS // OUT_GROUPS) + at) * 2 * SHARD
            source = weight_ref.at[pl.ds(pl.multiple_of(start, 2 * SHARD), 2 * SHARD), :]
            to = wide.at[which, :, at * SHARD : (at + 1) * SHARD]
            copies.append(pltpu.make_async_copy(source, to, arrived.at[at, which]))
    for copy in loads + copies[:8]:
        copy.start()
    for copy in loads:
        copy.wait()
    for at, step in enumerate(Z_ORDER):
        rows = pl.ds(pl.multiple_of(((z + step) % 4) * 64, 64), 64)
        rows_of[0, at * 64 : at * 64 + 64, :] = mine[rows, :]
        rows_of[1, at * 64 : at * 64 + 64, :] = got[rows, :]
    stores = []
    for part in range(OUT_PARTS):
        for copy in copies[part * 4 : part * 4 + 4]:
            copy.wait()
        for copy in copies[part * 4 + 8 : part * 4 + 12]:
            copy.start()
        columns = slice(part * 2 * SHARD, (part + 1) * 2 * SHARD)
        total = jnp.dot(rows_of[0], wide[0, :, columns], preferred_element_type=F32)
        total += jnp.dot(rows_of[1], wide[1, :, columns], preferred_element_type=F32)
        result[part] = total.astype(BF16)
        for index, out in enumerate(outs):
            source = result.at[part, index * 64 : index * 64 + 64, :]
            stores.append(pltpu.make_async_copy(source, out.at[:, columns], stored.at[part, index]))
            stores[-1].start()
    for store in stores:
        store.wait()


def output_partial(group, place, mine, got, weights):
    anywhere = pl.BlockSpec(memory_space=pl.ANY)
    half = TOK // 2
    return pl.pallas_call(
        functools.partial(output_kernel, group),
        in_specs=[pl.BlockSpec(memory_space=pltpu.SMEM)] + [anywhere] * 3,
        out_specs=[anywhere] * 4,
        out_shape=[jax.ShapeDtypeStruct((64, OUT_COLS), BF16)] * 4,
        scratch_shapes=[
            pltpu.VMEM((half, 2 * GCOLS), BF16),
            pltpu.VMEM((half, 2 * GCOLS), BF16),
            pltpu.VMEM((2, half, 2 * GCOLS), BF16),
            pltpu.VMEM((2, 2 * SHARD, OUT_COLS), BF16),
            pltpu.VMEM((OUT_PARTS, half, 2 * SHARD), BF16),
            pltpu.SemaphoreType.DMA((2,)),
            pltpu.SemaphoreType.DMA((SPANS // OUT_GROUPS, 2)),
            pltpu.SemaphoreType.DMA((OUT_PARTS, 4)),
        ],
        compiler_params=pltpu.CompilerParams(vmem_limit_bytes=VMEM_LIMIT),
        cost_estimate=pl.CostEstimate(
            flops=2 * TOK // 2 * OUT_COLS * 4 * GCOLS, bytes_accessed=6 * 2**20, transcendentals=0
        ),
    )(place, mine, got, weights)


def reduce_over_z(far, up, down, stay, sign):
    near, back = (up, down) if sign > 0 else (down, up)
    passed = move(far, dz=sign)
    behind = move(back, dz=-sign)
    near = (near.astype(F32) + passed.astype(F32)).astype(BF16)
    ahead = move(near, dz=sign)
    return (stay.astype(F32) + ahead.astype(F32) + behind.astype(F32)).astype(BF16)


def per_device(hidden, span_ids, w_query, w_keyval, w_out):
    span, uly = lax.axis_index("span"), lax.axis_index("uly")
    xl, y, core = span // 8, (span // 2) % 4, span % 2
    z, xh = uly // 2, uly % 2
    as_int = lambda values: jnp.stack([jnp.asarray(v, jnp.int32) for v in values])

    chips = [x * 4 + (y + dy) % 4 for dy in (0, 3, 1, 2) for x in (xl, 1 - xl)]
    which = as_int([j * 2 + core for j in chips] + chips)
    place = as_int([z, xh])
    block_ids = span_ids.reshape(SPANS, TOK)[:, 0]
    seen = (block_ids <= block_ids[span]).astype(jnp.int32)
    order = [chips[at] * 2 + core for at in (0, 1, 2, 4, 3, 5, 6, 7)]
    seen = seen[as_int(order + [at + 1 - 2 * core for at in order])]
    send_flags = jnp.concatenate([seen, as_int([1 - xh])])
    mine_flags = jnp.concatenate([seen, as_int([xh])])

    query_weight = lax.all_gather(w_query, "span", axis=0, tiled=True)

    own = jnp.concatenate([w_keyval[:, 0], w_keyval[:, 1]], axis=1)
    side = move(own, swap_xl=True)
    up, down = move(own, dy=1), move(own, dy=-1)
    elsewhere = after(as_int([j * 2 + 1 - core for j in range(8)]), own)
    picked = pick_columns(hidden, elsewhere)
    side, up, down, picked, which, place, send_flags, mine_flags = lax.optimization_barrier(
        (side, up, down, picked, which, place, send_flags, mine_flags)
    )
    other_hidden = move(picked, swap_c=True)
    side_up, side_down, far = move(up, swap_xl=True), move(down, swap_xl=True), move(up, dy=1)
    side_up, side_down, far, other_hidden = lax.optimization_barrier((side_up, side_down, far, other_hidden))
    side_far = move(far, swap_xl=True)

    planes = [
        [index_of(span // 8, span // 2 % 4, span % 2, at, side) for side in range(2) for span in range(SPANS)]
        for at in range(4)
    ]
    weights = lax.all_gather(
        after(w_out, far, side_far), BOTH, axis=0, tiled=True, axis_index_groups=planes
    )
    pieces = [own, side, up, side_up, down, side_down, far, side_far]
    pair_own, pair_other = project(hidden, other_hidden, which, pieces)
    pair = (pair_own + move(pair_other, swap_c=True)).astype(BF16)

    pair_side = move(pair, swap_xl=True)
    pair_up, pair_down = move(pair, dy=1), move(pair, dy=-1)
    pair_side, pair_up, pair_down = lax.optimization_barrier((pair_side, pair_up, pair_down))
    pair_side_up, pair_side_down = move(pair_up, swap_xl=True), move(pair_down, swap_xl=True)
    pair_far = move(pair_down, dy=-1)
    pairs = jnp.concatenate([pair, pair_side, pair_up, pair_down], axis=0)
    other_pairs = move(pairs, swap_c=True)
    pair_far, pair_side_up, pair_side_down = lax.optimization_barrier((pair_far, pair_side_up, pair_side_down))
    queries = project_queries(hidden, after(query_weight, pair_side_up))
    pair_side_far, queries = lax.optimization_barrier((move(pair_far, swap_xl=True), queries))
    more_pairs = jnp.concatenate([pair_side_up, pair_side_down, pair_far, pair_side_far], axis=0)
    pairs = [pairs, more_pairs, other_pairs, move(more_pairs, swap_c=True)]

    send = attend(send_flags, queries, pairs)
    got = move(send, swap_xh=True)
    mine = attend(after(mine_flags, send), queries, pairs)

    totals = []
    for group in range(OUT_GROUPS):
        parts = output_partial(group, place, mine, got, weights)
        totals.append(reduce_over_z(*parts, 1 if group % 2 == 0 else -1))
    return jnp.concatenate(totals, axis=1)


def solution(mesh):
    in_specs = (P("span", None), P(), P("span", "uly"), P("span", None, "uly"), P("uly", "span"))
    out_specs = P(("span", "uly"), None)
    return jax.shard_map(
        per_device, mesh=mesh, in_specs=in_specs, out_specs=out_specs, check_vma=False
    )
```

```python
import functools
import math

import jax
import jax.numpy as jnp
from jax import lax
from jax.experimental import pallas as pl
from jax.experimental.pallas import tpu as pltpu
from jax.sharding import PartitionSpec as P

HEADS = 48
HEAD = 128
D = 6144
SPANS = 16
TOK = 512
SHARD = D // SPANS
GROUP = 3
GCOLS = GROUP * HEAD
SCALE2 = math.log2(math.e) / math.sqrt(HEAD)
SAFE_EXPONENT = 90.0
NEG_LARGE = -1e30
VMEM_LIMIT = 60 * 2**20
BOTH = ("span", "uly")
F32 = jnp.float32
BF16 = jnp.bfloat16


def coords(index):
    span, uly = index // 8, index % 8
    return span // 8, (span // 2) % 4, span % 2, uly // 2, uly % 2


def index_of(xl, y, c, z, xh):
    return (xl * 8 + y * 2 + c) * 8 + z * 2 + xh


def move(array, dx=0, dy=0, dz=0, swap_xl=False, swap_xh=False, swap_c=False):
    pairs = []
    for source in range(128):
        xl, y, c, z, xh = coords(source)
        x = (xh * 2 + xl + dx) % 4
        xh, xl = x // 2, x % 2
        if swap_xl:
            xl = 1 - xl
        if swap_xh:
            xh = 1 - xh
        if swap_c:
            c = 1 - c
        pairs.append((source, index_of(xl, (y + dy) % 4, c, (z + dz) % 4, xh)))
    return lax.ppermute(array, BOTH, pairs)


def after(array, *results):
    return lax.optimization_barrier((array, *results))[0]


def pick_kernel(which, hidden_ref, out_ref, arrived):
    copies = []
    for at in range(8):
        columns = pl.ds(pl.multiple_of(which[at] * SHARD, 128), SHARD)
        to = out_ref.at[:, at * SHARD : (at + 1) * SHARD]
        copies.append(pltpu.make_async_copy(hidden_ref.at[:, columns], to, arrived.at[at]))
    for copy in copies:
        copy.start()
    for copy in copies:
        copy.wait()


def pick_columns(hidden, which):
    return pl.pallas_call(
        pick_kernel,
        in_specs=[pl.BlockSpec(memory_space=pltpu.SMEM), pl.BlockSpec(memory_space=pl.ANY)],
        out_specs=pl.BlockSpec(memory_space=pltpu.VMEM),
        out_shape=jax.ShapeDtypeStruct((TOK, 8 * SHARD), BF16),
        scratch_shapes=[pltpu.SemaphoreType.DMA((8,))],
        compiler_params=pltpu.CompilerParams(vmem_limit_bytes=VMEM_LIMIT),
        cost_estimate=pl.CostEstimate(flops=0, bytes_accessed=4 * TOK * 8 * SHARD, transcendentals=0),
    )(which, hidden)


def project_kernel(first, which, own_ref, other_ref, *refs):
    pieces, (own_out, other_out, own_rows, other_rows, weight, arrived) = refs[:8], refs[8:]
    copies = []
    for at in range(8):
        columns = pl.ds(pl.multiple_of(which[at] * SHARD, 128), SHARD)
        other = pl.ds(pl.multiple_of(which[8 + at] * SHARD, 128), SHARD)
        to = slice(at * SHARD, (at + 1) * SHARD)
        copies.append(
            [
                pltpu.make_async_copy(
                    pieces[at].at[:, first : first + weight.shape[1]], weight.at[to, :], arrived.at[at, 0]
                ),
                pltpu.make_async_copy(own_ref.at[:, columns], own_rows.at[:, to], arrived.at[at, 1]),
                pltpu.make_async_copy(other_ref.at[:, other], other_rows.at[:, to], arrived.at[at, 2]),
            ]
        )
    for copy in copies:
        for one in copy:
            one.start()
    for at in range(4):
        for copy in copies[2 * at : 2 * at + 2]:
            for one in copy:
                one.wait()
        to = slice(2 * at * SHARD, (2 * at + 2) * SHARD)
        for rows, out in ((own_rows, own_out), (other_rows, other_out)):
            part = jnp.dot(rows[:, to], weight[to, :], preferred_element_type=F32)
            if at == 0:
                out[...] = part
            else:
                out[...] += part


def project(hidden, other, which, pieces, first, cols):
    out = jax.ShapeDtypeStruct((TOK, cols), F32)
    return pl.pallas_call(
        functools.partial(project_kernel, first),
        in_specs=[pl.BlockSpec(memory_space=pltpu.SMEM)] + [pl.BlockSpec(memory_space=pl.ANY)] * 10,
        out_specs=[pl.BlockSpec(memory_space=pltpu.VMEM)] * 2,
        out_shape=[out, out],
        scratch_shapes=[
            pltpu.VMEM((TOK, 8 * SHARD), BF16),
            pltpu.VMEM((TOK, 8 * SHARD), BF16),
            pltpu.VMEM((8 * SHARD, cols), BF16),
            pltpu.SemaphoreType.DMA((8, 3)),
        ],
        compiler_params=pltpu.CompilerParams(vmem_limit_bytes=VMEM_LIMIT),
        cost_estimate=pl.CostEstimate(
            flops=4 * TOK * 8 * SHARD * cols, bytes_accessed=12 * 2**20, transcendentals=0
        ),
    )(which, hidden, other, *pieces)


def attend_kernel(
    flags, query_ref, *refs
):
    pair_refs, refs = refs[:4], refs[4:]
    out_ref, query, keys, value, accum, best, largest, ready, arrived = refs
    side = flags[SPANS]
    heads = HEADS // 8
    loads = []
    for at in range(4):
        rows = pl.ds(pl.multiple_of(at * 128 + side * 64, 64), 64)
        to = query.at[at * 64 : at * 64 + 64, :]
        loads.append(pltpu.make_async_copy(query_ref.at[rows, :], to, ready.at[at]))
    pairs = []
    for ref in pair_refs:
        for at in range(SPANS // 4):
            block, rows = len(pairs), slice(at * TOK, (at + 1) * TOK)
            pairs.append(
                (
                    pltpu.make_async_copy(ref.at[rows, :HEAD], keys.at[block], arrived.at[block, 0]),
                    pltpu.make_async_copy(ref.at[rows, HEAD:], value.at[block, :, :HEAD], arrived.at[block, 1]),
                )
            )
    for load in loads:
        load.start()
    for key, mixed in pairs:
        key.start()
        mixed.start()
    value[:, :, HEAD:] = jnp.ones((SPANS, TOK, HEAD), BF16)
    accum[...] = jnp.zeros_like(accum)
    largest[...] = jnp.zeros_like(largest)
    for load in loads:
        load.wait()
    ones = jnp.ones((HEAD, HEAD), BF16)

    def squares(rows):
        sums = jnp.dot(rows * rows, ones, preferred_element_type=F32)
        return jnp.max(sums.reshape(rows.shape[0] // 8, 8, HEAD), axis=0)

    for head in range(heads):
        largest[0] = jnp.maximum(largest[0], squares(query[:, head * HEAD : (head + 1) * HEAD]))

    def step_small(block):
        key, extended = keys[block], value[block]
        largest[1] = jnp.maximum(largest[1], squares(key))
        for head in range(heads):
            scores = lax.dot_general(
                query[:, head * HEAD : (head + 1) * HEAD],
                key,
                (((1,), (1,)), ((), ())),
                preferred_element_type=F32,
            )
            probs = jnp.exp2(scores * SCALE2).astype(BF16)
            accum[head] += jnp.dot(probs, extended, preferred_element_type=F32)

    def step_any(block):
        def one(head, carry):
            scores = lax.dot_general(
                query[:, pl.ds(pl.multiple_of(head * HEAD, HEAD), HEAD)],
                keys[block],
                (((1,), (1,)), ((), ())),
                preferred_element_type=F32,
            )
            old = best[head]
            new = jnp.maximum(old, jnp.max(scores, axis=1, keepdims=True))
            best[head] = new
            probs = jnp.exp2((scores - new[:, :1]) * SCALE2).astype(BF16)
            factor = jnp.exp2((old - new) * SCALE2)
            accum[head] = accum[head] * factor[:, :1] + jnp.dot(
                probs, value[block], preferred_element_type=F32
            )
            return carry

        lax.fori_loop(0, heads, one, 0)

    def step(block, carry):
        for at, to in enumerate((keys.at[block], value.at[block, :, :HEAD])):
            pltpu.make_async_copy(pair_refs[0].at[:TOK, :HEAD], to, arrived.at[block, at]).wait()

        @pl.when(flags[block] > 0)
        def _():
            step_small(block)

        return carry

    lax.fori_loop(0, SPANS, step, 0)
    bound = jnp.max(largest[0]) * jnp.max(largest[1]) * (1.03 * SCALE2 * SCALE2)

    @pl.when(jnp.logical_not(bound <= SAFE_EXPONENT * SAFE_EXPONENT))
    def _():
        accum[...] = jnp.zeros_like(accum)
        best[...] = jnp.full_like(best, NEG_LARGE)

        def again(block, carry):
            @pl.when(flags[block] > 0)
            def _():
                step_any(block)

            return carry

        lax.fori_loop(0, SPANS, again, 0)

    for head in range(heads):
        mixed = accum[head]
        out_ref[:, head * HEAD : (head + 1) * HEAD] = (mixed[:, :HEAD] / mixed[:, HEAD:]).astype(BF16)


def attend(flags, queries, pairs):
    half, heads = TOK // 2, HEADS // 8
    return pl.pallas_call(
        attend_kernel,
        in_specs=[pl.BlockSpec(memory_space=pltpu.SMEM)] + [pl.BlockSpec(memory_space=pl.ANY)] * 5,
        out_specs=pl.BlockSpec(memory_space=pltpu.VMEM),
        out_shape=jax.ShapeDtypeStruct((half, 2 * GCOLS), BF16),
        scratch_shapes=[
            pltpu.VMEM((half, 2 * GCOLS), BF16),
            pltpu.VMEM((SPANS, TOK, HEAD), BF16),
            pltpu.VMEM((SPANS, TOK, 2 * HEAD), BF16),
            pltpu.VMEM((heads, half, 2 * HEAD), F32),
            pltpu.VMEM((heads, half, HEAD), F32),
            pltpu.VMEM((2, 8, HEAD), F32),
            pltpu.SemaphoreType.DMA((4,)),
            pltpu.SemaphoreType.DMA((SPANS, 2)),
        ],
        compiler_params=pltpu.CompilerParams(vmem_limit_bytes=VMEM_LIMIT),
        cost_estimate=pl.CostEstimate(
            flops=heads * 6 * half * SPANS * TOK * HEAD, bytes_accessed=6 * 2**20, transcendentals=0
        ),
    )(flags, queries, *pairs)


OUT_GROUPS = 2
OUT_PARTS = 8 // OUT_GROUPS
OUT_COLS = D // OUT_GROUPS
Z_ORDER = (2, 1, 3, 0)


def output_kernel(group, place, mine_ref, got_ref, weight_ref, *refs):
    outs, (mine, got, rows_of, wide, result, loaded, arrived, stored) = refs[:4], refs[4:]
    z, side = place[0], place[1]
    loads = [
        pltpu.make_async_copy(mine_ref, mine, loaded.at[0]),
        pltpu.make_async_copy(got_ref, got, loaded.at[1]),
    ]
    copies = []
    for at in range(SPANS // OUT_GROUPS):
        for which, chosen in enumerate((side, 1 - side)):
            start = (chosen * SPANS + group * (SPANS // OUT_GROUPS) + at) * 2 * SHARD
            source = weight_ref.at[pl.ds(pl.multiple_of(start, 2 * SHARD), 2 * SHARD), :]
            to = wide.at[which, :, at * SHARD : (at + 1) * SHARD]
            copies.append(pltpu.make_async_copy(source, to, arrived.at[at, which]))
    for copy in loads + copies[:8]:
        copy.start()
    for copy in loads:
        copy.wait()
    for at, step in enumerate(Z_ORDER):
        rows = pl.ds(pl.multiple_of(((z + step) % 4) * 64, 64), 64)
        rows_of[0, at * 64 : at * 64 + 64, :] = mine[rows, :]
        rows_of[1, at * 64 : at * 64 + 64, :] = got[rows, :]
    stores = []
    for part in range(OUT_PARTS):
        for copy in copies[part * 4 : part * 4 + 4]:
            copy.wait()
        for copy in copies[part * 4 + 8 : part * 4 + 12]:
            copy.start()
        columns = slice(part * 2 * SHARD, (part + 1) * 2 * SHARD)
        total = jnp.dot(rows_of[0], wide[0, :, columns], preferred_element_type=F32)
        total += jnp.dot(rows_of[1], wide[1, :, columns], preferred_element_type=F32)
        result[part] = total.astype(BF16)
        for index, out in enumerate(outs):
            source = result.at[part, index * 64 : index * 64 + 64, :]
            stores.append(pltpu.make_async_copy(source, out.at[:, columns], stored.at[part, index]))
            stores[-1].start()
    for store in stores:
        store.wait()


def output_partial(group, place, mine, got, weights):
    anywhere = pl.BlockSpec(memory_space=pl.ANY)
    half = TOK // 2
    return pl.pallas_call(
        functools.partial(output_kernel, group),
        in_specs=[pl.BlockSpec(memory_space=pltpu.SMEM)] + [anywhere] * 3,
        out_specs=[anywhere] * 4,
        out_shape=[jax.ShapeDtypeStruct((64, OUT_COLS), BF16)] * 4,
        scratch_shapes=[
            pltpu.VMEM((half, 2 * GCOLS), BF16),
            pltpu.VMEM((half, 2 * GCOLS), BF16),
            pltpu.VMEM((2, half, 2 * GCOLS), BF16),
            pltpu.VMEM((2, 2 * SHARD, OUT_COLS), BF16),
            pltpu.VMEM((OUT_PARTS, half, 2 * SHARD), BF16),
            pltpu.SemaphoreType.DMA((2,)),
            pltpu.SemaphoreType.DMA((SPANS // OUT_GROUPS, 2)),
            pltpu.SemaphoreType.DMA((OUT_PARTS, 4)),
        ],
        compiler_params=pltpu.CompilerParams(vmem_limit_bytes=VMEM_LIMIT),
        cost_estimate=pl.CostEstimate(
            flops=2 * TOK // 2 * OUT_COLS * 4 * GCOLS, bytes_accessed=6 * 2**20, transcendentals=0
        ),
    )(place, mine, got, weights)


def reduce_over_z(far, up, down, stay, sign):
    near, back = (up, down) if sign > 0 else (down, up)
    passed = move(far, dz=sign)
    behind = move(back, dz=-sign)
    near = (near.astype(F32) + passed.astype(F32)).astype(BF16)
    ahead = move(near, dz=sign)
    return (stay.astype(F32) + ahead.astype(F32) + behind.astype(F32)).astype(BF16)


def per_device(hidden, span_ids, w_query, w_keyval, w_out):
    span, uly = lax.axis_index("span"), lax.axis_index("uly")
    xl, y, core = span // 8, (span // 2) % 4, span % 2
    z, xh = uly // 2, uly % 2
    as_int = lambda values: jnp.stack([jnp.asarray(v, jnp.int32) for v in values])

    chips = [x * 4 + (y + dy) % 4 for dy in (0, 3, 1, 2) for x in (xl, 1 - xl)]
    which = as_int([j * 2 + core for j in chips] + chips)
    place = as_int([z, xh])
    block_ids = span_ids.reshape(SPANS, TOK)[:, 0]
    seen = (block_ids <= block_ids[span]).astype(jnp.int32)
    order = [chips[at] * 2 + core for at in (0, 1, 2, 4, 3, 5, 6, 7)]
    seen = seen[as_int(order + [at + 1 - 2 * core for at in order])]
    send_flags = jnp.concatenate([seen, as_int([1 - xh])])
    mine_flags = jnp.concatenate([seen, as_int([xh])])

    own = jnp.concatenate([w_keyval[:, 0], w_keyval[:, 1], w_query], axis=1)
    side = move(own, swap_xl=True)
    up, down = move(own, dy=1), move(own, dy=-1)
    elsewhere = after(as_int([j * 2 + 1 - core for j in range(8)]), own)
    picked = pick_columns(hidden, elsewhere)
    side, up, down, picked, which, place, send_flags, mine_flags = lax.optimization_barrier(
        (side, up, down, picked, which, place, send_flags, mine_flags)
    )
    other_hidden = move(picked, swap_c=True)
    side_up, side_down = move(side, dy=1), move(side, dy=-1)
    up, side_up, side_down, other_hidden, out_shard = lax.optimization_barrier(
        (up, side_up, side_down, other_hidden, w_out)
    )
    far, side_far = move(up, dy=1), move(side_down, dy=-1)

    planes = [
        [index_of(span // 8, span // 2 % 4, span % 2, at, side) for side in range(2) for span in range(SPANS)]
        for at in range(4)
    ]
    weights = lax.all_gather(out_shard, BOTH, axis=0, tiled=True, axis_index_groups=planes)

    pieces = [own, side, up, side_up, down, side_down, far, side_far]
    pair_own, pair_other = project(hidden, other_hidden, which, pieces, 0, 2 * HEAD)
    pair = (pair_own + move(pair_other, swap_c=True)).astype(BF16)

    pair_side = move(pair, swap_xl=True)
    pair_up, pair_down = move(pair, dy=1), move(pair, dy=-1)
    query_own, query_other = project(hidden, other_hidden, after(which, pair), pieces, 2 * HEAD, 2 * GCOLS)
    pair_side, pair_up, pair_down, query_other = lax.optimization_barrier(
        (pair_side, pair_up, pair_down, query_other)
    )
    pair_side_up, pair_side_down = move(pair_side, dy=1), move(pair_side, dy=-1)
    query_other = move(query_other, swap_c=True)
    pairs = jnp.concatenate([pair, pair_side, pair_up, pair_down], axis=0)
    other_pairs = move(pairs, swap_c=True)
    pair_down, pair_side_up, pair_side_down, query_other = lax.optimization_barrier(
        (pair_down, pair_side_up, pair_side_down, query_other)
    )
    pair_far, pair_side_far = move(pair_down, dy=-1), move(pair_side_up, dy=1)
    queries = (query_own + query_other).astype(BF16)
    pair_far, pair_side_far, queries = lax.optimization_barrier((pair_far, pair_side_far, queries))
    more_pairs = jnp.concatenate([pair_side_up, pair_side_down, pair_far, pair_side_far], axis=0)
    pairs = [pairs, more_pairs, other_pairs, move(more_pairs, swap_c=True)]

    send = attend(send_flags, queries, pairs)
    got = move(send, swap_xh=True)
    mine = attend(after(mine_flags, send), queries, pairs)

    totals = []
    for group in range(OUT_GROUPS):
        parts = output_partial(group, place, mine, got, weights)
        totals.append(reduce_over_z(*parts, 1 if group % 2 == 0 else -1))
    return jnp.concatenate(totals, axis=1)


def solution(mesh):
    in_specs = (P("span", None), P(), P("span", "uly"), P("span", None, "uly"), P("uly", "span"))
    out_specs = P(("span", "uly"), None)
    return jax.shard_map(
        per_device, mesh=mesh, in_specs=in_specs, out_specs=out_specs, check_vma=False
    )
```

```python
import functools
import math

import jax
import jax.numpy as jnp
from jax import lax
from jax.experimental import pallas as pl
from jax.experimental.pallas import tpu as pltpu
from jax.sharding import PartitionSpec as P

HEADS = 48
HEAD = 128
D = 6144
SPANS = 16
TOK = 512
SHARD = D // SPANS
GROUP = 3
GCOLS = GROUP * HEAD
SCALE2 = math.log2(math.e) / math.sqrt(HEAD)
SAFE_EXPONENT = 90.0
NEG_LARGE = -1e30
VMEM_LIMIT = 60 * 2**20
BOTH = ("span", "uly")
F32 = jnp.float32
BF16 = jnp.bfloat16


def coords(index):
    span, uly = index // 8, index % 8
    return span // 8, (span // 2) % 4, span % 2, uly // 2, uly % 2


def index_of(xl, y, c, z, xh):
    return (xl * 8 + y * 2 + c) * 8 + z * 2 + xh


def move(array, dx=0, dy=0, dz=0, swap_xl=False, swap_xh=False, swap_c=False):
    pairs = []
    for source in range(128):
        xl, y, c, z, xh = coords(source)
        x = (xh * 2 + xl + dx) % 4
        xh, xl = x // 2, x % 2
        if swap_xl:
            xl = 1 - xl
        if swap_xh:
            xh = 1 - xh
        if swap_c:
            c = 1 - c
        pairs.append((source, index_of(xl, (y + dy) % 4, c, (z + dz) % 4, xh)))
    return lax.ppermute(array, BOTH, pairs)


def after(array, *results):
    return lax.optimization_barrier((array, *results))[0]


def pick_kernel(which, hidden_ref, out_ref, arrived):
    copies = []
    for at in range(8):
        columns = pl.ds(pl.multiple_of(which[at] * SHARD, 128), SHARD)
        to = out_ref.at[:, at * SHARD : (at + 1) * SHARD]
        copies.append(pltpu.make_async_copy(hidden_ref.at[:, columns], to, arrived.at[at]))
    for copy in copies:
        copy.start()
    for copy in copies:
        copy.wait()


def pick_columns(hidden, which):
    return pl.pallas_call(
        pick_kernel,
        in_specs=[pl.BlockSpec(memory_space=pltpu.SMEM), pl.BlockSpec(memory_space=pl.ANY)],
        out_specs=pl.BlockSpec(memory_space=pltpu.VMEM),
        out_shape=jax.ShapeDtypeStruct((TOK, 8 * SHARD), BF16),
        scratch_shapes=[pltpu.SemaphoreType.DMA((8,))],
        compiler_params=pltpu.CompilerParams(vmem_limit_bytes=VMEM_LIMIT),
        cost_estimate=pl.CostEstimate(flops=0, bytes_accessed=4 * TOK * 8 * SHARD, transcendentals=0),
    )(which, hidden)


def project_kernel(which, own_ref, other_ref, *refs):
    pieces, (own_out, other_out, own_rows, other_rows, weight, arrived) = refs[:8], refs[8:]
    copies = []
    for at in range(8):
        columns = pl.ds(pl.multiple_of(which[at] * SHARD, 128), SHARD)
        other = pl.ds(pl.multiple_of(which[8 + at] * SHARD, 128), SHARD)
        to = slice(at * SHARD, (at + 1) * SHARD)
        copies.append(
            [
                pltpu.make_async_copy(pieces[at], weight.at[to, :], arrived.at[at, 0]),
                pltpu.make_async_copy(own_ref.at[:, columns], own_rows.at[:, to], arrived.at[at, 1]),
                pltpu.make_async_copy(other_ref.at[:, other], other_rows.at[:, to], arrived.at[at, 2]),
            ]
        )
    for copy in copies:
        for one in copy:
            one.start()
    for at in range(4):
        for copy in copies[2 * at : 2 * at + 2]:
            for one in copy:
                one.wait()
        to = slice(2 * at * SHARD, (2 * at + 2) * SHARD)
        for rows, out in ((own_rows, own_out), (other_rows, other_out)):
            part = jnp.dot(rows[:, to], weight[to, :], preferred_element_type=F32)
            if at == 0:
                out[...] = part
            else:
                out[...] += part


def project(hidden, other, which, pieces):
    cols = pieces[0].shape[1]
    out = jax.ShapeDtypeStruct((TOK, cols), F32)
    return pl.pallas_call(
        project_kernel,
        in_specs=[pl.BlockSpec(memory_space=pltpu.SMEM)] + [pl.BlockSpec(memory_space=pl.ANY)] * 10,
        out_specs=[pl.BlockSpec(memory_space=pltpu.VMEM)] * 2,
        out_shape=[out, out],
        scratch_shapes=[
            pltpu.VMEM((TOK, 8 * SHARD), BF16),
            pltpu.VMEM((TOK, 8 * SHARD), BF16),
            pltpu.VMEM((8 * SHARD, cols), BF16),
            pltpu.SemaphoreType.DMA((8, 3)),
        ],
        compiler_params=pltpu.CompilerParams(vmem_limit_bytes=VMEM_LIMIT),
        cost_estimate=pl.CostEstimate(
            flops=4 * TOK * 8 * SHARD * cols, bytes_accessed=12 * 2**20, transcendentals=0
        ),
    )(which, hidden, other, *pieces)


QUERY_STEP = 768


def query_kernel(hidden_ref, weight_ref, out_ref, total):
    step = pl.program_id(0)
    part = jnp.dot(hidden_ref[...], weight_ref[...], preferred_element_type=F32)

    @pl.when(step == 0)
    def _():
        total[...] = part

    @pl.when(step > 0)
    def _():
        total[...] += part

    @pl.when(step == pl.num_programs(0) - 1)
    def _():
        out_ref[...] = total[...].astype(BF16)


def project_queries(hidden, weight):
    cols = weight.shape[1]
    return pl.pallas_call(
        query_kernel,
        grid=(D // QUERY_STEP,),
        in_specs=[
            pl.BlockSpec((TOK, QUERY_STEP), lambda i: (0, i)),
            pl.BlockSpec((QUERY_STEP, cols), lambda i: (i, 0)),
        ],
        out_specs=pl.BlockSpec((TOK, cols), lambda i: (0, 0)),
        out_shape=jax.ShapeDtypeStruct((TOK, cols), BF16),
        scratch_shapes=[pltpu.VMEM((TOK, cols), F32)],
        compiler_params=pltpu.CompilerParams(vmem_limit_bytes=VMEM_LIMIT),
        cost_estimate=pl.CostEstimate(
            flops=2 * TOK * D * cols, bytes_accessed=16 * 2**20, transcendentals=0
        ),
    )(hidden, weight)


def attend_kernel(
    flags, query_ref, *refs
):
    pair_refs, refs = refs[:4], refs[4:]
    out_ref, query, keys, value, accum, best, largest, ready, arrived = refs
    side = flags[SPANS]
    heads = HEADS // 8
    loads = []
    for at in range(4):
        rows = pl.ds(pl.multiple_of(at * 128 + side * 64, 64), 64)
        to = query.at[at * 64 : at * 64 + 64, :]
        loads.append(pltpu.make_async_copy(query_ref.at[rows, :], to, ready.at[at]))
    pairs = []
    for ref in pair_refs:
        for at in range(SPANS // 4):
            block, rows = len(pairs), slice(at * TOK, (at + 1) * TOK)
            pairs.append(
                (
                    pltpu.make_async_copy(ref.at[rows, :HEAD], keys.at[block], arrived.at[block, 0]),
                    pltpu.make_async_copy(ref.at[rows, HEAD:], value.at[block, :, :HEAD], arrived.at[block, 1]),
                )
            )
    for load in loads:
        load.start()
    for key, mixed in pairs:
        key.start()
        mixed.start()
    value[:, :, HEAD:] = jnp.ones((SPANS, TOK, HEAD), BF16)
    accum[...] = jnp.zeros_like(accum)
    largest[...] = jnp.zeros_like(largest)
    for load in loads:
        load.wait()
    ones = jnp.ones((HEAD, HEAD), BF16)

    def squares(rows):
        sums = jnp.dot(rows * rows, ones, preferred_element_type=F32)
        return jnp.max(sums.reshape(rows.shape[0] // 8, 8, HEAD), axis=0)

    for head in range(heads):
        largest[0] = jnp.maximum(largest[0], squares(query[:, head * HEAD : (head + 1) * HEAD]))

    def step_small(block):
        key, extended = keys[block], value[block]
        largest[1] = jnp.maximum(largest[1], squares(key))
        for head in range(heads):
            scores = lax.dot_general(
                query[:, head * HEAD : (head + 1) * HEAD],
                key,
                (((1,), (1,)), ((), ())),
                preferred_element_type=F32,
            )
            probs = jnp.exp2(scores * SCALE2).astype(BF16)
            accum[head] += jnp.dot(probs, extended, preferred_element_type=F32)

    def step_any(block):
        def one(head, carry):
            scores = lax.dot_general(
                query[:, pl.ds(pl.multiple_of(head * HEAD, HEAD), HEAD)],
                keys[block],
                (((1,), (1,)), ((), ())),
                preferred_element_type=F32,
            )
            old = best[head]
            new = jnp.maximum(old, jnp.max(scores, axis=1, keepdims=True))
            best[head] = new
            probs = jnp.exp2((scores - new[:, :1]) * SCALE2).astype(BF16)
            factor = jnp.exp2((old - new) * SCALE2)
            accum[head] = accum[head] * factor[:, :1] + jnp.dot(
                probs, value[block], preferred_element_type=F32
            )
            return carry

        lax.fori_loop(0, heads, one, 0)

    def step(block, carry):
        for at, to in enumerate((keys.at[block], value.at[block, :, :HEAD])):
            pltpu.make_async_copy(pair_refs[0].at[:TOK, :HEAD], to, arrived.at[block, at]).wait()

        @pl.when(flags[block] > 0)
        def _():
            step_small(block)

        return carry

    lax.fori_loop(0, SPANS, step, 0)
    bound = jnp.max(largest[0]) * jnp.max(largest[1]) * (1.03 * SCALE2 * SCALE2)

    @pl.when(jnp.logical_not(bound <= SAFE_EXPONENT * SAFE_EXPONENT))
    def _():
        accum[...] = jnp.zeros_like(accum)
        best[...] = jnp.full_like(best, NEG_LARGE)

        def again(block, carry):
            @pl.when(flags[block] > 0)
            def _():
                step_any(block)

            return carry

        lax.fori_loop(0, SPANS, again, 0)

    for head in range(heads):
        mixed = accum[head]
        out_ref[:, head * HEAD : (head + 1) * HEAD] = (mixed[:, :HEAD] / mixed[:, HEAD:]).astype(BF16)


def attend(flags, queries, pairs):
    half, heads = TOK // 2, HEADS // 8
    return pl.pallas_call(
        attend_kernel,
        in_specs=[pl.BlockSpec(memory_space=pltpu.SMEM)] + [pl.BlockSpec(memory_space=pl.ANY)] * 5,
        out_specs=pl.BlockSpec(memory_space=pltpu.VMEM),
        out_shape=jax.ShapeDtypeStruct((half, 2 * GCOLS), BF16),
        scratch_shapes=[
            pltpu.VMEM((half, 2 * GCOLS), BF16),
            pltpu.VMEM((SPANS, TOK, HEAD), BF16),
            pltpu.VMEM((SPANS, TOK, 2 * HEAD), BF16),
            pltpu.VMEM((heads, half, 2 * HEAD), F32),
            pltpu.VMEM((heads, half, HEAD), F32),
            pltpu.VMEM((2, 8, HEAD), F32),
            pltpu.SemaphoreType.DMA((4,)),
            pltpu.SemaphoreType.DMA((SPANS, 2)),
        ],
        compiler_params=pltpu.CompilerParams(vmem_limit_bytes=VMEM_LIMIT),
        cost_estimate=pl.CostEstimate(
            flops=heads * 6 * half * SPANS * TOK * HEAD, bytes_accessed=6 * 2**20, transcendentals=0
        ),
    )(flags, queries, *pairs)


OUT_GROUPS = 2
OUT_PARTS = 8 // OUT_GROUPS
OUT_COLS = D // OUT_GROUPS
Z_ORDER = (2, 1, 3, 0)


def output_kernel(group, place, mine_ref, got_ref, weight_ref, *refs):
    outs, (mine, got, rows_of, wide, result, loaded, arrived, stored) = refs[:4], refs[4:]
    z, side = place[0], place[1]
    loads = [
        pltpu.make_async_copy(mine_ref, mine, loaded.at[0]),
        pltpu.make_async_copy(got_ref, got, loaded.at[1]),
    ]
    copies = []
    for at in range(SPANS // OUT_GROUPS):
        for which, chosen in enumerate((side, 1 - side)):
            start = (chosen * SPANS + group * (SPANS // OUT_GROUPS) + at) * 2 * SHARD
            source = weight_ref.at[pl.ds(pl.multiple_of(start, 2 * SHARD), 2 * SHARD), :]
            to = wide.at[which, :, at * SHARD : (at + 1) * SHARD]
            copies.append(pltpu.make_async_copy(source, to, arrived.at[at, which]))
    for copy in loads + copies[:8]:
        copy.start()
    for copy in loads:
        copy.wait()
    for at, step in enumerate(Z_ORDER):
        rows = pl.ds(pl.multiple_of(((z + step) % 4) * 64, 64), 64)
        rows_of[0, at * 64 : at * 64 + 64, :] = mine[rows, :]
        rows_of[1, at * 64 : at * 64 + 64, :] = got[rows, :]
    stores = []
    for part in range(OUT_PARTS):
        for copy in copies[part * 4 : part * 4 + 4]:
            copy.wait()
        for copy in copies[part * 4 + 8 : part * 4 + 12]:
            copy.start()
        columns = slice(part * 2 * SHARD, (part + 1) * 2 * SHARD)
        total = jnp.dot(rows_of[0], wide[0, :, columns], preferred_element_type=F32)
        total += jnp.dot(rows_of[1], wide[1, :, columns], preferred_element_type=F32)
        result[part] = total.astype(BF16)
        for index, out in enumerate(outs):
            source = result.at[part, index * 64 : index * 64 + 64, :]
            stores.append(pltpu.make_async_copy(source, out.at[:, columns], stored.at[part, index]))
            stores[-1].start()
    for store in stores:
        store.wait()


def output_partial(group, place, mine, got, weights):
    anywhere = pl.BlockSpec(memory_space=pl.ANY)
    half = TOK // 2
    return pl.pallas_call(
        functools.partial(output_kernel, group),
        in_specs=[pl.BlockSpec(memory_space=pltpu.SMEM)] + [anywhere] * 3,
        out_specs=[anywhere] * 4,
        out_shape=[jax.ShapeDtypeStruct((64, OUT_COLS), BF16)] * 4,
        scratch_shapes=[
            pltpu.VMEM((half, 2 * GCOLS), BF16),
            pltpu.VMEM((half, 2 * GCOLS), BF16),
            pltpu.VMEM((2, half, 2 * GCOLS), BF16),
            pltpu.VMEM((2, 2 * SHARD, OUT_COLS), BF16),
            pltpu.VMEM((OUT_PARTS, half, 2 * SHARD), BF16),
            pltpu.SemaphoreType.DMA((2,)),
            pltpu.SemaphoreType.DMA((SPANS // OUT_GROUPS, 2)),
            pltpu.SemaphoreType.DMA((OUT_PARTS, 4)),
        ],
        compiler_params=pltpu.CompilerParams(vmem_limit_bytes=VMEM_LIMIT),
        cost_estimate=pl.CostEstimate(
            flops=2 * TOK // 2 * OUT_COLS * 4 * GCOLS, bytes_accessed=6 * 2**20, transcendentals=0
        ),
    )(place, mine, got, weights)


def reduce_over_z(far, up, down, stay, sign):
    near, back = (up, down) if sign > 0 else (down, up)
    passed = move(far, dz=sign)
    behind = move(back, dz=-sign)
    near = (near.astype(F32) + passed.astype(F32)).astype(BF16)
    ahead = move(near, dz=sign)
    return (stay.astype(F32) + ahead.astype(F32) + behind.astype(F32)).astype(BF16)


def per_device(hidden, span_ids, w_query, w_keyval, w_out):
    span, uly = lax.axis_index("span"), lax.axis_index("uly")
    xl, y, core = span // 8, (span // 2) % 4, span % 2
    z, xh = uly // 2, uly % 2
    as_int = lambda values: jnp.stack([jnp.asarray(v, jnp.int32) for v in values])

    chips = [x * 4 + (y + dy) % 4 for dy in (0, 3, 1, 2) for x in (xl, 1 - xl)]
    which = as_int([j * 2 + core for j in chips] + chips)
    place = as_int([z, xh])
    block_ids = span_ids.reshape(SPANS, TOK)[:, 0]
    seen = (block_ids <= block_ids[span]).astype(jnp.int32)
    order = [chips[at] * 2 + core for at in (0, 1, 2, 4, 3, 5, 6, 7)]
    seen = seen[as_int(order + [at + 1 - 2 * core for at in order])]
    send_flags = jnp.concatenate([seen, as_int([1 - xh])])
    mine_flags = jnp.concatenate([seen, as_int([xh])])

    query_weight = lax.all_gather(w_query, "span", axis=0, tiled=True)

    own = jnp.concatenate([w_keyval[:, 0], w_keyval[:, 1]], axis=1)
    side = move(own, swap_xl=True)
    up, down = move(own, dy=1), move(own, dy=-1)
    elsewhere = after(as_int([j * 2 + 1 - core for j in range(8)]), own)
    picked = pick_columns(hidden, elsewhere)
    side, up, down, picked, which, place, send_flags, mine_flags = lax.optimization_barrier(
        (side, up, down, picked, which, place, send_flags, mine_flags)
    )
    other_hidden = move(picked, swap_c=True)
    side_up, side_down = move(side, dy=1), move(side, dy=-1)
    up, side_up, side_down, other_hidden = lax.optimization_barrier((up, side_up, side_down, other_hidden))
    far, side_far = move(up, dy=1), move(side_down, dy=-1)

    planes = [
        [index_of(span // 8, span // 2 % 4, span % 2, at, side) for side in range(2) for span in range(SPANS)]
        for at in range(4)
    ]
    weights = lax.all_gather(
        after(w_out, far, side_far), BOTH, axis=0, tiled=True, axis_index_groups=planes
    )
    pieces = [own, side, up, side_up, down, side_down, far, side_far]
    pair_own, pair_other = project(hidden, other_hidden, which, pieces)
    pair = (pair_own + move(pair_other, swap_c=True)).astype(BF16)

    pair, query_weight = lax.optimization_barrier((pair, query_weight))
    pair_side = move(pair, swap_xl=True)
    pair_up, pair_down = move(pair, dy=1), move(pair, dy=-1)
    queries = project_queries(hidden, query_weight)
    pair_side, pair_up, pair_down, queries = lax.optimization_barrier((pair_side, pair_up, pair_down, queries))
    pair_side_up, pair_side_down = move(pair_side, dy=1), move(pair_side, dy=-1)
    pairs = jnp.concatenate([pair, pair_side, pair_up, pair_down], axis=0)
    other_pairs = move(pairs, swap_c=True)
    pair_down, pair_side_up, pair_side_down = lax.optimization_barrier((pair_down, pair_side_up, pair_side_down))
    pair_far, pair_side_far = move(pair_down, dy=-1), move(pair_side_up, dy=1)
    more_pairs = jnp.concatenate([pair_side_up, pair_side_down, pair_far, pair_side_far], axis=0)
    pairs = [pairs, more_pairs, other_pairs, move(more_pairs, swap_c=True)]

    send = attend(send_flags, queries, pairs)
    got = move(send, swap_xh=True)
    mine = attend(after(mine_flags, send), queries, pairs)

    totals = []
    for group in range(OUT_GROUPS):
        parts = output_partial(group, place, mine, got, weights)
        totals.append(reduce_over_z(*parts, 1 if group % 2 == 0 else -1))
    return jnp.concatenate(totals, axis=1)


def solution(mesh):
    in_specs = (P("span", None), P(), P("span", "uly"), P("span", None, "uly"), P("uly", "span"))
    out_specs = P(("span", "uly"), None)
    return jax.shard_map(
        per_device, mesh=mesh, in_specs=in_specs, out_specs=out_specs, check_vma=False
    )
```

```python
import functools
import math

import jax
import jax.numpy as jnp
from jax import lax
from jax.experimental import pallas as pl
from jax.experimental.pallas import tpu as pltpu
from jax.sharding import PartitionSpec as P

HEADS = 48
HEAD = 128
D = 6144
SPANS = 16
TOK = 512
SHARD = D // SPANS
GROUP = 3
GCOLS = GROUP * HEAD
FIRST = 2 * HEAD
SCALE2 = math.log2(math.e) / math.sqrt(HEAD)
SAFE_EXPONENT = 90.0
NEG_LARGE = -1e30
VMEM_LIMIT = 60 * 2**20
BOTH = ("span", "uly")
F32 = jnp.float32
BF16 = jnp.bfloat16


def coords(index):
    span, uly = index // 8, index % 8
    return span // 8, (span // 2) % 4, span % 2, uly // 2, uly % 2


def index_of(xl, y, c, z, xh):
    return (xl * 8 + y * 2 + c) * 8 + z * 2 + xh


def move(array, dx=0, dy=0, dz=0, swap_xl=False, swap_xh=False, swap_c=False):
    pairs = []
    for source in range(128):
        xl, y, c, z, xh = coords(source)
        x = (xh * 2 + xl + dx) % 4
        xh, xl = x // 2, x % 2
        if swap_xl:
            xl = 1 - xl
        if swap_xh:
            xh = 1 - xh
        if swap_c:
            c = 1 - c
        pairs.append((source, index_of(xl, (y + dy) % 4, c, (z + dz) % 4, xh)))
    return lax.ppermute(array, BOTH, pairs)


def after(array, *results):
    return lax.optimization_barrier((array, *results))[0]


def pick_kernel(which, hidden_ref, out_ref, arrived):
    copies = []
    for at in range(8):
        columns = pl.ds(pl.multiple_of(which[at] * SHARD, 128), SHARD)
        to = out_ref.at[:, at * SHARD : (at + 1) * SHARD]
        copies.append(pltpu.make_async_copy(hidden_ref.at[:, columns], to, arrived.at[at]))
    for copy in copies:
        copy.start()
    for copy in copies:
        copy.wait()


def pick_columns(hidden, which):
    return pl.pallas_call(
        pick_kernel,
        in_specs=[pl.BlockSpec(memory_space=pltpu.SMEM), pl.BlockSpec(memory_space=pl.ANY)],
        out_specs=pl.BlockSpec(memory_space=pltpu.VMEM),
        out_shape=jax.ShapeDtypeStruct((TOK, 8 * SHARD), BF16),
        scratch_shapes=[pltpu.SemaphoreType.DMA((8,))],
        compiler_params=pltpu.CompilerParams(vmem_limit_bytes=VMEM_LIMIT),
        cost_estimate=pl.CostEstimate(flops=0, bytes_accessed=4 * TOK * 8 * SHARD, transcendentals=0),
    )(which, hidden)


def project_kernel(which, own_ref, other_ref, *refs):
    pieces, (own_out, other_out, own_rows, other_rows, weight, arrived) = refs[:8], refs[8:]
    copies = []
    for at in range(8):
        columns = pl.ds(pl.multiple_of(which[at] * SHARD, 128), SHARD)
        other = pl.ds(pl.multiple_of(which[8 + at] * SHARD, 128), SHARD)
        to = slice(at * SHARD, (at + 1) * SHARD)
        copies.append(
            [
                pltpu.make_async_copy(pieces[at], weight.at[to, :], arrived.at[at, 0]),
                pltpu.make_async_copy(own_ref.at[:, columns], own_rows.at[:, to], arrived.at[at, 1]),
                pltpu.make_async_copy(other_ref.at[:, other], other_rows.at[:, to], arrived.at[at, 2]),
            ]
        )
    for copy in copies:
        for one in copy:
            one.start()
    for at in range(4):
        for copy in copies[2 * at : 2 * at + 2]:
            for one in copy:
                one.wait()
        to = slice(2 * at * SHARD, (2 * at + 2) * SHARD)
        for rows, out in ((own_rows, own_out), (other_rows, other_out)):
            part = jnp.dot(rows[:, to], weight[to, :], preferred_element_type=F32)
            if at == 0:
                out[...] = part
            else:
                out[...] += part


def project(hidden, other, which, pieces):
    cols = pieces[0].shape[1]
    out = jax.ShapeDtypeStruct((TOK, cols), F32)
    return pl.pallas_call(
        project_kernel,
        in_specs=[pl.BlockSpec(memory_space=pltpu.SMEM)] + [pl.BlockSpec(memory_space=pl.ANY)] * 10,
        out_specs=[pl.BlockSpec(memory_space=pltpu.VMEM)] * 2,
        out_shape=[out, out],
        scratch_shapes=[
            pltpu.VMEM((TOK, 8 * SHARD), BF16),
            pltpu.VMEM((TOK, 8 * SHARD), BF16),
            pltpu.VMEM((8 * SHARD, cols), BF16),
            pltpu.SemaphoreType.DMA((8, 3)),
        ],
        compiler_params=pltpu.CompilerParams(vmem_limit_bytes=VMEM_LIMIT),
        cost_estimate=pl.CostEstimate(
            flops=4 * TOK * 8 * SHARD * cols, bytes_accessed=12 * 2**20, transcendentals=0
        ),
    )(which, hidden, other, *pieces)


QUERY_STEP = 768


def query_kernel(hidden_ref, weight_ref, out_ref, total):
    step = pl.program_id(0)
    part = jnp.dot(hidden_ref[...], weight_ref[...], preferred_element_type=F32)

    @pl.when(step == 0)
    def _():
        total[...] = part

    @pl.when(step > 0)
    def _():
        total[...] += part

    @pl.when(step == pl.num_programs(0) - 1)
    def _():
        out_ref[...] = total[...].astype(BF16)


def project_queries(hidden, weight):
    cols = weight.shape[1]
    return pl.pallas_call(
        query_kernel,
        grid=(D // QUERY_STEP,),
        in_specs=[
            pl.BlockSpec((TOK, QUERY_STEP), lambda i: (0, i)),
            pl.BlockSpec((QUERY_STEP, cols), lambda i: (i, 0)),
        ],
        out_specs=pl.BlockSpec((TOK, cols), lambda i: (0, 0)),
        out_shape=jax.ShapeDtypeStruct((TOK, cols), BF16),
        scratch_shapes=[pltpu.VMEM((TOK, cols), F32)],
        compiler_params=pltpu.CompilerParams(vmem_limit_bytes=VMEM_LIMIT),
        cost_estimate=pl.CostEstimate(
            flops=2 * TOK * D * cols, bytes_accessed=16 * 2**20, transcendentals=0
        ),
    )(hidden, weight)


def attend_kernel(flags, first_ref, query_ref, *refs):
    pair_refs, refs = refs[:4], refs[4:]
    out_ref, query, keys, value, accum, best, largest, ready, arrived = refs
    side = flags[SPANS]
    heads = HEADS // 8
    loads = []
    for at in range(4):
        rows = pl.ds(pl.multiple_of(at * 128 + side * 64, 64), 64)
        to = query.at[at * 64 : at * 64 + 64, :FIRST]
        loads.append(pltpu.make_async_copy(first_ref.at[rows, :], to, ready.at[at, 0]))
        to = query.at[at * 64 : at * 64 + 64, FIRST:]
        loads.append(pltpu.make_async_copy(query_ref.at[rows, :], to, ready.at[at, 1]))
    pairs = []
    for ref in pair_refs:
        for at in range(SPANS // 4):
            block, rows = len(pairs), slice(at * TOK, (at + 1) * TOK)
            pairs.append(
                (
                    pltpu.make_async_copy(ref.at[rows, :HEAD], keys.at[block], arrived.at[block, 0]),
                    pltpu.make_async_copy(ref.at[rows, HEAD:], value.at[block, :, :HEAD], arrived.at[block, 1]),
                )
            )
    for load in loads:
        load.start()
    for key, mixed in pairs:
        key.start()
        mixed.start()
    value[:, :, HEAD:] = jnp.ones((SPANS, TOK, HEAD), BF16)
    accum[...] = jnp.zeros_like(accum)
    largest[...] = jnp.zeros_like(largest)
    for load in loads:
        load.wait()
    ones = jnp.ones((HEAD, HEAD), BF16)

    def squares(rows):
        sums = jnp.dot(rows * rows, ones, preferred_element_type=F32)
        return jnp.max(sums.reshape(rows.shape[0] // 8, 8, HEAD), axis=0)

    for head in range(heads):
        largest[0] = jnp.maximum(largest[0], squares(query[:, head * HEAD : (head + 1) * HEAD]))

    def step_small(block):
        key, extended = keys[block], value[block]
        largest[1] = jnp.maximum(largest[1], squares(key))
        for head in range(heads):
            scores = lax.dot_general(
                query[:, head * HEAD : (head + 1) * HEAD],
                key,
                (((1,), (1,)), ((), ())),
                preferred_element_type=F32,
            )
            probs = jnp.exp2(scores * SCALE2).astype(BF16)
            accum[head] += jnp.dot(probs, extended, preferred_element_type=F32)

    def step_any(block):
        def one(head, carry):
            scores = lax.dot_general(
                query[:, pl.ds(pl.multiple_of(head * HEAD, HEAD), HEAD)],
                keys[block],
                (((1,), (1,)), ((), ())),
                preferred_element_type=F32,
            )
            old = best[head]
            new = jnp.maximum(old, jnp.max(scores, axis=1, keepdims=True))
            best[head] = new
            probs = jnp.exp2((scores - new[:, :1]) * SCALE2).astype(BF16)
            factor = jnp.exp2((old - new) * SCALE2)
            accum[head] = accum[head] * factor[:, :1] + jnp.dot(
                probs, value[block], preferred_element_type=F32
            )
            return carry

        lax.fori_loop(0, heads, one, 0)

    def step(block, carry):
        for at, to in enumerate((keys.at[block], value.at[block, :, :HEAD])):
            pltpu.make_async_copy(pair_refs[0].at[:TOK, :HEAD], to, arrived.at[block, at]).wait()

        @pl.when(flags[block] > 0)
        def _():
            step_small(block)

        return carry

    lax.fori_loop(0, SPANS, step, 0)
    bound = jnp.max(largest[0]) * jnp.max(largest[1]) * (1.03 * SCALE2 * SCALE2)

    @pl.when(jnp.logical_not(bound <= SAFE_EXPONENT * SAFE_EXPONENT))
    def _():
        accum[...] = jnp.zeros_like(accum)
        best[...] = jnp.full_like(best, NEG_LARGE)

        def again(block, carry):
            @pl.when(flags[block] > 0)
            def _():
                step_any(block)

            return carry

        lax.fori_loop(0, SPANS, again, 0)

    for head in range(heads):
        mixed = accum[head]
        out_ref[:, head * HEAD : (head + 1) * HEAD] = (mixed[:, :HEAD] / mixed[:, HEAD:]).astype(BF16)


def attend(flags, queries, pairs):
    half, heads = TOK // 2, HEADS // 8
    return pl.pallas_call(
        attend_kernel,
        in_specs=[pl.BlockSpec(memory_space=pltpu.SMEM)] + [pl.BlockSpec(memory_space=pl.ANY)] * 6,
        out_specs=pl.BlockSpec(memory_space=pltpu.VMEM),
        out_shape=jax.ShapeDtypeStruct((half, 2 * GCOLS), BF16),
        scratch_shapes=[
            pltpu.VMEM((half, 2 * GCOLS), BF16),
            pltpu.VMEM((SPANS, TOK, HEAD), BF16),
            pltpu.VMEM((SPANS, TOK, 2 * HEAD), BF16),
            pltpu.VMEM((heads, half, 2 * HEAD), F32),
            pltpu.VMEM((heads, half, HEAD), F32),
            pltpu.VMEM((2, 8, HEAD), F32),
            pltpu.SemaphoreType.DMA((4, 2)),
            pltpu.SemaphoreType.DMA((SPANS, 2)),
        ],
        compiler_params=pltpu.CompilerParams(vmem_limit_bytes=VMEM_LIMIT),
        cost_estimate=pl.CostEstimate(
            flops=heads * 6 * half * SPANS * TOK * HEAD, bytes_accessed=6 * 2**20, transcendentals=0
        ),
    )(flags, *queries, *pairs)


OUT_GROUPS = 2
OUT_PARTS = 8 // OUT_GROUPS
OUT_COLS = D // OUT_GROUPS
Z_ORDER = (2, 1, 3, 0)


def output_kernel(group, place, mine_ref, got_ref, weight_ref, *refs):
    outs, (mine, got, rows_of, wide, result, loaded, arrived, stored) = refs[:4], refs[4:]
    z, side = place[0], place[1]
    loads = [
        pltpu.make_async_copy(mine_ref, mine, loaded.at[0]),
        pltpu.make_async_copy(got_ref, got, loaded.at[1]),
    ]
    copies = []
    for at in range(SPANS // OUT_GROUPS):
        for which, chosen in enumerate((side, 1 - side)):
            start = (chosen * SPANS + group * (SPANS // OUT_GROUPS) + at) * 2 * SHARD
            source = weight_ref.at[pl.ds(pl.multiple_of(start, 2 * SHARD), 2 * SHARD), :]
            to = wide.at[which, :, at * SHARD : (at + 1) * SHARD]
            copies.append(pltpu.make_async_copy(source, to, arrived.at[at, which]))
    for copy in loads + copies[:8]:
        copy.start()
    for copy in loads:
        copy.wait()
    for at, step in enumerate(Z_ORDER):
        rows = pl.ds(pl.multiple_of(((z + step) % 4) * 64, 64), 64)
        rows_of[0, at * 64 : at * 64 + 64, :] = mine[rows, :]
        rows_of[1, at * 64 : at * 64 + 64, :] = got[rows, :]
    stores = []
    for part in range(OUT_PARTS):
        for copy in copies[part * 4 : part * 4 + 4]:
            copy.wait()
        for copy in copies[part * 4 + 8 : part * 4 + 12]:
            copy.start()
        columns = slice(part * 2 * SHARD, (part + 1) * 2 * SHARD)
        total = jnp.dot(rows_of[0], wide[0, :, columns], preferred_element_type=F32)
        total += jnp.dot(rows_of[1], wide[1, :, columns], preferred_element_type=F32)
        result[part] = total.astype(BF16)
        for index, out in enumerate(outs):
            source = result.at[part, index * 64 : index * 64 + 64, :]
            stores.append(pltpu.make_async_copy(source, out.at[:, columns], stored.at[part, index]))
            stores[-1].start()
    for store in stores:
        store.wait()


def output_partial(group, place, mine, got, weights):
    anywhere = pl.BlockSpec(memory_space=pl.ANY)
    half = TOK // 2
    return pl.pallas_call(
        functools.partial(output_kernel, group),
        in_specs=[pl.BlockSpec(memory_space=pltpu.SMEM)] + [anywhere] * 3,
        out_specs=[anywhere] * 4,
        out_shape=[jax.ShapeDtypeStruct((64, OUT_COLS), BF16)] * 4,
        scratch_shapes=[
            pltpu.VMEM((half, 2 * GCOLS), BF16),
            pltpu.VMEM((half, 2 * GCOLS), BF16),
            pltpu.VMEM((2, half, 2 * GCOLS), BF16),
            pltpu.VMEM((2, 2 * SHARD, OUT_COLS), BF16),
            pltpu.VMEM((OUT_PARTS, half, 2 * SHARD), BF16),
            pltpu.SemaphoreType.DMA((2,)),
            pltpu.SemaphoreType.DMA((SPANS // OUT_GROUPS, 2)),
            pltpu.SemaphoreType.DMA((OUT_PARTS, 4)),
        ],
        compiler_params=pltpu.CompilerParams(vmem_limit_bytes=VMEM_LIMIT),
        cost_estimate=pl.CostEstimate(
            flops=2 * TOK // 2 * OUT_COLS * 4 * GCOLS, bytes_accessed=6 * 2**20, transcendentals=0
        ),
    )(place, mine, got, weights)


def reduce_over_z(far, up, down, stay, sign):
    near, back = (up, down) if sign > 0 else (down, up)
    passed = move(far, dz=sign)
    behind = move(back, dz=-sign)
    near = (near.astype(F32) + passed.astype(F32)).astype(BF16)
    ahead = move(near, dz=sign)
    return (stay.astype(F32) + ahead.astype(F32) + behind.astype(F32)).astype(BF16)


def per_device(hidden, span_ids, w_query, w_keyval, w_out):
    span, uly = lax.axis_index("span"), lax.axis_index("uly")
    xl, y, core = span // 8, (span // 2) % 4, span % 2
    z, xh = uly // 2, uly % 2
    as_int = lambda values: jnp.stack([jnp.asarray(v, jnp.int32) for v in values])

    chips = [x * 4 + (y + dy) % 4 for dy in (0, 3, 1, 2) for x in (xl, 1 - xl)]
    which = as_int([j * 2 + core for j in chips] + chips)
    place = as_int([z, xh])
    block_ids = span_ids.reshape(SPANS, TOK)[:, 0]
    seen = (block_ids <= block_ids[span]).astype(jnp.int32)
    order = [chips[at] * 2 + core for at in (0, 1, 2, 4, 3, 5, 6, 7)]
    seen = seen[as_int(order + [at + 1 - 2 * core for at in order])]
    send_flags = jnp.concatenate([seen, as_int([1 - xh])])
    mine_flags = jnp.concatenate([seen, as_int([xh])])

    query_weight = lax.all_gather(w_query[:, FIRST:], "span", axis=0, tiled=True)

    own = jnp.concatenate([w_keyval[:, 0], w_keyval[:, 1], w_query[:, :FIRST]], axis=1)
    side = move(own, swap_xl=True)
    up, down = move(own, dy=1), move(own, dy=-1)
    elsewhere = after(as_int([j * 2 + 1 - core for j in range(8)]), own)
    picked = pick_columns(hidden, elsewhere)
    side, up, down, picked, which, place, send_flags, mine_flags = lax.optimization_barrier(
        (side, up, down, picked, which, place, send_flags, mine_flags)
    )
    other_hidden = move(picked, swap_c=True)
    side_up, side_down = move(side, dy=1), move(side, dy=-1)
    up, side_up, side_down, other_hidden = lax.optimization_barrier((up, side_up, side_down, other_hidden))
    far, side_far = move(up, dy=1), move(side_down, dy=-1)

    planes = [
        [index_of(span // 8, span // 2 % 4, span % 2, at, side) for side in range(2) for span in range(SPANS)]
        for at in range(4)
    ]
    weights = lax.all_gather(
        after(w_out, far, side_far), BOTH, axis=0, tiled=True, axis_index_groups=planes
    )
    pieces = [own, side, up, side_up, down, side_down, far, side_far]
    joint_own, joint_other = project(hidden, other_hidden, which, pieces)
    joint_other = move(joint_other, swap_c=True)
    pair = (joint_own[:, : 2 * HEAD] + joint_other[:, : 2 * HEAD]).astype(BF16)
    first_queries = (joint_own[:, 2 * HEAD :] + joint_other[:, 2 * HEAD :]).astype(BF16)

    pair_side = move(pair, swap_xl=True)
    pair_up, pair_down = move(pair, dy=1), move(pair, dy=-1)
    pair_side, pair_up, pair_down, query_weight = lax.optimization_barrier(
        (pair_side, pair_up, pair_down, query_weight)
    )
    pair_side_up, pair_side_down = move(pair_side, dy=1), move(pair_side, dy=-1)
    pairs = jnp.concatenate([pair, pair_side, pair_up, pair_down], axis=0)
    other_pairs = move(pairs, swap_c=True)
    queries = project_queries(hidden, query_weight)
    pair_down, pair_side_up, pair_side_down, queries = lax.optimization_barrier(
        (pair_down, pair_side_up, pair_side_down, queries)
    )
    pair_far, pair_side_far = move(pair_down, dy=-1), move(pair_side_up, dy=1)
    more_pairs = jnp.concatenate([pair_side_up, pair_side_down, pair_far, pair_side_far], axis=0)
    pairs = [pairs, more_pairs, other_pairs, move(more_pairs, swap_c=True)]

    send = attend(send_flags, [first_queries, queries], pairs)
    got = move(send, swap_xh=True)
    mine = attend(after(mine_flags, send), [first_queries, queries], pairs)

    totals = []
    for group in range(OUT_GROUPS):
        parts = output_partial(group, place, mine, got, weights)
        totals.append(reduce_over_z(*parts, 1 if group % 2 == 0 else -1))
    return jnp.concatenate(totals, axis=1)


def solution(mesh):
    in_specs = (P("span", None), P(), P("span", "uly"), P("span", None, "uly"), P("uly", "span"))
    out_specs = P(("span", "uly"), None)
    return jax.shard_map(
        per_device, mesh=mesh, in_specs=in_specs, out_specs=out_specs, check_vma=False
    )
```

```python
import functools
import math

import jax
import jax.numpy as jnp
from jax import lax
from jax.experimental import pallas as pl
from jax.experimental.pallas import tpu as pltpu
from jax.sharding import PartitionSpec as P

HEADS = 48
HEAD = 128
D = 6144
SPANS = 16
TOK = 512
SHARD = D // SPANS
GROUP = 3
GCOLS = GROUP * HEAD
FIRST = HEAD
SCALE2 = math.log2(math.e) / math.sqrt(HEAD)
SAFE_EXPONENT = 90.0
NEG_LARGE = -1e30
VMEM_LIMIT = 60 * 2**20
BOTH = ("span", "uly")
F32 = jnp.float32
BF16 = jnp.bfloat16


def coords(index):
    span, uly = index // 8, index % 8
    return span // 8, (span // 2) % 4, span % 2, uly // 2, uly % 2


def index_of(xl, y, c, z, xh):
    return (xl * 8 + y * 2 + c) * 8 + z * 2 + xh


def move(array, dx=0, dy=0, dz=0, swap_xl=False, swap_xh=False, swap_c=False):
    pairs = []
    for source in range(128):
        xl, y, c, z, xh = coords(source)
        x = (xh * 2 + xl + dx) % 4
        xh, xl = x // 2, x % 2
        if swap_xl:
            xl = 1 - xl
        if swap_xh:
            xh = 1 - xh
        if swap_c:
            c = 1 - c
        pairs.append((source, index_of(xl, (y + dy) % 4, c, (z + dz) % 4, xh)))
    return lax.ppermute(array, BOTH, pairs)


def after(array, *results):
    return lax.optimization_barrier((array, *results))[0]


def pick_kernel(which, hidden_ref, out_ref, arrived):
    copies = []
    for at in range(8):
        columns = pl.ds(pl.multiple_of(which[at] * SHARD, 128), SHARD)
        to = out_ref.at[:, at * SHARD : (at + 1) * SHARD]
        copies.append(pltpu.make_async_copy(hidden_ref.at[:, columns], to, arrived.at[at]))
    for copy in copies:
        copy.start()
    for copy in copies:
        copy.wait()


def pick_columns(hidden, which):
    return pl.pallas_call(
        pick_kernel,
        in_specs=[pl.BlockSpec(memory_space=pltpu.SMEM), pl.BlockSpec(memory_space=pl.ANY)],
        out_specs=pl.BlockSpec(memory_space=pltpu.VMEM),
        out_shape=jax.ShapeDtypeStruct((TOK, 8 * SHARD), BF16),
        scratch_shapes=[pltpu.SemaphoreType.DMA((8,))],
        compiler_params=pltpu.CompilerParams(vmem_limit_bytes=VMEM_LIMIT),
        cost_estimate=pl.CostEstimate(flops=0, bytes_accessed=4 * TOK * 8 * SHARD, transcendentals=0),
    )(which, hidden)


def project_kernel(which, own_ref, other_ref, *refs):
    pieces, (own_out, other_out, own_rows, other_rows, weight, arrived) = refs[:8], refs[8:]
    copies = []
    for at in range(8):
        columns = pl.ds(pl.multiple_of(which[at] * SHARD, 128), SHARD)
        other = pl.ds(pl.multiple_of(which[8 + at] * SHARD, 128), SHARD)
        to = slice(at * SHARD, (at + 1) * SHARD)
        copies.append(
            [
                pltpu.make_async_copy(pieces[at], weight.at[to, :], arrived.at[at, 0]),
                pltpu.make_async_copy(own_ref.at[:, columns], own_rows.at[:, to], arrived.at[at, 1]),
                pltpu.make_async_copy(other_ref.at[:, other], other_rows.at[:, to], arrived.at[at, 2]),
            ]
        )
    for copy in copies:
        for one in copy:
            one.start()
    for at in range(4):
        for copy in copies[2 * at : 2 * at + 2]:
            for one in copy:
                one.wait()
        to = slice(2 * at * SHARD, (2 * at + 2) * SHARD)
        for rows, out in ((own_rows, own_out), (other_rows, other_out)):
            part = jnp.dot(rows[:, to], weight[to, :], preferred_element_type=F32)
            if at == 0:
                out[...] = part
            else:
                out[...] += part


def project(hidden, other, which, pieces):
    cols = pieces[0].shape[1]
    out = jax.ShapeDtypeStruct((TOK, cols), F32)
    return pl.pallas_call(
        project_kernel,
        in_specs=[pl.BlockSpec(memory_space=pltpu.SMEM)] + [pl.BlockSpec(memory_space=pl.ANY)] * 10,
        out_specs=[pl.BlockSpec(memory_space=pltpu.VMEM)] * 2,
        out_shape=[out, out],
        scratch_shapes=[
            pltpu.VMEM((TOK, 8 * SHARD), BF16),
            pltpu.VMEM((TOK, 8 * SHARD), BF16),
            pltpu.VMEM((8 * SHARD, cols), BF16),
            pltpu.SemaphoreType.DMA((8, 3)),
        ],
        compiler_params=pltpu.CompilerParams(vmem_limit_bytes=VMEM_LIMIT),
        cost_estimate=pl.CostEstimate(
            flops=4 * TOK * 8 * SHARD * cols, bytes_accessed=12 * 2**20, transcendentals=0
        ),
    )(which, hidden, other, *pieces)


QUERY_STEP = 768


def query_kernel(hidden_ref, weight_ref, out_ref, total):
    step = pl.program_id(0)
    part = jnp.dot(hidden_ref[...], weight_ref[...], preferred_element_type=F32)

    @pl.when(step == 0)
    def _():
        total[...] = part

    @pl.when(step > 0)
    def _():
        total[...] += part

    @pl.when(step == pl.num_programs(0) - 1)
    def _():
        out_ref[...] = total[...].astype(BF16)


def project_queries(hidden, weight):
    cols = weight.shape[1]
    return pl.pallas_call(
        query_kernel,
        grid=(D // QUERY_STEP,),
        in_specs=[
            pl.BlockSpec((TOK, QUERY_STEP), lambda i: (0, i)),
            pl.BlockSpec((QUERY_STEP, cols), lambda i: (i, 0)),
        ],
        out_specs=pl.BlockSpec((TOK, cols), lambda i: (0, 0)),
        out_shape=jax.ShapeDtypeStruct((TOK, cols), BF16),
        scratch_shapes=[pltpu.VMEM((TOK, cols), F32)],
        compiler_params=pltpu.CompilerParams(vmem_limit_bytes=VMEM_LIMIT),
        cost_estimate=pl.CostEstimate(
            flops=2 * TOK * D * cols, bytes_accessed=16 * 2**20, transcendentals=0
        ),
    )(hidden, weight)


def attend_kernel(flags, first_ref, query_ref, *refs):
    pair_refs, refs = refs[:4], refs[4:]
    out_ref, query, keys, value, accum, best, largest, ready, arrived = refs
    side = flags[SPANS]
    heads = HEADS // 8
    loads = []
    for at in range(4):
        rows = pl.ds(pl.multiple_of(at * 128 + side * 64, 64), 64)
        to = query.at[at * 64 : at * 64 + 64, :FIRST]
        loads.append(pltpu.make_async_copy(first_ref.at[rows, :], to, ready.at[at, 0]))
        to = query.at[at * 64 : at * 64 + 64, FIRST:]
        loads.append(pltpu.make_async_copy(query_ref.at[rows, :], to, ready.at[at, 1]))
    pairs = []
    for ref in pair_refs:
        for at in range(SPANS // 4):
            block, rows = len(pairs), slice(at * TOK, (at + 1) * TOK)
            pairs.append(
                (
                    pltpu.make_async_copy(ref.at[rows, :HEAD], keys.at[block], arrived.at[block, 0]),
                    pltpu.make_async_copy(ref.at[rows, HEAD:], value.at[block, :, :HEAD], arrived.at[block, 1]),
                )
            )
    for load in loads:
        load.start()
    for key, mixed in pairs:
        key.start()
        mixed.start()
    value[:, :, HEAD:] = jnp.ones((SPANS, TOK, HEAD), BF16)
    accum[...] = jnp.zeros_like(accum)
    largest[...] = jnp.zeros_like(largest)
    for load in loads:
        load.wait()
    ones = jnp.ones((HEAD, HEAD), BF16)

    def squares(rows):
        sums = jnp.dot(rows * rows, ones, preferred_element_type=F32)
        return jnp.max(sums.reshape(rows.shape[0] // 8, 8, HEAD), axis=0)

    for head in range(heads):
        largest[0] = jnp.maximum(largest[0], squares(query[:, head * HEAD : (head + 1) * HEAD]))

    def step_small(block):
        key, extended = keys[block], value[block]
        largest[1] = jnp.maximum(largest[1], squares(key))
        for head in range(heads):
            scores = lax.dot_general(
                query[:, head * HEAD : (head + 1) * HEAD],
                key,
                (((1,), (1,)), ((), ())),
                preferred_element_type=F32,
            )
            probs = jnp.exp2(scores * SCALE2).astype(BF16)
            accum[head] += jnp.dot(probs, extended, preferred_element_type=F32)

    def step_any(block):
        def one(head, carry):
            scores = lax.dot_general(
                query[:, pl.ds(pl.multiple_of(head * HEAD, HEAD), HEAD)],
                keys[block],
                (((1,), (1,)), ((), ())),
                preferred_element_type=F32,
            )
            old = best[head]
            new = jnp.maximum(old, jnp.max(scores, axis=1, keepdims=True))
            best[head] = new
            probs = jnp.exp2((scores - new[:, :1]) * SCALE2).astype(BF16)
            factor = jnp.exp2((old - new) * SCALE2)
            accum[head] = accum[head] * factor[:, :1] + jnp.dot(
                probs, value[block], preferred_element_type=F32
            )
            return carry

        lax.fori_loop(0, heads, one, 0)

    def step(block, carry):
        for at, to in enumerate((keys.at[block], value.at[block, :, :HEAD])):
            pltpu.make_async_copy(pair_refs[0].at[:TOK, :HEAD], to, arrived.at[block, at]).wait()

        @pl.when(flags[block] > 0)
        def _():
            step_small(block)

        return carry

    lax.fori_loop(0, SPANS, step, 0)
    bound = jnp.max(largest[0]) * jnp.max(largest[1]) * (1.03 * SCALE2 * SCALE2)

    @pl.when(jnp.logical_not(bound <= SAFE_EXPONENT * SAFE_EXPONENT))
    def _():
        accum[...] = jnp.zeros_like(accum)
        best[...] = jnp.full_like(best, NEG_LARGE)

        def again(block, carry):
            @pl.when(flags[block] > 0)
            def _():
                step_any(block)

            return carry

        lax.fori_loop(0, SPANS, again, 0)

    for head in range(heads):
        mixed = accum[head]
        out_ref[:, head * HEAD : (head + 1) * HEAD] = (mixed[:, :HEAD] / mixed[:, HEAD:]).astype(BF16)


def attend(flags, queries, pairs):
    half, heads = TOK // 2, HEADS // 8
    return pl.pallas_call(
        attend_kernel,
        in_specs=[pl.BlockSpec(memory_space=pltpu.SMEM)] + [pl.BlockSpec(memory_space=pl.ANY)] * 6,
        out_specs=pl.BlockSpec(memory_space=pltpu.VMEM),
        out_shape=jax.ShapeDtypeStruct((half, 2 * GCOLS), BF16),
        scratch_shapes=[
            pltpu.VMEM((half, 2 * GCOLS), BF16),
            pltpu.VMEM((SPANS, TOK, HEAD), BF16),
            pltpu.VMEM((SPANS, TOK, 2 * HEAD), BF16),
            pltpu.VMEM((heads, half, 2 * HEAD), F32),
            pltpu.VMEM((heads, half, HEAD), F32),
            pltpu.VMEM((2, 8, HEAD), F32),
            pltpu.SemaphoreType.DMA((4, 2)),
            pltpu.SemaphoreType.DMA((SPANS, 2)),
        ],
        compiler_params=pltpu.CompilerParams(vmem_limit_bytes=VMEM_LIMIT),
        cost_estimate=pl.CostEstimate(
            flops=heads * 6 * half * SPANS * TOK * HEAD, bytes_accessed=6 * 2**20, transcendentals=0
        ),
    )(flags, *queries, *pairs)


OUT_GROUPS = 2
OUT_PARTS = 8 // OUT_GROUPS
OUT_COLS = D // OUT_GROUPS
Z_ORDER = (2, 1, 3, 0)


def output_kernel(group, place, mine_ref, got_ref, weight_ref, *refs):
    outs, (mine, got, rows_of, wide, result, loaded, arrived, stored) = refs[:4], refs[4:]
    z, side = place[0], place[1]
    loads = [
        pltpu.make_async_copy(mine_ref, mine, loaded.at[0]),
        pltpu.make_async_copy(got_ref, got, loaded.at[1]),
    ]
    copies = []
    for at in range(SPANS // OUT_GROUPS):
        for which, chosen in enumerate((side, 1 - side)):
            start = (chosen * SPANS + group * (SPANS // OUT_GROUPS) + at) * 2 * SHARD
            source = weight_ref.at[pl.ds(pl.multiple_of(start, 2 * SHARD), 2 * SHARD), :]
            to = wide.at[which, :, at * SHARD : (at + 1) * SHARD]
            copies.append(pltpu.make_async_copy(source, to, arrived.at[at, which]))
    for copy in loads + copies[:8]:
        copy.start()
    for copy in loads:
        copy.wait()
    for at, step in enumerate(Z_ORDER):
        rows = pl.ds(pl.multiple_of(((z + step) % 4) * 64, 64), 64)
        rows_of[0, at * 64 : at * 64 + 64, :] = mine[rows, :]
        rows_of[1, at * 64 : at * 64 + 64, :] = got[rows, :]
    stores = []
    for part in range(OUT_PARTS):
        for copy in copies[part * 4 : part * 4 + 4]:
            copy.wait()
        for copy in copies[part * 4 + 8 : part * 4 + 12]:
            copy.start()
        columns = slice(part * 2 * SHARD, (part + 1) * 2 * SHARD)
        total = jnp.dot(rows_of[0], wide[0, :, columns], preferred_element_type=F32)
        total += jnp.dot(rows_of[1], wide[1, :, columns], preferred_element_type=F32)
        result[part] = total.astype(BF16)
        for index, out in enumerate(outs):
            source = result.at[part, index * 64 : index * 64 + 64, :]
            stores.append(pltpu.make_async_copy(source, out.at[:, columns], stored.at[part, index]))
            stores[-1].start()
    for store in stores:
        store.wait()


def output_partial(group, place, mine, got, weights):
    anywhere = pl.BlockSpec(memory_space=pl.ANY)
    half = TOK // 2
    return pl.pallas_call(
        functools.partial(output_kernel, group),
        in_specs=[pl.BlockSpec(memory_space=pltpu.SMEM)] + [anywhere] * 3,
        out_specs=[anywhere] * 4,
        out_shape=[jax.ShapeDtypeStruct((64, OUT_COLS), BF16)] * 4,
        scratch_shapes=[
            pltpu.VMEM((half, 2 * GCOLS), BF16),
            pltpu.VMEM((half, 2 * GCOLS), BF16),
            pltpu.VMEM((2, half, 2 * GCOLS), BF16),
            pltpu.VMEM((2, 2 * SHARD, OUT_COLS), BF16),
            pltpu.VMEM((OUT_PARTS, half, 2 * SHARD), BF16),
            pltpu.SemaphoreType.DMA((2,)),
            pltpu.SemaphoreType.DMA((SPANS // OUT_GROUPS, 2)),
            pltpu.SemaphoreType.DMA((OUT_PARTS, 4)),
        ],
        compiler_params=pltpu.CompilerParams(vmem_limit_bytes=VMEM_LIMIT),
        cost_estimate=pl.CostEstimate(
            flops=2 * TOK // 2 * OUT_COLS * 4 * GCOLS, bytes_accessed=6 * 2**20, transcendentals=0
        ),
    )(place, mine, got, weights)


def reduce_over_z(far, up, down, stay, sign):
    near, back = (up, down) if sign > 0 else (down, up)
    passed = move(far, dz=sign)
    behind = move(back, dz=-sign)
    near = (near.astype(F32) + passed.astype(F32)).astype(BF16)
    ahead = move(near, dz=sign)
    return (stay.astype(F32) + ahead.astype(F32) + behind.astype(F32)).astype(BF16)


def per_device(hidden, span_ids, w_query, w_keyval, w_out):
    span, uly = lax.axis_index("span"), lax.axis_index("uly")
    xl, y, core = span // 8, (span // 2) % 4, span % 2
    z, xh = uly // 2, uly % 2
    as_int = lambda values: jnp.stack([jnp.asarray(v, jnp.int32) for v in values])

    chips = [x * 4 + (y + dy) % 4 for dy in (0, 3, 1, 2) for x in (xl, 1 - xl)]
    which = as_int([j * 2 + core for j in chips] + chips)
    place = as_int([z, xh])
    block_ids = span_ids.reshape(SPANS, TOK)[:, 0]
    seen = (block_ids <= block_ids[span]).astype(jnp.int32)
    order = [chips[at] * 2 + core for at in (0, 1, 2, 4, 3, 5, 6, 7)]
    seen = seen[as_int(order + [at + 1 - 2 * core for at in order])]
    send_flags = jnp.concatenate([seen, as_int([1 - xh])])
    mine_flags = jnp.concatenate([seen, as_int([xh])])

    query_weight = lax.all_gather(w_query[:, FIRST:], "span", axis=0, tiled=True)

    own = jnp.concatenate([w_keyval[:, 0], w_keyval[:, 1], w_query[:, :FIRST]], axis=1)
    side = move(own, swap_xl=True)
    up, down = move(own, dy=1), move(own, dy=-1)
    elsewhere = after(as_int([j * 2 + 1 - core for j in range(8)]), own)
    picked = pick_columns(hidden, elsewhere)
    side, up, down, picked = lax.optimization_barrier((side, up, down, picked))
    other_hidden = move(picked, swap_c=True)
    side_up, side_down = move(side, dy=1), move(side, dy=-1)
    up, side_up, side_down, other_hidden, which, place, send_flags, mine_flags = lax.optimization_barrier(
        (up, side_up, side_down, other_hidden, which, place, send_flags, mine_flags)
    )
    far, side_far = move(up, dy=1), move(side_down, dy=-1)

    planes = [
        [index_of(span // 8, span // 2 % 4, span % 2, at, side) for side in range(2) for span in range(SPANS)]
        for at in range(4)
    ]
    weights = lax.all_gather(
        after(w_out, far, side_far), BOTH, axis=0, tiled=True, axis_index_groups=planes
    )
    pieces = [own, side, up, side_up, down, side_down, far, side_far]
    joint_own, joint_other = project(hidden, other_hidden, which, pieces)
    joint_other = move(joint_other, swap_c=True)
    pair = (joint_own[:, : 2 * HEAD] + joint_other[:, : 2 * HEAD]).astype(BF16)
    first_queries = (joint_own[:, 2 * HEAD :] + joint_other[:, 2 * HEAD :]).astype(BF16)

    pair_side = move(pair, swap_xl=True)
    pair_up, pair_down = move(pair, dy=1), move(pair, dy=-1)
    pair_side, pair_up, pair_down, query_weight = lax.optimization_barrier(
        (pair_side, pair_up, pair_down, query_weight)
    )
    pair_side_up, pair_side_down = move(pair_side, dy=1), move(pair_side, dy=-1)
    pairs = jnp.concatenate([pair, pair_side, pair_up, pair_down], axis=0)
    other_pairs = move(pairs, swap_c=True)
    queries = project_queries(hidden, query_weight)
    pair_down, pair_side_up, pair_side_down, queries = lax.optimization_barrier(
        (pair_down, pair_side_up, pair_side_down, queries)
    )
    pair_far, pair_side_far = move(pair_down, dy=-1), move(pair_side_up, dy=1)
    more_pairs = jnp.concatenate([pair_side_up, pair_side_down, pair_far, pair_side_far], axis=0)
    pairs = [pairs, more_pairs, other_pairs, move(more_pairs, swap_c=True)]

    send = attend(send_flags, [first_queries, queries], pairs)
    got = move(send, swap_xh=True)
    mine = attend(after(mine_flags, send), [first_queries, queries], pairs)

    totals = []
    for group in range(OUT_GROUPS):
        parts = output_partial(group, place, mine, got, weights)
        totals.append(reduce_over_z(*parts, 1 if group % 2 == 0 else -1))
    return jnp.concatenate(totals, axis=1)


def solution(mesh):
    in_specs = (P("span", None), P(), P("span", "uly"), P("span", None, "uly"), P("uly", "span"))
    out_specs = P(("span", "uly"), None)
    return jax.shard_map(
        per_device, mesh=mesh, in_specs=in_specs, out_specs=out_specs, check_vma=False
    )
```

```python
import functools
import math

import jax
import jax.numpy as jnp
from jax import lax
from jax.experimental import pallas as pl
from jax.experimental.pallas import tpu as pltpu
from jax.sharding import PartitionSpec as P

HEADS = 48
HEAD = 128
D = 6144
SPANS = 16
TOK = 512
SHARD = D // SPANS
GROUP = 3
GCOLS = GROUP * HEAD
FIRST = HEAD
SCALE2 = math.log2(math.e) / math.sqrt(HEAD)
SAFE_EXPONENT = 90.0
NEG_LARGE = -1e30
VMEM_LIMIT = 60 * 2**20
BOTH = ("span", "uly")
F32 = jnp.float32
BF16 = jnp.bfloat16


def coords(index):
    span, uly = index // 8, index % 8
    return span // 8, (span // 2) % 4, span % 2, uly // 2, uly % 2


def index_of(xl, y, c, z, xh):
    return (xl * 8 + y * 2 + c) * 8 + z * 2 + xh


def move(array, dx=0, dy=0, dz=0, swap_xl=False, swap_xh=False, swap_c=False):
    pairs = []
    for source in range(128):
        xl, y, c, z, xh = coords(source)
        x = (xh * 2 + xl + dx) % 4
        xh, xl = x // 2, x % 2
        if swap_xl:
            xl = 1 - xl
        if swap_xh:
            xh = 1 - xh
        if swap_c:
            c = 1 - c
        pairs.append((source, index_of(xl, (y + dy) % 4, c, (z + dz) % 4, xh)))
    return lax.ppermute(array, BOTH, pairs)


def after(array, *results):
    return lax.optimization_barrier((array, *results))[0]


def pick_kernel(which, hidden_ref, out_ref, arrived):
    copies = []
    for at in range(8):
        columns = pl.ds(pl.multiple_of(which[at] * SHARD, 128), SHARD)
        to = out_ref.at[:, at * SHARD : (at + 1) * SHARD]
        copies.append(pltpu.make_async_copy(hidden_ref.at[:, columns], to, arrived.at[at]))
    for copy in copies:
        copy.start()
    for copy in copies:
        copy.wait()


def pick_columns(hidden, which):
    return pl.pallas_call(
        pick_kernel,
        in_specs=[pl.BlockSpec(memory_space=pltpu.SMEM), pl.BlockSpec(memory_space=pl.ANY)],
        out_specs=pl.BlockSpec(memory_space=pltpu.VMEM),
        out_shape=jax.ShapeDtypeStruct((TOK, 8 * SHARD), BF16),
        scratch_shapes=[pltpu.SemaphoreType.DMA((8,))],
        compiler_params=pltpu.CompilerParams(vmem_limit_bytes=VMEM_LIMIT),
        cost_estimate=pl.CostEstimate(flops=0, bytes_accessed=4 * TOK * 8 * SHARD, transcendentals=0),
    )(which, hidden)


def project_kernel(which, own_ref, other_ref, *refs):
    pieces, (own_out, other_out, own_rows, other_rows, weight, arrived) = refs[:8], refs[8:]
    copies = []
    for at in range(8):
        columns = pl.ds(pl.multiple_of(which[at] * SHARD, 128), SHARD)
        other = pl.ds(pl.multiple_of(which[8 + at] * SHARD, 128), SHARD)
        to = slice(at * SHARD, (at + 1) * SHARD)
        copies.append(
            [
                pltpu.make_async_copy(pieces[at], weight.at[to, :], arrived.at[at, 0]),
                pltpu.make_async_copy(own_ref.at[:, columns], own_rows.at[:, to], arrived.at[at, 1]),
                pltpu.make_async_copy(other_ref.at[:, other], other_rows.at[:, to], arrived.at[at, 2]),
            ]
        )
    for copy in copies:
        for one in copy:
            one.start()
    for at in range(4):
        for copy in copies[2 * at : 2 * at + 2]:
            for one in copy:
                one.wait()
        to = slice(2 * at * SHARD, (2 * at + 2) * SHARD)
        for rows, out in ((own_rows, own_out), (other_rows, other_out)):
            part = jnp.dot(rows[:, to], weight[to, :], preferred_element_type=F32)
            if at == 0:
                out[...] = part
            else:
                out[...] += part


def project(hidden, other, which, pieces):
    cols = pieces[0].shape[1]
    out = jax.ShapeDtypeStruct((TOK, cols), F32)
    return pl.pallas_call(
        project_kernel,
        in_specs=[pl.BlockSpec(memory_space=pltpu.SMEM)] + [pl.BlockSpec(memory_space=pl.ANY)] * 10,
        out_specs=[pl.BlockSpec(memory_space=pltpu.VMEM)] * 2,
        out_shape=[out, out],
        scratch_shapes=[
            pltpu.VMEM((TOK, 8 * SHARD), BF16),
            pltpu.VMEM((TOK, 8 * SHARD), BF16),
            pltpu.VMEM((8 * SHARD, cols), BF16),
            pltpu.SemaphoreType.DMA((8, 3)),
        ],
        compiler_params=pltpu.CompilerParams(vmem_limit_bytes=VMEM_LIMIT),
        cost_estimate=pl.CostEstimate(
            flops=4 * TOK * 8 * SHARD * cols, bytes_accessed=12 * 2**20, transcendentals=0
        ),
    )(which, hidden, other, *pieces)


QUERY_STEP = 768


def query_kernel(hidden_ref, weight_ref, out_ref, total):
    step = pl.program_id(0)
    part = jnp.dot(hidden_ref[...], weight_ref[...], preferred_element_type=F32)

    @pl.when(step == 0)
    def _():
        total[...] = part

    @pl.when(step > 0)
    def _():
        total[...] += part

    @pl.when(step == pl.num_programs(0) - 1)
    def _():
        out_ref[...] = total[...].astype(BF16)


def project_queries(hidden, weight):
    cols = weight.shape[1]
    return pl.pallas_call(
        query_kernel,
        grid=(D // QUERY_STEP,),
        in_specs=[
            pl.BlockSpec((TOK, QUERY_STEP), lambda i: (0, i)),
            pl.BlockSpec((QUERY_STEP, cols), lambda i: (i, 0)),
        ],
        out_specs=pl.BlockSpec((TOK, cols), lambda i: (0, 0)),
        out_shape=jax.ShapeDtypeStruct((TOK, cols), BF16),
        scratch_shapes=[pltpu.VMEM((TOK, cols), F32)],
        compiler_params=pltpu.CompilerParams(vmem_limit_bytes=VMEM_LIMIT),
        cost_estimate=pl.CostEstimate(
            flops=2 * TOK * D * cols, bytes_accessed=16 * 2**20, transcendentals=0
        ),
    )(hidden, weight)


def attend_kernel(flags, first_ref, query_ref, *refs):
    pair_refs, refs = refs[:4], refs[4:]
    out_ref, query, keys, value, accum, best, largest, ready, arrived = refs
    side = flags[SPANS]
    heads = HEADS // 8
    loads = []
    for at in range(4):
        rows = pl.ds(pl.multiple_of(at * 128 + side * 64, 64), 64)
        to = query.at[at * 64 : at * 64 + 64, :FIRST]
        loads.append(pltpu.make_async_copy(first_ref.at[rows, :], to, ready.at[at, 0]))
        to = query.at[at * 64 : at * 64 + 64, FIRST:]
        loads.append(pltpu.make_async_copy(query_ref.at[rows, :], to, ready.at[at, 1]))
    pairs = []
    for ref in pair_refs:
        for at in range(SPANS // 4):
            block, rows = len(pairs), slice(at * TOK, (at + 1) * TOK)
            pairs.append(
                (
                    pltpu.make_async_copy(ref.at[rows, :HEAD], keys.at[block], arrived.at[block, 0]),
                    pltpu.make_async_copy(ref.at[rows, HEAD:], value.at[block, :, :HEAD], arrived.at[block, 1]),
                )
            )
    for load in loads:
        load.start()
    for key, mixed in pairs:
        key.start()
        mixed.start()
    value[:, :, HEAD:] = jnp.ones((SPANS, TOK, HEAD), BF16)
    accum[...] = jnp.zeros_like(accum)
    largest[...] = jnp.zeros_like(largest)
    for load in loads:
        load.wait()
    ones = jnp.ones((HEAD, HEAD), BF16)

    def squares(rows):
        sums = jnp.dot(rows * rows, ones, preferred_element_type=F32)
        return jnp.max(sums.reshape(rows.shape[0] // 8, 8, HEAD), axis=0)

    for head in range(heads):
        largest[0] = jnp.maximum(largest[0], squares(query[:, head * HEAD : (head + 1) * HEAD]))

    def step_small(block):
        key, extended = keys[block], value[block]
        largest[1] = jnp.maximum(largest[1], squares(key))
        for head in range(heads):
            scores = lax.dot_general(
                query[:, head * HEAD : (head + 1) * HEAD],
                key,
                (((1,), (1,)), ((), ())),
                preferred_element_type=F32,
            )
            probs = jnp.exp2(scores * SCALE2).astype(BF16)
            accum[head] += jnp.dot(probs, extended, preferred_element_type=F32)

    def step_any(block):
        def one(head, carry):
            scores = lax.dot_general(
                query[:, pl.ds(pl.multiple_of(head * HEAD, HEAD), HEAD)],
                keys[block],
                (((1,), (1,)), ((), ())),
                preferred_element_type=F32,
            )
            old = best[head]
            new = jnp.maximum(old, jnp.max(scores, axis=1, keepdims=True))
            best[head] = new
            probs = jnp.exp2((scores - new[:, :1]) * SCALE2).astype(BF16)
            factor = jnp.exp2((old - new) * SCALE2)
            accum[head] = accum[head] * factor[:, :1] + jnp.dot(
                probs, value[block], preferred_element_type=F32
            )
            return carry

        lax.fori_loop(0, heads, one, 0)

    def step(block, carry):
        for at, to in enumerate((keys.at[block], value.at[block, :, :HEAD])):
            pltpu.make_async_copy(pair_refs[0].at[:TOK, :HEAD], to, arrived.at[block, at]).wait()

        @pl.when(flags[block] > 0)
        def _():
            step_small(block)

        return carry

    lax.fori_loop(0, SPANS, step, 0)
    bound = jnp.max(largest[0]) * jnp.max(largest[1]) * (1.03 * SCALE2 * SCALE2)

    @pl.when(jnp.logical_not(bound <= SAFE_EXPONENT * SAFE_EXPONENT))
    def _():
        accum[...] = jnp.zeros_like(accum)
        best[...] = jnp.full_like(best, NEG_LARGE)

        def again(block, carry):
            @pl.when(flags[block] > 0)
            def _():
                step_any(block)

            return carry

        lax.fori_loop(0, SPANS, again, 0)

    for head in range(heads):
        mixed = accum[head]
        out_ref[:, head * HEAD : (head + 1) * HEAD] = (mixed[:, :HEAD] / mixed[:, HEAD:]).astype(BF16)


def attend(flags, queries, pairs):
    half, heads = TOK // 2, HEADS // 8
    return pl.pallas_call(
        attend_kernel,
        in_specs=[pl.BlockSpec(memory_space=pltpu.SMEM)] + [pl.BlockSpec(memory_space=pl.ANY)] * 6,
        out_specs=pl.BlockSpec(memory_space=pltpu.VMEM),
        out_shape=jax.ShapeDtypeStruct((half, 2 * GCOLS), BF16),
        scratch_shapes=[
            pltpu.VMEM((half, 2 * GCOLS), BF16),
            pltpu.VMEM((SPANS, TOK, HEAD), BF16),
            pltpu.VMEM((SPANS, TOK, 2 * HEAD), BF16),
            pltpu.VMEM((heads, half, 2 * HEAD), F32),
            pltpu.VMEM((heads, half, HEAD), F32),
            pltpu.VMEM((2, 8, HEAD), F32),
            pltpu.SemaphoreType.DMA((4, 2)),
            pltpu.SemaphoreType.DMA((SPANS, 2)),
        ],
        compiler_params=pltpu.CompilerParams(vmem_limit_bytes=VMEM_LIMIT),
        cost_estimate=pl.CostEstimate(
            flops=heads * 6 * half * SPANS * TOK * HEAD, bytes_accessed=6 * 2**20, transcendentals=0
        ),
    )(flags, *queries, *pairs)


OUT_GROUPS = 2
OUT_PARTS = 8 // OUT_GROUPS
OUT_COLS = D // OUT_GROUPS
Z_ORDER = (2, 1, 3, 0)


def output_kernel(group, place, mine_ref, got_ref, weight_ref, *refs):
    outs, (mine, got, rows_of, wide, result, loaded, arrived, stored) = refs[:4], refs[4:]
    z, side = place[0], place[1]
    loads = [
        pltpu.make_async_copy(mine_ref, mine, loaded.at[0]),
        pltpu.make_async_copy(got_ref, got, loaded.at[1]),
    ]
    copies = []
    for part in range(OUT_PARTS):
        for which, chosen in enumerate((side, 1 - side)):
            start = (chosen * SPANS + group * (SPANS // OUT_GROUPS) + part * 2) * SHARD
            source = weight_ref.at[pl.ds(pl.multiple_of(start, 2 * SHARD), 2 * SHARD), :]
            copies.append(pltpu.make_async_copy(source, wide.at[which, part], arrived.at[part, which]))
    for copy in loads + copies[:4]:
        copy.start()
    for copy in loads:
        copy.wait()
    for at, step in enumerate(Z_ORDER):
        rows = pl.ds(pl.multiple_of(((z + step) % 4) * 64, 64), 64)
        rows_of[0, at * 64 : at * 64 + 64, :] = mine[rows, :]
        rows_of[1, at * 64 : at * 64 + 64, :] = got[rows, :]
    stores = []
    by_row = (((1,), (1,)), ((), ()))
    for part in range(OUT_PARTS):
        for copy in copies[part * 2 : part * 2 + 2]:
            copy.wait()
        for copy in copies[part * 2 + 4 : part * 2 + 6]:
            copy.start()
        columns = slice(part * 2 * SHARD, (part + 1) * 2 * SHARD)
        total = lax.dot_general(wide[0, part], rows_of[0], by_row, preferred_element_type=F32)
        total += lax.dot_general(wide[1, part], rows_of[1], by_row, preferred_element_type=F32)
        result[part] = total.astype(BF16).T
        for index, out in enumerate(outs):
            source = result.at[part, index * 64 : index * 64 + 64, :]
            stores.append(pltpu.make_async_copy(source, out.at[:, columns], stored.at[part, index]))
            stores[-1].start()
    for store in stores:
        store.wait()


def output_partial(group, place, mine, got, weights):
    anywhere = pl.BlockSpec(memory_space=pl.ANY)
    half = TOK // 2
    return pl.pallas_call(
        functools.partial(output_kernel, group),
        in_specs=[pl.BlockSpec(memory_space=pltpu.SMEM)] + [anywhere] * 3,
        out_specs=[anywhere] * 4,
        out_shape=[jax.ShapeDtypeStruct((64, OUT_COLS), BF16)] * 4,
        scratch_shapes=[
            pltpu.VMEM((half, 2 * GCOLS), BF16),
            pltpu.VMEM((half, 2 * GCOLS), BF16),
            pltpu.VMEM((2, half, 2 * GCOLS), BF16),
            pltpu.VMEM((2, OUT_PARTS, 2 * SHARD, 2 * GCOLS), BF16),
            pltpu.VMEM((OUT_PARTS, half, 2 * SHARD), BF16),
            pltpu.SemaphoreType.DMA((2,)),
            pltpu.SemaphoreType.DMA((OUT_PARTS, 2)),
            pltpu.SemaphoreType.DMA((OUT_PARTS, 4)),
        ],
        compiler_params=pltpu.CompilerParams(vmem_limit_bytes=VMEM_LIMIT),
        cost_estimate=pl.CostEstimate(
            flops=2 * TOK // 2 * OUT_COLS * 4 * GCOLS, bytes_accessed=6 * 2**20, transcendentals=0
        ),
    )(place, mine, got, weights)


def reduce_over_z(far, up, down, stay, sign):
    near, back = (up, down) if sign > 0 else (down, up)
    passed = move(far, dz=sign)
    behind = move(back, dz=-sign)
    near = (near.astype(F32) + passed.astype(F32)).astype(BF16)
    ahead = move(near, dz=sign)
    return (stay.astype(F32) + ahead.astype(F32) + behind.astype(F32)).astype(BF16)


def per_device(hidden, span_ids, w_query, w_keyval, w_out):
    span, uly = lax.axis_index("span"), lax.axis_index("uly")
    xl, y, core = span // 8, (span // 2) % 4, span % 2
    z, xh = uly // 2, uly % 2
    as_int = lambda values: jnp.stack([jnp.asarray(v, jnp.int32) for v in values])

    chips = [x * 4 + (y + dy) % 4 for dy in (0, 3, 1, 2) for x in (xl, 1 - xl)]
    which = as_int([j * 2 + core for j in chips] + chips)
    place = as_int([z, xh])
    block_ids = span_ids.reshape(SPANS, TOK)[:, 0]
    seen = (block_ids <= block_ids[span]).astype(jnp.int32)
    order = [chips[at] * 2 + core for at in (0, 1, 2, 4, 3, 5, 6, 7)]
    seen = seen[as_int(order + [at + 1 - 2 * core for at in order])]
    send_flags = jnp.concatenate([seen, as_int([1 - xh])])
    mine_flags = jnp.concatenate([seen, as_int([xh])])

    query_weight = lax.all_gather(w_query[:, FIRST:], "span", axis=0, tiled=True)

    own = jnp.concatenate([w_keyval[:, 0], w_keyval[:, 1], w_query[:, :FIRST]], axis=1)
    side = move(own, swap_xl=True)
    up, down = move(own, dy=1), move(own, dy=-1)
    elsewhere = after(as_int([j * 2 + 1 - core for j in range(8)]), own)
    picked = pick_columns(hidden, elsewhere)
    side, up, down, picked = lax.optimization_barrier((side, up, down, picked))
    other_hidden = move(picked, swap_c=True)
    side_up, side_down = move(side, dy=1), move(side, dy=-1)
    out_shard = w_out.T
    up, side_up, side_down, other_hidden, which, place, send_flags, mine_flags, out_shard = lax.optimization_barrier(
        (up, side_up, side_down, other_hidden, which, place, send_flags, mine_flags, out_shard)
    )
    far, side_far = move(up, dy=1), move(side_down, dy=-1)

    planes = [
        [index_of(span // 8, span // 2 % 4, span % 2, at, side) for side in range(2) for span in range(SPANS)]
        for at in range(4)
    ]
    weights = lax.all_gather(
        after(out_shard, far, side_far), BOTH, axis=0, tiled=True, axis_index_groups=planes
    )
    pieces = [own, side, up, side_up, down, side_down, far, side_far]
    joint_own, joint_other = project(hidden, other_hidden, which, pieces)
    joint_other = move(joint_other, swap_c=True)
    pair = (joint_own[:, : 2 * HEAD] + joint_other[:, : 2 * HEAD]).astype(BF16)
    first_queries = (joint_own[:, 2 * HEAD :] + joint_other[:, 2 * HEAD :]).astype(BF16)

    pair_side = move(pair, swap_xl=True)
    pair_up, pair_down = move(pair, dy=1), move(pair, dy=-1)
    pair_side, pair_up, pair_down, query_weight, first_queries = lax.optimization_barrier(
        (pair_side, pair_up, pair_down, query_weight, first_queries)
    )
    pair_side_up, pair_side_down = move(pair_side, dy=1), move(pair_side, dy=-1)
    pairs = jnp.concatenate([pair, pair_side, pair_up, pair_down], axis=0)
    other_pairs = move(pairs, swap_c=True)
    queries = project_queries(hidden, query_weight)
    pair_down, pair_side_up, pair_side_down, queries = lax.optimization_barrier(
        (pair_down, pair_side_up, pair_side_down, queries)
    )
    pair_far, pair_side_far = move(pair_down, dy=-1), move(pair_side_up, dy=1)
    more_pairs = jnp.concatenate([pair_side_up, pair_side_down, pair_far, pair_side_far], axis=0)
    pairs = [pairs, more_pairs, other_pairs, move(more_pairs, swap_c=True)]

    send = attend(send_flags, [first_queries, queries], pairs)
    got = move(send, swap_xh=True)
    mine = attend(after(mine_flags, send), [first_queries, queries], pairs)

    totals = []
    for group in range(OUT_GROUPS):
        parts = output_partial(group, place, mine, got, weights)
        totals.append(reduce_over_z(*parts, 1 if group % 2 == 0 else -1))
    return jnp.concatenate(totals, axis=1)


def solution(mesh):
    in_specs = (P("span", None), P(), P("span", "uly"), P("span", None, "uly"), P("uly", "span"))
    out_specs = P(("span", "uly"), None)
    return jax.shard_map(
        per_device, mesh=mesh, in_specs=in_specs, out_specs=out_specs, check_vma=False
    )
```

```python
import functools
import math

import jax
import jax.numpy as jnp
from jax import lax
from jax.experimental import pallas as pl
from jax.experimental.pallas import tpu as pltpu
from jax.sharding import PartitionSpec as P

HEADS = 48
HEAD = 128
D = 6144
SPANS = 16
TOK = 512
SHARD = D // SPANS
GROUP = 3
GCOLS = GROUP * HEAD
FIRST = HEAD
SCALE2 = math.log2(math.e) / math.sqrt(HEAD)
SAFE_EXPONENT = 90.0
NEG_LARGE = -1e30
VMEM_LIMIT = 60 * 2**20
BOTH = ("span", "uly")
F32 = jnp.float32
BF16 = jnp.bfloat16


def coords(index):
    span, uly = index // 8, index % 8
    return span // 8, (span // 2) % 4, span % 2, uly // 2, uly % 2


def index_of(xl, y, c, z, xh):
    return (xl * 8 + y * 2 + c) * 8 + z * 2 + xh


def move(array, dx=0, dy=0, dz=0, swap_xl=False, swap_xh=False, swap_c=False):
    pairs = []
    for source in range(128):
        xl, y, c, z, xh = coords(source)
        x = (xh * 2 + xl + dx) % 4
        xh, xl = x // 2, x % 2
        if swap_xl:
            xl = 1 - xl
        if swap_xh:
            xh = 1 - xh
        if swap_c:
            c = 1 - c
        pairs.append((source, index_of(xl, (y + dy) % 4, c, (z + dz) % 4, xh)))
    return lax.ppermute(array, BOTH, pairs)


def after(array, *results):
    return lax.optimization_barrier((array, *results))[0]


def pick_kernel(which, hidden_ref, out_ref, arrived):
    copies = []
    for at in range(8):
        columns = pl.ds(pl.multiple_of(which[at] * SHARD, 128), SHARD)
        to = out_ref.at[:, at * SHARD : (at + 1) * SHARD]
        copies.append(pltpu.make_async_copy(hidden_ref.at[:, columns], to, arrived.at[at]))
    for copy in copies:
        copy.start()
    for copy in copies:
        copy.wait()


def pick_columns(hidden, which):
    return pl.pallas_call(
        pick_kernel,
        in_specs=[pl.BlockSpec(memory_space=pltpu.SMEM), pl.BlockSpec(memory_space=pl.ANY)],
        out_specs=pl.BlockSpec(memory_space=pltpu.VMEM),
        out_shape=jax.ShapeDtypeStruct((TOK, 8 * SHARD), BF16),
        scratch_shapes=[pltpu.SemaphoreType.DMA((8,))],
        compiler_params=pltpu.CompilerParams(vmem_limit_bytes=VMEM_LIMIT),
        cost_estimate=pl.CostEstimate(flops=0, bytes_accessed=4 * TOK * 8 * SHARD, transcendentals=0),
    )(which, hidden)


def project_kernel(which, own_ref, other_ref, *refs):
    pieces, (own_out, other_out, own_rows, other_rows, weight, arrived) = refs[:8], refs[8:]
    copies = []
    for at in range(8):
        columns = pl.ds(pl.multiple_of(which[at] * SHARD, 128), SHARD)
        other = pl.ds(pl.multiple_of(which[8 + at] * SHARD, 128), SHARD)
        to = slice(at * SHARD, (at + 1) * SHARD)
        copies.append(
            [
                pltpu.make_async_copy(pieces[at], weight.at[to, :], arrived.at[at, 0]),
                pltpu.make_async_copy(own_ref.at[:, columns], own_rows.at[:, to], arrived.at[at, 1]),
                pltpu.make_async_copy(other_ref.at[:, other], other_rows.at[:, to], arrived.at[at, 2]),
            ]
        )
    for copy in copies:
        for one in copy:
            one.start()
    for at in range(4):
        for copy in copies[2 * at : 2 * at + 2]:
            for one in copy:
                one.wait()
        to = slice(2 * at * SHARD, (2 * at + 2) * SHARD)
        for rows, out in ((own_rows, own_out), (other_rows, other_out)):
            part = jnp.dot(rows[:, to], weight[to, :], preferred_element_type=F32)
            if at == 0:
                out[...] = part
            else:
                out[...] += part


def project(hidden, other, which, pieces):
    cols = pieces[0].shape[1]
    out = jax.ShapeDtypeStruct((TOK, cols), F32)
    return pl.pallas_call(
        project_kernel,
        in_specs=[pl.BlockSpec(memory_space=pltpu.SMEM)] + [pl.BlockSpec(memory_space=pl.ANY)] * 10,
        out_specs=[pl.BlockSpec(memory_space=pltpu.VMEM)] * 2,
        out_shape=[out, out],
        scratch_shapes=[
            pltpu.VMEM((TOK, 8 * SHARD), BF16),
            pltpu.VMEM((TOK, 8 * SHARD), BF16),
            pltpu.VMEM((8 * SHARD, cols), BF16),
            pltpu.SemaphoreType.DMA((8, 3)),
        ],
        compiler_params=pltpu.CompilerParams(vmem_limit_bytes=VMEM_LIMIT),
        cost_estimate=pl.CostEstimate(
            flops=4 * TOK * 8 * SHARD * cols, bytes_accessed=12 * 2**20, transcendentals=0
        ),
    )(which, hidden, other, *pieces)


QUERY_STEP = 768


def query_kernel(hidden_ref, weight_ref, out_ref, total):
    step = pl.program_id(0)
    part = jnp.dot(hidden_ref[...], weight_ref[...], preferred_element_type=F32)

    @pl.when(step == 0)
    def _():
        total[...] = part

    @pl.when(step > 0)
    def _():
        total[...] += part

    @pl.when(step == pl.num_programs(0) - 1)
    def _():
        out_ref[...] = total[...].astype(BF16)


def project_queries(hidden, weight):
    cols = weight.shape[1]
    return pl.pallas_call(
        query_kernel,
        grid=(D // QUERY_STEP,),
        in_specs=[
            pl.BlockSpec((TOK, QUERY_STEP), lambda i: (0, i)),
            pl.BlockSpec((QUERY_STEP, cols), lambda i: (i, 0)),
        ],
        out_specs=pl.BlockSpec((TOK, cols), lambda i: (0, 0)),
        out_shape=jax.ShapeDtypeStruct((TOK, cols), BF16),
        scratch_shapes=[pltpu.VMEM((TOK, cols), F32)],
        compiler_params=pltpu.CompilerParams(vmem_limit_bytes=VMEM_LIMIT),
        cost_estimate=pl.CostEstimate(
            flops=2 * TOK * D * cols, bytes_accessed=16 * 2**20, transcendentals=0
        ),
    )(hidden, weight)


def attend_kernel(flags, first_ref, query_ref, *refs):
    pair_refs, refs = refs[:4], refs[4:]
    out_ref, query, keys, value, accum, best, largest, ready, arrived = refs
    side = flags[SPANS]
    heads = HEADS // 8
    loads = []
    for at in range(4):
        rows = pl.ds(pl.multiple_of(at * 128 + side * 64, 64), 64)
        to = query.at[at * 64 : at * 64 + 64, :FIRST]
        loads.append(pltpu.make_async_copy(first_ref.at[rows, :], to, ready.at[at, 0]))
        to = query.at[at * 64 : at * 64 + 64, FIRST:]
        loads.append(pltpu.make_async_copy(query_ref.at[rows, :], to, ready.at[at, 1]))
    pairs = []
    for ref in pair_refs:
        for at in range(SPANS // 4):
            block, rows = len(pairs), slice(at * TOK, (at + 1) * TOK)
            pairs.append(
                (
                    pltpu.make_async_copy(ref.at[rows, :HEAD], keys.at[block], arrived.at[block, 0]),
                    pltpu.make_async_copy(ref.at[rows, HEAD:], value.at[block, :, :HEAD], arrived.at[block, 1]),
                )
            )
    for load in loads:
        load.start()
    for key, mixed in pairs:
        key.start()
        mixed.start()
    value[:, :, HEAD:] = jnp.ones((SPANS, TOK, HEAD), BF16)
    accum[...] = jnp.zeros_like(accum)
    largest[...] = jnp.zeros_like(largest)
    for load in loads:
        load.wait()
    ones = jnp.ones((HEAD, HEAD), BF16)

    def squares(rows):
        sums = jnp.dot(rows * rows, ones, preferred_element_type=F32)
        return jnp.max(sums.reshape(rows.shape[0] // 8, 8, HEAD), axis=0)

    for head in range(heads):
        largest[0] = jnp.maximum(largest[0], squares(query[:, head * HEAD : (head + 1) * HEAD]))

    def step_small(block):
        key, extended = keys[block], value[block]
        largest[1] = jnp.maximum(largest[1], squares(key))
        for head in range(heads):
            scores = lax.dot_general(
                query[:, head * HEAD : (head + 1) * HEAD],
                key,
                (((1,), (1,)), ((), ())),
                preferred_element_type=F32,
            )
            probs = jnp.exp2(scores * SCALE2).astype(BF16)
            accum[head] += jnp.dot(probs, extended, preferred_element_type=F32)

    def step_any(block):
        def one(head, carry):
            scores = lax.dot_general(
                query[:, pl.ds(pl.multiple_of(head * HEAD, HEAD), HEAD)],
                keys[block],
                (((1,), (1,)), ((), ())),
                preferred_element_type=F32,
            )
            old = best[head]
            new = jnp.maximum(old, jnp.max(scores, axis=1, keepdims=True))
            best[head] = new
            probs = jnp.exp2((scores - new[:, :1]) * SCALE2).astype(BF16)
            factor = jnp.exp2((old - new) * SCALE2)
            accum[head] = accum[head] * factor[:, :1] + jnp.dot(
                probs, value[block], preferred_element_type=F32
            )
            return carry

        lax.fori_loop(0, heads, one, 0)

    def step(block, carry):
        for at, to in enumerate((keys.at[block], value.at[block, :, :HEAD])):
            pltpu.make_async_copy(pair_refs[0].at[:TOK, :HEAD], to, arrived.at[block, at]).wait()

        @pl.when(flags[block] > 0)
        def _():
            step_small(block)

        return carry

    lax.fori_loop(0, SPANS, step, 0)
    bound = jnp.max(largest[0]) * jnp.max(largest[1]) * (1.03 * SCALE2 * SCALE2)

    @pl.when(jnp.logical_not(bound <= SAFE_EXPONENT * SAFE_EXPONENT))
    def _():
        accum[...] = jnp.zeros_like(accum)
        best[...] = jnp.full_like(best, NEG_LARGE)

        def again(block, carry):
            @pl.when(flags[block] > 0)
            def _():
                step_any(block)

            return carry

        lax.fori_loop(0, SPANS, again, 0)

    for head in range(heads):
        mixed = accum[head]
        out_ref[:, head * HEAD : (head + 1) * HEAD] = (mixed[:, :HEAD] / mixed[:, HEAD:]).astype(BF16)


def attend(flags, queries, pairs):
    half, heads = TOK // 2, HEADS // 8
    return pl.pallas_call(
        attend_kernel,
        in_specs=[pl.BlockSpec(memory_space=pltpu.SMEM)] + [pl.BlockSpec(memory_space=pl.ANY)] * 6,
        out_specs=pl.BlockSpec(memory_space=pltpu.VMEM),
        out_shape=jax.ShapeDtypeStruct((half, 2 * GCOLS), BF16),
        scratch_shapes=[
            pltpu.VMEM((half, 2 * GCOLS), BF16),
            pltpu.VMEM((SPANS, TOK, HEAD), BF16),
            pltpu.VMEM((SPANS, TOK, 2 * HEAD), BF16),
            pltpu.VMEM((heads, half, 2 * HEAD), F32),
            pltpu.VMEM((heads, half, HEAD), F32),
            pltpu.VMEM((2, 8, HEAD), F32),
            pltpu.SemaphoreType.DMA((4, 2)),
            pltpu.SemaphoreType.DMA((SPANS, 2)),
        ],
        compiler_params=pltpu.CompilerParams(vmem_limit_bytes=VMEM_LIMIT),
        cost_estimate=pl.CostEstimate(
            flops=heads * 6 * half * SPANS * TOK * HEAD, bytes_accessed=6 * 2**20, transcendentals=0
        ),
    )(flags, *queries, *pairs)


OUT_GROUPS = 2
OUT_PARTS = 8 // OUT_GROUPS
OUT_COLS = D // OUT_GROUPS
Z_ORDER = (2, 1, 3, 0)


def output_kernel(group, place, mine_ref, got_ref, weight_ref, *refs):
    outs, (mine, got, rows_of, wide, result, loaded, arrived, stored) = refs[:4], refs[4:]
    z, side = place[0], place[1]
    loads = [
        pltpu.make_async_copy(mine_ref, mine, loaded.at[0]),
        pltpu.make_async_copy(got_ref, got, loaded.at[1]),
    ]
    copies = []
    for at in range(SPANS // OUT_GROUPS):
        for which, chosen in enumerate((side, 1 - side)):
            start = (chosen * SPANS + group * (SPANS // OUT_GROUPS) + at) * 2 * SHARD
            source = weight_ref.at[pl.ds(pl.multiple_of(start, 2 * SHARD), 2 * SHARD), :]
            to = wide.at[which * 2 * SHARD : (which + 1) * 2 * SHARD, at * SHARD : (at + 1) * SHARD]
            copies.append(pltpu.make_async_copy(source, to, arrived.at[at, which]))
    for copy in loads + copies[:8]:
        copy.start()
    for copy in loads:
        copy.wait()
    for at, step in enumerate(Z_ORDER):
        rows = pl.ds(pl.multiple_of(((z + step) % 4) * 64, 64), 64)
        rows_of[at * 64 : at * 64 + 64, : 2 * GCOLS] = mine[rows, :]
        rows_of[at * 64 : at * 64 + 64, 2 * GCOLS :] = got[rows, :]
    stores = []
    for part in range(OUT_PARTS):
        for copy in copies[part * 4 : part * 4 + 4]:
            copy.wait()
        for copy in copies[part * 4 + 8 : part * 4 + 12]:
            copy.start()
        columns = slice(part * 2 * SHARD, (part + 1) * 2 * SHARD)
        result[part] = jnp.dot(rows_of[...], wide[:, columns], preferred_element_type=F32).astype(BF16)
        for index, out in enumerate(outs):
            source = result.at[part, index * 64 : index * 64 + 64, :]
            stores.append(pltpu.make_async_copy(source, out.at[:, columns], stored.at[part, index]))
            stores[-1].start()
    for store in stores:
        store.wait()


def output_partial(group, place, mine, got, weights):
    anywhere = pl.BlockSpec(memory_space=pl.ANY)
    half = TOK // 2
    return pl.pallas_call(
        functools.partial(output_kernel, group),
        in_specs=[pl.BlockSpec(memory_space=pltpu.SMEM)] + [anywhere] * 3,
        out_specs=[anywhere] * 4,
        out_shape=[jax.ShapeDtypeStruct((64, OUT_COLS), BF16)] * 4,
        scratch_shapes=[
            pltpu.VMEM((half, 2 * GCOLS), BF16),
            pltpu.VMEM((half, 2 * GCOLS), BF16),
            pltpu.VMEM((half, 4 * GCOLS), BF16),
            pltpu.VMEM((4 * SHARD, OUT_COLS), BF16),
            pltpu.VMEM((OUT_PARTS, half, 2 * SHARD), BF16),
            pltpu.SemaphoreType.DMA((2,)),
            pltpu.SemaphoreType.DMA((SPANS // OUT_GROUPS, 2)),
            pltpu.SemaphoreType.DMA((OUT_PARTS, 4)),
        ],
        compiler_params=pltpu.CompilerParams(vmem_limit_bytes=VMEM_LIMIT),
        cost_estimate=pl.CostEstimate(
            flops=2 * TOK // 2 * OUT_COLS * 4 * GCOLS, bytes_accessed=6 * 2**20, transcendentals=0
        ),
    )(place, mine, got, weights)


def reduce_over_z(far, up, down, stay, sign):
    near, back = (up, down) if sign > 0 else (down, up)
    passed = move(far, dz=sign)
    behind = move(back, dz=-sign)
    near = (near.astype(F32) + passed.astype(F32)).astype(BF16)
    ahead = move(near, dz=sign)
    return (stay.astype(F32) + ahead.astype(F32) + behind.astype(F32)).astype(BF16)


def per_device(hidden, span_ids, w_query, w_keyval, w_out):
    span, uly = lax.axis_index("span"), lax.axis_index("uly")
    xl, y, core = span // 8, (span // 2) % 4, span % 2
    z, xh = uly // 2, uly % 2
    as_int = lambda values: jnp.stack([jnp.asarray(v, jnp.int32) for v in values])

    chips = [x * 4 + (y + dy) % 4 for dy in (0, 3, 1, 2) for x in (xl, 1 - xl)]
    which = as_int([j * 2 + core for j in chips] + chips)
    place = as_int([z, xh])
    block_ids = span_ids.reshape(SPANS, TOK)[:, 0]
    seen = (block_ids <= block_ids[span]).astype(jnp.int32)
    order = [chips[at] * 2 + core for at in (0, 1, 2, 4, 3, 5, 6, 7)]
    seen = seen[as_int(order + [at + 1 - 2 * core for at in order])]
    send_flags = jnp.concatenate([seen, as_int([1 - xh])])
    mine_flags = jnp.concatenate([seen, as_int([xh])])

    query_weight = lax.all_gather(w_query[:, FIRST:], "span", axis=0, tiled=True)

    own = jnp.concatenate([w_keyval[:, 0], w_keyval[:, 1], w_query[:, :FIRST]], axis=1)
    side = move(own, swap_xl=True)
    up, down = move(own, dy=1), move(own, dy=-1)
    elsewhere = after(as_int([j * 2 + 1 - core for j in range(8)]), own)
    picked = pick_columns(hidden, elsewhere)
    side, up, down, picked = lax.optimization_barrier((side, up, down, picked))
    other_hidden = move(picked, swap_c=True)
    side_up, side_down = move(side, dy=1), move(side, dy=-1)
    up, side_up, side_down, other_hidden, which, place, send_flags, mine_flags = lax.optimization_barrier(
        (up, side_up, side_down, other_hidden, which, place, send_flags, mine_flags)
    )
    far, side_far = move(up, dy=1), move(side_down, dy=-1)

    planes = [
        [index_of(span // 8, span // 2 % 4, span % 2, at, side) for side in range(2) for span in range(SPANS)]
        for at in range(4)
    ]
    weights = lax.all_gather(
        after(w_out, far, side_far), BOTH, axis=0, tiled=True, axis_index_groups=planes
    )
    pieces = [own, side, up, side_up, down, side_down, far, side_far]
    joint_own, joint_other = project(hidden, other_hidden, which, pieces)
    joint_other = move(joint_other, swap_c=True)
    pair = (joint_own[:, : 2 * HEAD] + joint_other[:, : 2 * HEAD]).astype(BF16)
    first_queries = (joint_own[:, 2 * HEAD :] + joint_other[:, 2 * HEAD :]).astype(BF16)

    pair_side = move(pair, swap_xl=True)
    pair_up, pair_down = move(pair, dy=1), move(pair, dy=-1)
    pair_side, pair_up, pair_down, query_weight, first_queries = lax.optimization_barrier(
        (pair_side, pair_up, pair_down, query_weight, first_queries)
    )
    pair_side_up, pair_side_down = move(pair_side, dy=1), move(pair_side, dy=-1)
    pairs = jnp.concatenate([pair, pair_side, pair_up, pair_down], axis=0)
    other_pairs = move(pairs, swap_c=True)
    queries = project_queries(hidden, query_weight)
    pair_down, pair_side_up, pair_side_down, queries = lax.optimization_barrier(
        (pair_down, pair_side_up, pair_side_down, queries)
    )
    pair_far, pair_side_far = move(pair_down, dy=-1), move(pair_side_up, dy=1)
    more_pairs = jnp.concatenate([pair_side_up, pair_side_down, pair_far, pair_side_far], axis=0)
    pairs = [pairs, more_pairs, other_pairs, move(more_pairs, swap_c=True)]

    send = attend(send_flags, [first_queries, queries], pairs)
    got = move(send, swap_xh=True)
    mine = attend(after(mine_flags, send), [first_queries, queries], pairs)

    totals = []
    for group in range(OUT_GROUPS):
        parts = output_partial(group, place, mine, got, weights)
        totals.append(reduce_over_z(*parts, 1 if group % 2 == 0 else -1))
    return jnp.concatenate(totals, axis=1)


def solution(mesh):
    in_specs = (P("span", None), P(), P("span", "uly"), P("span", None, "uly"), P("uly", "span"))
    out_specs = P(("span", "uly"), None)
    return jax.shard_map(
        per_device, mesh=mesh, in_specs=in_specs, out_specs=out_specs, check_vma=False
    )
```

```python
import functools
import math

import jax
import jax.numpy as jnp
from jax import lax
from jax.experimental import pallas as pl
from jax.experimental.pallas import tpu as pltpu
from jax.sharding import PartitionSpec as P

HEADS = 48
HEAD = 128
D = 6144
SPANS = 16
TOK = 512
SHARD = D // SPANS
GROUP = 3
GCOLS = GROUP * HEAD
FIRST = HEAD
SCALE2 = math.log2(math.e) / math.sqrt(HEAD)
SAFE_EXPONENT = 90.0
NEG_LARGE = -1e30
VMEM_LIMIT = 60 * 2**20
BOTH = ("span", "uly")
F32 = jnp.float32
BF16 = jnp.bfloat16


def coords(index):
    span, uly = index // 8, index % 8
    return span // 8, (span // 2) % 4, span % 2, uly // 2, uly % 2


def index_of(xl, y, c, z, xh):
    return (xl * 8 + y * 2 + c) * 8 + z * 2 + xh


def move(array, dx=0, dy=0, dz=0, swap_xl=False, swap_xh=False, swap_c=False):
    pairs = []
    for source in range(128):
        xl, y, c, z, xh = coords(source)
        x = (xh * 2 + xl + dx) % 4
        xh, xl = x // 2, x % 2
        if swap_xl:
            xl = 1 - xl
        if swap_xh:
            xh = 1 - xh
        if swap_c:
            c = 1 - c
        pairs.append((source, index_of(xl, (y + dy) % 4, c, (z + dz) % 4, xh)))
    return lax.ppermute(array, BOTH, pairs)


def after(array, *results):
    return lax.optimization_barrier((array, *results))[0]


def pick_kernel(which, hidden_ref, out_ref, arrived):
    copies = []
    for at in range(8):
        columns = pl.ds(pl.multiple_of(which[at] * SHARD, 128), SHARD)
        to = out_ref.at[:, at * SHARD : (at + 1) * SHARD]
        copies.append(pltpu.make_async_copy(hidden_ref.at[:, columns], to, arrived.at[at]))
    for copy in copies:
        copy.start()
    for copy in copies:
        copy.wait()


def pick_columns(hidden, which):
    return pl.pallas_call(
        pick_kernel,
        in_specs=[pl.BlockSpec(memory_space=pltpu.SMEM), pl.BlockSpec(memory_space=pl.ANY)],
        out_specs=pl.BlockSpec(memory_space=pltpu.VMEM),
        out_shape=jax.ShapeDtypeStruct((TOK, 8 * SHARD), BF16),
        scratch_shapes=[pltpu.SemaphoreType.DMA((8,))],
        compiler_params=pltpu.CompilerParams(vmem_limit_bytes=VMEM_LIMIT),
        cost_estimate=pl.CostEstimate(flops=0, bytes_accessed=4 * TOK * 8 * SHARD, transcendentals=0),
    )(which, hidden)


def project_kernel(which, own_ref, other_ref, *refs):
    pieces, (own_out, other_out, own_rows, other_rows, weight, arrived) = refs[:8], refs[8:]
    copies = []
    for at in range(8):
        columns = pl.ds(pl.multiple_of(which[at] * SHARD, 128), SHARD)
        other = pl.ds(pl.multiple_of(which[8 + at] * SHARD, 128), SHARD)
        to = slice(at * SHARD, (at + 1) * SHARD)
        copies.append(
            [
                pltpu.make_async_copy(pieces[at], weight.at[to, :], arrived.at[at, 0]),
                pltpu.make_async_copy(own_ref.at[:, columns], own_rows.at[:, to], arrived.at[at, 1]),
                pltpu.make_async_copy(other_ref.at[:, other], other_rows.at[:, to], arrived.at[at, 2]),
            ]
        )
    for copy in copies:
        for one in copy:
            one.start()
    for at in range(4):
        for copy in copies[2 * at : 2 * at + 2]:
            for one in copy:
                one.wait()
        to = slice(2 * at * SHARD, (2 * at + 2) * SHARD)
        for rows, out in ((own_rows, own_out), (other_rows, other_out)):
            part = jnp.dot(rows[:, to], weight[to, :], preferred_element_type=F32)
            if at == 0:
                out[...] = part
            else:
                out[...] += part


def project(hidden, other, which, pieces):
    cols = pieces[0].shape[1]
    out = jax.ShapeDtypeStruct((TOK, cols), F32)
    return pl.pallas_call(
        project_kernel,
        in_specs=[pl.BlockSpec(memory_space=pltpu.SMEM)] + [pl.BlockSpec(memory_space=pl.ANY)] * 10,
        out_specs=[pl.BlockSpec(memory_space=pltpu.VMEM)] * 2,
        out_shape=[out, out],
        scratch_shapes=[
            pltpu.VMEM((TOK, 8 * SHARD), BF16),
            pltpu.VMEM((TOK, 8 * SHARD), BF16),
            pltpu.VMEM((8 * SHARD, cols), BF16),
            pltpu.SemaphoreType.DMA((8, 3)),
        ],
        compiler_params=pltpu.CompilerParams(vmem_limit_bytes=VMEM_LIMIT),
        cost_estimate=pl.CostEstimate(
            flops=4 * TOK * 8 * SHARD * cols, bytes_accessed=12 * 2**20, transcendentals=0
        ),
    )(which, hidden, other, *pieces)


QUERY_STEP = 768


def query_kernel(hidden_ref, weight_ref, out_ref, total):
    step = pl.program_id(0)
    part = jnp.dot(hidden_ref[...], weight_ref[...], preferred_element_type=F32)

    @pl.when(step == 0)
    def _():
        total[...] = part

    @pl.when(step > 0)
    def _():
        total[...] += part

    @pl.when(step == pl.num_programs(0) - 1)
    def _():
        out_ref[...] = total[...].astype(BF16)


def project_queries(hidden, weight):
    cols = weight.shape[1]
    return pl.pallas_call(
        query_kernel,
        grid=(D // QUERY_STEP,),
        in_specs=[
            pl.BlockSpec((TOK, QUERY_STEP), lambda i: (0, i)),
            pl.BlockSpec((QUERY_STEP, cols), lambda i: (i, 0)),
        ],
        out_specs=pl.BlockSpec((TOK, cols), lambda i: (0, 0)),
        out_shape=jax.ShapeDtypeStruct((TOK, cols), BF16),
        scratch_shapes=[pltpu.VMEM((TOK, cols), F32)],
        compiler_params=pltpu.CompilerParams(vmem_limit_bytes=VMEM_LIMIT),
        cost_estimate=pl.CostEstimate(
            flops=2 * TOK * D * cols, bytes_accessed=16 * 2**20, transcendentals=0
        ),
    )(hidden, weight)


def attend_kernel(flags, first_ref, query_ref, *refs):
    pair_refs, refs = refs[:4], refs[4:]
    out_ref, query, keys, value, accum, best, largest, ready, arrived = refs
    side = flags[SPANS]
    heads = HEADS // 8
    loads = []
    for at in range(4):
        rows = pl.ds(pl.multiple_of(at * 128 + side * 64, 64), 64)
        to = query.at[at * 64 : at * 64 + 64, :FIRST]
        loads.append(pltpu.make_async_copy(first_ref.at[rows, :], to, ready.at[at, 0]))
        to = query.at[at * 64 : at * 64 + 64, FIRST:]
        loads.append(pltpu.make_async_copy(query_ref.at[rows, :], to, ready.at[at, 1]))
    pairs = []
    for ref in pair_refs:
        for at in range(SPANS // 4):
            block, rows = len(pairs), slice(at * TOK, (at + 1) * TOK)
            pairs.append(
                (
                    pltpu.make_async_copy(ref.at[rows, :HEAD], keys.at[block], arrived.at[block, 0]),
                    pltpu.make_async_copy(ref.at[rows, HEAD:], value.at[block, :, :HEAD], arrived.at[block, 1]),
                )
            )
    for load in loads:
        load.start()
    for key, mixed in pairs:
        key.start()
        mixed.start()
    value[:, :, HEAD:] = jnp.ones((SPANS, TOK, HEAD), BF16)
    accum[...] = jnp.zeros_like(accum)
    largest[...] = jnp.zeros_like(largest)
    for load in loads:
        load.wait()
    ones = jnp.ones((HEAD, HEAD), BF16)

    def squares(rows):
        sums = jnp.dot(rows * rows, ones, preferred_element_type=F32)
        return jnp.max(sums.reshape(rows.shape[0] // 8, 8, HEAD), axis=0)

    for head in range(heads):
        largest[0] = jnp.maximum(largest[0], squares(query[:, head * HEAD : (head + 1) * HEAD]))

    def step_small(block):
        key, extended = keys[block], value[block]
        largest[1] = jnp.maximum(largest[1], squares(key))
        for head in range(heads):
            scores = lax.dot_general(
                query[:, head * HEAD : (head + 1) * HEAD],
                key,
                (((1,), (1,)), ((), ())),
                preferred_element_type=F32,
            )
            probs = jnp.exp2(scores * SCALE2).astype(BF16)
            accum[head] += jnp.dot(probs, extended, preferred_element_type=F32)

    def step_any(block):
        def one(head, carry):
            scores = lax.dot_general(
                query[:, pl.ds(pl.multiple_of(head * HEAD, HEAD), HEAD)],
                keys[block],
                (((1,), (1,)), ((), ())),
                preferred_element_type=F32,
            )
            old = best[head]
            new = jnp.maximum(old, jnp.max(scores, axis=1, keepdims=True))
            best[head] = new
            probs = jnp.exp2((scores - new[:, :1]) * SCALE2).astype(BF16)
            factor = jnp.exp2((old - new) * SCALE2)
            accum[head] = accum[head] * factor[:, :1] + jnp.dot(
                probs, value[block], preferred_element_type=F32
            )
            return carry

        lax.fori_loop(0, heads, one, 0)

    def step(block, carry):
        for at, to in enumerate((keys.at[block], value.at[block, :, :HEAD])):
            pltpu.make_async_copy(pair_refs[0].at[:TOK, :HEAD], to, arrived.at[block, at]).wait()

        @pl.when(flags[block] > 0)
        def _():
            step_small(block)

        return carry

    lax.fori_loop(0, SPANS, step, 0)
    bound = jnp.max(largest[0]) * jnp.max(largest[1]) * (1.03 * SCALE2 * SCALE2)

    @pl.when(jnp.logical_not(bound <= SAFE_EXPONENT * SAFE_EXPONENT))
    def _():
        accum[...] = jnp.zeros_like(accum)
        best[...] = jnp.full_like(best, NEG_LARGE)

        def again(block, carry):
            @pl.when(flags[block] > 0)
            def _():
                step_any(block)

            return carry

        lax.fori_loop(0, SPANS, again, 0)

    for head in range(heads):
        mixed = accum[head]
        out_ref[:, head * HEAD : (head + 1) * HEAD] = (mixed[:, :HEAD] / mixed[:, HEAD:]).astype(BF16)


def attend(flags, queries, pairs):
    half, heads = TOK // 2, HEADS // 8
    return pl.pallas_call(
        attend_kernel,
        in_specs=[pl.BlockSpec(memory_space=pltpu.SMEM)] + [pl.BlockSpec(memory_space=pl.ANY)] * 6,
        out_specs=pl.BlockSpec(memory_space=pltpu.VMEM),
        out_shape=jax.ShapeDtypeStruct((half, 2 * GCOLS), BF16),
        scratch_shapes=[
            pltpu.VMEM((half, 2 * GCOLS), BF16),
            pltpu.VMEM((SPANS, TOK, HEAD), BF16),
            pltpu.VMEM((SPANS, TOK, 2 * HEAD), BF16),
            pltpu.VMEM((heads, half, 2 * HEAD), F32),
            pltpu.VMEM((heads, half, HEAD), F32),
            pltpu.VMEM((2, 8, HEAD), F32),
            pltpu.SemaphoreType.DMA((4, 2)),
            pltpu.SemaphoreType.DMA((SPANS, 2)),
        ],
        compiler_params=pltpu.CompilerParams(vmem_limit_bytes=VMEM_LIMIT),
        cost_estimate=pl.CostEstimate(
            flops=heads * 6 * half * SPANS * TOK * HEAD, bytes_accessed=6 * 2**20, transcendentals=0
        ),
    )(flags, *queries, *pairs)


OUT_GROUPS = 2
OUT_PARTS = 8 // OUT_GROUPS
OUT_COLS = D // OUT_GROUPS
Z_ORDER = (2, 1, 3, 0)


def output_kernel(group, place, mine_ref, got_ref, weight_ref, *refs):
    outs, (mine, got, rows_of, wide, result, loaded, arrived, stored) = refs[:4], refs[4:]
    z, side = place[0], place[1]
    loads = [
        pltpu.make_async_copy(mine_ref, mine, loaded.at[0]),
        pltpu.make_async_copy(got_ref, got, loaded.at[1]),
    ]
    copies = []
    for at in range(SPANS // OUT_GROUPS):
        for which, chosen in enumerate((side, 1 - side)):
            start = (chosen * SPANS + group * (SPANS // OUT_GROUPS) + at) * 2 * SHARD
            source = weight_ref.at[pl.ds(pl.multiple_of(start, 2 * SHARD), 2 * SHARD), :]
            to = wide.at[which * 2 * SHARD : (which + 1) * 2 * SHARD, at * SHARD : (at + 1) * SHARD]
            copies.append(pltpu.make_async_copy(source, to, arrived.at[at, which]))
    for copy in loads + copies[:8]:
        copy.start()
    for copy in loads:
        copy.wait()
    for at, step in enumerate(Z_ORDER):
        rows = pl.ds(pl.multiple_of(((z + step) % 4) * 64, 64), 64)
        rows_of[at * 64 : at * 64 + 64, : 2 * GCOLS] = mine[rows, :]
        rows_of[at * 64 : at * 64 + 64, 2 * GCOLS :] = got[rows, :]
    stores = []
    for part in range(OUT_PARTS):
        for copy in copies[part * 4 : part * 4 + 4]:
            copy.wait()
        for copy in copies[part * 4 + 8 : part * 4 + 12]:
            copy.start()
        columns = slice(part * 2 * SHARD, (part + 1) * 2 * SHARD)
        result[part] = jnp.dot(rows_of[...], wide[:, columns], preferred_element_type=F32).astype(BF16)
        for index, out in enumerate(outs):
            source = result.at[part, index * 64 : index * 64 + 64, :]
            stores.append(pltpu.make_async_copy(source, out.at[:, columns], stored.at[part, index]))
            stores[-1].start()
    for store in stores:
        store.wait()


def output_partial(group, place, mine, got, weights):
    anywhere = pl.BlockSpec(memory_space=pl.ANY)
    half = TOK // 2
    return pl.pallas_call(
        functools.partial(output_kernel, group),
        in_specs=[pl.BlockSpec(memory_space=pltpu.SMEM)] + [anywhere] * 3,
        out_specs=[anywhere] * 4,
        out_shape=[jax.ShapeDtypeStruct((64, OUT_COLS), BF16)] * 4,
        scratch_shapes=[
            pltpu.VMEM((half, 2 * GCOLS), BF16),
            pltpu.VMEM((half, 2 * GCOLS), BF16),
            pltpu.VMEM((half, 4 * GCOLS), BF16),
            pltpu.VMEM((4 * SHARD, OUT_COLS), BF16),
            pltpu.VMEM((OUT_PARTS, half, 2 * SHARD), BF16),
            pltpu.SemaphoreType.DMA((2,)),
            pltpu.SemaphoreType.DMA((SPANS // OUT_GROUPS, 2)),
            pltpu.SemaphoreType.DMA((OUT_PARTS, 4)),
        ],
        compiler_params=pltpu.CompilerParams(vmem_limit_bytes=VMEM_LIMIT),
        cost_estimate=pl.CostEstimate(
            flops=2 * TOK // 2 * OUT_COLS * 4 * GCOLS, bytes_accessed=6 * 2**20, transcendentals=0
        ),
    )(place, mine, got, weights)


def reduce_over_z(far, up, down, stay, sign):
    near, back = (up, down) if sign > 0 else (down, up)
    passed = move(far, dz=sign)
    behind = move(back, dz=-sign)
    near = (near.astype(F32) + passed.astype(F32)).astype(BF16)
    ahead = move(near, dz=sign)
    return (stay.astype(F32) + ahead.astype(F32) + behind.astype(F32)).astype(BF16)


def per_device(hidden, span_ids, w_query, w_keyval, w_out):
    span, uly = lax.axis_index("span"), lax.axis_index("uly")
    xl, y, core = span // 8, (span // 2) % 4, span % 2
    z, xh = uly // 2, uly % 2
    as_int = lambda values: jnp.stack([jnp.asarray(v, jnp.int32) for v in values])

    chips = [x * 4 + (y + dy) % 4 for dy in (0, 3, 1, 2) for x in (xl, 1 - xl)]
    which = as_int([j * 2 + core for j in chips] + chips)
    place = as_int([z, xh])
    block_ids = span_ids.reshape(SPANS, TOK)[:, 0]
    seen = (block_ids <= block_ids[span]).astype(jnp.int32)
    order = [chips[at] * 2 + core for at in (0, 1, 2, 4, 3, 5, 6, 7)]
    seen = seen[as_int(order + [at + 1 - 2 * core for at in order])]
    send_flags = jnp.concatenate([seen, as_int([1 - xh])])
    mine_flags = jnp.concatenate([seen, as_int([xh])])

    query_weight = lax.all_gather(w_query[:, FIRST:], "span", axis=0, tiled=True)

    own = jnp.concatenate([w_keyval[:, 0], w_keyval[:, 1], w_query[:, :FIRST]], axis=1)
    side = move(own, swap_xl=True)
    up, down = move(own, dy=1), move(own, dy=-1)
    elsewhere = after(as_int([j * 2 + 1 - core for j in range(8)]), own)
    picked = pick_columns(hidden, elsewhere)
    side, up, down, picked = lax.optimization_barrier((side, up, down, picked))
    other_hidden = move(picked, swap_c=True)
    side_up, side_down = move(side, dy=1), move(side, dy=-1)
    up, side_up, side_down, other_hidden, which, place, send_flags, mine_flags = lax.optimization_barrier(
        (up, side_up, side_down, other_hidden, which, place, send_flags, mine_flags)
    )
    far, side_far = move(up, dy=1), move(side_down, dy=-1)

    planes = [
        [index_of(span // 8, span // 2 % 4, span % 2, at, side) for side in range(2) for span in range(SPANS)]
        for at in range(4)
    ]
    weights = lax.all_gather(
        after(w_out, far, side_far), BOTH, axis=0, tiled=True, axis_index_groups=planes
    )
    pieces = [own, side, up, side_up, down, side_down, far, side_far]
    joint_own, joint_other = project(hidden, other_hidden, which, pieces)
    joint_other = move(joint_other, swap_c=True)
    pair = (joint_own[:, : 2 * HEAD] + joint_other[:, : 2 * HEAD]).astype(BF16)
    first_queries = (joint_own[:, 2 * HEAD :] + joint_other[:, 2 * HEAD :]).astype(BF16)

    pair_side = move(pair, swap_xl=True)
    pair_up, pair_down = move(pair, dy=1), move(pair, dy=-1)
    pair_side, pair_up, pair_down, query_weight, first_queries = lax.optimization_barrier(
        (pair_side, pair_up, pair_down, query_weight, first_queries)
    )
    pair_side_up, pair_side_down = move(pair_up, swap_xl=True), move(pair_down, swap_xl=True)
    pair_far = move(pair_down, dy=-1)
    pairs = jnp.concatenate([pair, pair_side, pair_up, pair_down], axis=0)
    other_pairs = move(pairs, swap_c=True)
    queries = project_queries(hidden, query_weight)
    pair_far, pair_side_up, pair_side_down, queries = lax.optimization_barrier(
        (pair_far, pair_side_up, pair_side_down, queries)
    )
    pair_side_far = move(pair_far, swap_xl=True)
    more_pairs = jnp.concatenate([pair_side_up, pair_side_down, pair_far, pair_side_far], axis=0)
    pairs = [pairs, more_pairs, other_pairs, move(more_pairs, swap_c=True)]

    send = attend(send_flags, [first_queries, queries], pairs)
    got = move(send, swap_xh=True)
    mine = attend(after(mine_flags, send), [first_queries, queries], pairs)

    totals = []
    for group in range(OUT_GROUPS):
        parts = output_partial(group, place, mine, got, weights)
        totals.append(reduce_over_z(*parts, 1 if group % 2 == 0 else -1))
    return jnp.concatenate(totals, axis=1)


def solution(mesh):
    in_specs = (P("span", None), P(), P("span", "uly"), P("span", None, "uly"), P("uly", "span"))
    out_specs = P(("span", "uly"), None)
    return jax.shard_map(
        per_device, mesh=mesh, in_specs=in_specs, out_specs=out_specs, check_vma=False
    )
```

```python
import functools
import math

import jax
import jax.numpy as jnp
from jax import lax
from jax.experimental import pallas as pl
from jax.experimental.pallas import tpu as pltpu
from jax.sharding import PartitionSpec as P

HEADS = 48
HEAD = 128
D = 6144
SPANS = 16
TOK = 512
SHARD = D // SPANS
GROUP = 3
GCOLS = GROUP * HEAD
FIRST = HEAD
SCALE2 = math.log2(math.e) / math.sqrt(HEAD)
SAFE_EXPONENT = 90.0
NEG_LARGE = -1e30
VMEM_LIMIT = 60 * 2**20
BOTH = ("span", "uly")
F32 = jnp.float32
BF16 = jnp.bfloat16


def coords(index):
    span, uly = index // 8, index % 8
    return span // 8, (span // 2) % 4, span % 2, uly // 2, uly % 2


def index_of(xl, y, c, z, xh):
    return (xl * 8 + y * 2 + c) * 8 + z * 2 + xh


def move(array, dx=0, dy=0, dz=0, swap_xl=False, swap_xh=False, swap_c=False):
    pairs = []
    for source in range(128):
        xl, y, c, z, xh = coords(source)
        x = (xh * 2 + xl + dx) % 4
        xh, xl = x // 2, x % 2
        if swap_xl:
            xl = 1 - xl
        if swap_xh:
            xh = 1 - xh
        if swap_c:
            c = 1 - c
        pairs.append((source, index_of(xl, (y + dy) % 4, c, (z + dz) % 4, xh)))
    return lax.ppermute(array, BOTH, pairs)


def after(array, *results):
    return lax.optimization_barrier((array, *results))[0]


def pick_kernel(which, hidden_ref, out_ref, arrived):
    copies = []
    for at in range(8):
        columns = pl.ds(pl.multiple_of(which[at] * SHARD, 128), SHARD)
        to = out_ref.at[:, at * SHARD : (at + 1) * SHARD]
        copies.append(pltpu.make_async_copy(hidden_ref.at[:, columns], to, arrived.at[at]))
    for copy in copies:
        copy.start()
    for copy in copies:
        copy.wait()


def pick_columns(hidden, which):
    return pl.pallas_call(
        pick_kernel,
        in_specs=[pl.BlockSpec(memory_space=pltpu.SMEM), pl.BlockSpec(memory_space=pl.ANY)],
        out_specs=pl.BlockSpec(memory_space=pltpu.VMEM),
        out_shape=jax.ShapeDtypeStruct((TOK, 8 * SHARD), BF16),
        scratch_shapes=[pltpu.SemaphoreType.DMA((8,))],
        compiler_params=pltpu.CompilerParams(vmem_limit_bytes=VMEM_LIMIT),
        cost_estimate=pl.CostEstimate(flops=0, bytes_accessed=4 * TOK * 8 * SHARD, transcendentals=0),
    )(which, hidden)


def project_kernel(which, own_ref, other_ref, *refs):
    pieces, (own_out, other_out, own_rows, other_rows, weight, arrived) = refs[:8], refs[8:]
    copies = []
    for at in range(8):
        columns = pl.ds(pl.multiple_of(which[at] * SHARD, 128), SHARD)
        other = pl.ds(pl.multiple_of(which[8 + at] * SHARD, 128), SHARD)
        to = slice(at * SHARD, (at + 1) * SHARD)
        copies.append(
            [
                pltpu.make_async_copy(pieces[at], weight.at[to, :], arrived.at[at, 0]),
                pltpu.make_async_copy(own_ref.at[:, columns], own_rows.at[:, to], arrived.at[at, 1]),
                pltpu.make_async_copy(other_ref.at[:, other], other_rows.at[:, to], arrived.at[at, 2]),
            ]
        )
    for copy in copies:
        for one in copy:
            one.start()
    for at in range(4):
        for copy in copies[2 * at : 2 * at + 2]:
            for one in copy:
                one.wait()
        to = slice(2 * at * SHARD, (2 * at + 2) * SHARD)
        for rows, out in ((own_rows, own_out), (other_rows, other_out)):
            part = jnp.dot(rows[:, to], weight[to, :], preferred_element_type=F32)
            if at == 0:
                out[...] = part
            else:
                out[...] += part


def project(hidden, other, which, pieces):
    cols = pieces[0].shape[1]
    out = jax.ShapeDtypeStruct((TOK, cols), F32)
    return pl.pallas_call(
        project_kernel,
        in_specs=[pl.BlockSpec(memory_space=pltpu.SMEM)] + [pl.BlockSpec(memory_space=pl.ANY)] * 10,
        out_specs=[pl.BlockSpec(memory_space=pltpu.VMEM)] * 2,
        out_shape=[out, out],
        scratch_shapes=[
            pltpu.VMEM((TOK, 8 * SHARD), BF16),
            pltpu.VMEM((TOK, 8 * SHARD), BF16),
            pltpu.VMEM((8 * SHARD, cols), BF16),
            pltpu.SemaphoreType.DMA((8, 3)),
        ],
        compiler_params=pltpu.CompilerParams(vmem_limit_bytes=VMEM_LIMIT),
        cost_estimate=pl.CostEstimate(
            flops=4 * TOK * 8 * SHARD * cols, bytes_accessed=12 * 2**20, transcendentals=0
        ),
    )(which, hidden, other, *pieces)


QUERY_STEP = 768


def query_kernel(hidden_ref, weight_ref, out_ref, total):
    step = pl.program_id(0)
    part = jnp.dot(hidden_ref[...], weight_ref[...], preferred_element_type=F32)

    @pl.when(step == 0)
    def _():
        total[...] = part

    @pl.when(step > 0)
    def _():
        total[...] += part

    @pl.when(step == pl.num_programs(0) - 1)
    def _():
        out_ref[...] = total[...].astype(BF16)


def project_queries(hidden, weight):
    cols = weight.shape[1]
    return pl.pallas_call(
        query_kernel,
        grid=(D // QUERY_STEP,),
        in_specs=[
            pl.BlockSpec((TOK, QUERY_STEP), lambda i: (0, i)),
            pl.BlockSpec((QUERY_STEP, cols), lambda i: (i, 0)),
        ],
        out_specs=pl.BlockSpec((TOK, cols), lambda i: (0, 0)),
        out_shape=jax.ShapeDtypeStruct((TOK, cols), BF16),
        scratch_shapes=[pltpu.VMEM((TOK, cols), F32)],
        compiler_params=pltpu.CompilerParams(vmem_limit_bytes=VMEM_LIMIT),
        cost_estimate=pl.CostEstimate(
            flops=2 * TOK * D * cols, bytes_accessed=16 * 2**20, transcendentals=0
        ),
    )(hidden, weight)


def attend_kernel(flags, first_ref, query_ref, *refs):
    pair_refs, refs = refs[:4], refs[4:]
    out_ref, query, keys, value, accum, best, largest, ready, arrived = refs
    side = flags[SPANS]
    heads = HEADS // 8
    loads = []
    for at in range(4):
        rows = pl.ds(pl.multiple_of(at * 128 + side * 64, 64), 64)
        to = query.at[at * 64 : at * 64 + 64, :FIRST]
        loads.append(pltpu.make_async_copy(first_ref.at[rows, :], to, ready.at[at, 0]))
        to = query.at[at * 64 : at * 64 + 64, FIRST:]
        loads.append(pltpu.make_async_copy(query_ref.at[rows, :], to, ready.at[at, 1]))
    pairs = []
    for ref in pair_refs:
        for at in range(SPANS // 4):
            block, rows = len(pairs), slice(at * TOK, (at + 1) * TOK)
            pairs.append(
                (
                    pltpu.make_async_copy(ref.at[rows, :HEAD], keys.at[block], arrived.at[block, 0]),
                    pltpu.make_async_copy(ref.at[rows, HEAD:], value.at[block, :, :HEAD], arrived.at[block, 1]),
                )
            )
    for load in loads:
        load.start()
    for key, mixed in pairs:
        key.start()
        mixed.start()
    value[:, :, HEAD:] = jnp.ones((SPANS, TOK, HEAD), BF16)
    accum[...] = jnp.zeros_like(accum)
    largest[...] = jnp.zeros_like(largest)
    for load in loads:
        load.wait()
    ones = jnp.ones((HEAD, HEAD), BF16)

    def squares(rows):
        sums = jnp.dot(rows * rows, ones, preferred_element_type=F32)
        return jnp.max(sums.reshape(rows.shape[0] // 8, 8, HEAD), axis=0)

    for head in range(heads):
        largest[0] = jnp.maximum(largest[0], squares(query[:, head * HEAD : (head + 1) * HEAD]))

    def step_small(block):
        key, extended = keys[block], value[block]
        largest[1] = jnp.maximum(largest[1], squares(key))
        for head in range(heads):
            scores = lax.dot_general(
                query[:, head * HEAD : (head + 1) * HEAD],
                key,
                (((1,), (1,)), ((), ())),
                preferred_element_type=F32,
            )
            probs = jnp.exp2(scores * SCALE2).astype(BF16)
            accum[head] += jnp.dot(probs, extended, preferred_element_type=F32)

    def step_any(block):
        def one(head, carry):
            scores = lax.dot_general(
                query[:, pl.ds(pl.multiple_of(head * HEAD, HEAD), HEAD)],
                keys[block],
                (((1,), (1,)), ((), ())),
                preferred_element_type=F32,
            )
            old = best[head]
            new = jnp.maximum(old, jnp.max(scores, axis=1, keepdims=True))
            best[head] = new
            probs = jnp.exp2((scores - new[:, :1]) * SCALE2).astype(BF16)
            factor = jnp.exp2((old - new) * SCALE2)
            accum[head] = accum[head] * factor[:, :1] + jnp.dot(
                probs, value[block], preferred_element_type=F32
            )
            return carry

        lax.fori_loop(0, heads, one, 0)

    def step(block, carry):
        for at, to in enumerate((keys.at[block], value.at[block, :, :HEAD])):
            pltpu.make_async_copy(pair_refs[0].at[:TOK, :HEAD], to, arrived.at[block, at]).wait()

        @pl.when(flags[block] > 0)
        def _():
            step_small(block)

        return carry

    lax.fori_loop(0, SPANS, step, 0)
    bound = jnp.max(largest[0]) * jnp.max(largest[1]) * (1.03 * SCALE2 * SCALE2)

    @pl.when(jnp.logical_not(bound <= SAFE_EXPONENT * SAFE_EXPONENT))
    def _():
        accum[...] = jnp.zeros_like(accum)
        best[...] = jnp.full_like(best, NEG_LARGE)

        def again(block, carry):
            @pl.when(flags[block] > 0)
            def _():
                step_any(block)

            return carry

        lax.fori_loop(0, SPANS, again, 0)

    for head in range(heads):
        mixed = accum[head]
        out_ref[:, head * HEAD : (head + 1) * HEAD] = (mixed[:, :HEAD] / mixed[:, HEAD:]).astype(BF16)


def attend(flags, queries, pairs):
    half, heads = TOK // 2, HEADS // 8
    return pl.pallas_call(
        attend_kernel,
        in_specs=[pl.BlockSpec(memory_space=pltpu.SMEM)] + [pl.BlockSpec(memory_space=pl.ANY)] * 6,
        out_specs=pl.BlockSpec(memory_space=pltpu.VMEM),
        out_shape=jax.ShapeDtypeStruct((half, 2 * GCOLS), BF16),
        scratch_shapes=[
            pltpu.VMEM((half, 2 * GCOLS), BF16),
            pltpu.VMEM((SPANS, TOK, HEAD), BF16),
            pltpu.VMEM((SPANS, TOK, 2 * HEAD), BF16),
            pltpu.VMEM((heads, half, 2 * HEAD), F32),
            pltpu.VMEM((heads, half, HEAD), F32),
            pltpu.VMEM((2, 8, HEAD), F32),
            pltpu.SemaphoreType.DMA((4, 2)),
            pltpu.SemaphoreType.DMA((SPANS, 2)),
        ],
        compiler_params=pltpu.CompilerParams(vmem_limit_bytes=VMEM_LIMIT),
        cost_estimate=pl.CostEstimate(
            flops=heads * 6 * half * SPANS * TOK * HEAD, bytes_accessed=6 * 2**20, transcendentals=0
        ),
    )(flags, *queries, *pairs)


OUT_GROUPS = 2
OUT_PARTS = 8 // OUT_GROUPS
OUT_COLS = D // OUT_GROUPS
Z_ORDER = (2, 1, 3, 0)


def output_kernel(group, place, mine_ref, got_ref, weight_ref, *refs):
    outs, (mine, got, rows_of, wide, result, loaded, arrived, stored) = refs[:4], refs[4:]
    z, side = place[0], place[1]
    loads = [
        pltpu.make_async_copy(mine_ref, mine, loaded.at[0]),
        pltpu.make_async_copy(got_ref, got, loaded.at[1]),
    ]
    copies = []
    for at in range(SPANS // OUT_GROUPS):
        for which, chosen in enumerate((side, 1 - side)):
            start = (chosen * SPANS + group * (SPANS // OUT_GROUPS) + at) * 2 * SHARD
            source = weight_ref.at[pl.ds(pl.multiple_of(start, 2 * SHARD), 2 * SHARD), :]
            to = wide.at[which * 2 * SHARD : (which + 1) * 2 * SHARD, at * SHARD : (at + 1) * SHARD]
            copies.append(pltpu.make_async_copy(source, to, arrived.at[at, which]))
    for copy in loads + copies:
        copy.start()
    for copy in loads:
        copy.wait()
    for at, step in enumerate(Z_ORDER):
        rows = pl.ds(pl.multiple_of(((z + step) % 4) * 64, 64), 64)
        rows_of[at * 64 : at * 64 + 64, : 2 * GCOLS] = mine[rows, :]
        rows_of[at * 64 : at * 64 + 64, 2 * GCOLS :] = got[rows, :]
    stores = []
    for part in range(OUT_PARTS):
        for copy in copies[part * 4 : part * 4 + 4]:
            copy.wait()
        columns = slice(part * 2 * SHARD, (part + 1) * 2 * SHARD)
        result[part] = jnp.dot(rows_of[...], wide[:, columns], preferred_element_type=F32).astype(BF16)
        for index, out in enumerate(outs):
            source = result.at[part, index * 64 : index * 64 + 64, :]
            stores.append(pltpu.make_async_copy(source, out.at[:, columns], stored.at[part, index]))
            stores[-1].start()
    for store in stores:
        store.wait()


def output_partial(group, place, mine, got, weights):
    anywhere = pl.BlockSpec(memory_space=pl.ANY)
    half = TOK // 2
    return pl.pallas_call(
        functools.partial(output_kernel, group),
        in_specs=[pl.BlockSpec(memory_space=pltpu.SMEM)] + [anywhere] * 3,
        out_specs=[anywhere] * 4,
        out_shape=[jax.ShapeDtypeStruct((64, OUT_COLS), BF16)] * 4,
        scratch_shapes=[
            pltpu.VMEM((half, 2 * GCOLS), BF16),
            pltpu.VMEM((half, 2 * GCOLS), BF16),
            pltpu.VMEM((half, 4 * GCOLS), BF16),
            pltpu.VMEM((4 * SHARD, OUT_COLS), BF16),
            pltpu.VMEM((OUT_PARTS, half, 2 * SHARD), BF16),
            pltpu.SemaphoreType.DMA((2,)),
            pltpu.SemaphoreType.DMA((SPANS // OUT_GROUPS, 2)),
            pltpu.SemaphoreType.DMA((OUT_PARTS, 4)),
        ],
        compiler_params=pltpu.CompilerParams(vmem_limit_bytes=VMEM_LIMIT),
        cost_estimate=pl.CostEstimate(
            flops=2 * TOK // 2 * OUT_COLS * 4 * GCOLS, bytes_accessed=6 * 2**20, transcendentals=0
        ),
    )(place, mine, got, weights)


def reduce_over_z(far, up, down, stay, sign):
    near, back = (up, down) if sign > 0 else (down, up)
    passed = move(far, dz=sign)
    behind = move(back, dz=-sign)
    near = (near.astype(F32) + passed.astype(F32)).astype(BF16)
    ahead = move(near, dz=sign)
    return (stay.astype(F32) + ahead.astype(F32) + behind.astype(F32)).astype(BF16)


def per_device(hidden, span_ids, w_query, w_keyval, w_out):
    span, uly = lax.axis_index("span"), lax.axis_index("uly")
    xl, y, core = span // 8, (span // 2) % 4, span % 2
    z, xh = uly // 2, uly % 2
    as_int = lambda values: jnp.stack([jnp.asarray(v, jnp.int32) for v in values])

    chips = [x * 4 + (y + dy) % 4 for dy in (0, 3, 1, 2) for x in (xl, 1 - xl)]
    which = as_int([j * 2 + core for j in chips] + chips)
    place = as_int([z, xh])
    block_ids = span_ids.reshape(SPANS, TOK)[:, 0]
    seen = (block_ids <= block_ids[span]).astype(jnp.int32)
    order = [chips[at] * 2 + core for at in (0, 1, 2, 4, 3, 5, 6, 7)]
    seen = seen[as_int(order + [at + 1 - 2 * core for at in order])]
    send_flags = jnp.concatenate([seen, as_int([1 - xh])])
    mine_flags = jnp.concatenate([seen, as_int([xh])])

    query_weight = lax.all_gather(w_query[:, FIRST:], "span", axis=0, tiled=True)

    own = jnp.concatenate([w_keyval[:, 0], w_keyval[:, 1], w_query[:, :FIRST]], axis=1)
    side = move(own, swap_xl=True)
    up, down = move(own, dy=1), move(own, dy=-1)
    elsewhere = after(as_int([j * 2 + 1 - core for j in range(8)]), own)
    picked = pick_columns(hidden, elsewhere)
    side, up, down, picked = lax.optimization_barrier((side, up, down, picked))
    other_hidden = move(picked, swap_c=True)
    side_up, side_down = move(side, dy=1), move(side, dy=-1)
    up, side_up, side_down, other_hidden, which, place, send_flags, mine_flags = lax.optimization_barrier(
        (up, side_up, side_down, other_hidden, which, place, send_flags, mine_flags)
    )
    far, side_far = move(up, dy=1), move(side_down, dy=-1)

    planes = [
        [index_of(span // 8, span // 2 % 4, span % 2, at, side) for side in range(2) for span in range(SPANS)]
        for at in range(4)
    ]
    weights = lax.all_gather(
        after(w_out, far, side_far), BOTH, axis=0, tiled=True, axis_index_groups=planes
    )
    pieces = [own, side, up, side_up, down, side_down, far, side_far]
    joint_own, joint_other = project(hidden, other_hidden, which, pieces)
    joint_other = move(joint_other, swap_c=True)
    pair = (joint_own[:, : 2 * HEAD] + joint_other[:, : 2 * HEAD]).astype(BF16)
    first_queries = (joint_own[:, 2 * HEAD :] + joint_other[:, 2 * HEAD :]).astype(BF16)

    pair_side = move(pair, swap_xl=True)
    pair_up, pair_down = move(pair, dy=1), move(pair, dy=-1)
    pair_side, pair_up, pair_down, query_weight, first_queries = lax.optimization_barrier(
        (pair_side, pair_up, pair_down, query_weight, first_queries)
    )
    pair_side_up, pair_side_down = move(pair_up, swap_xl=True), move(pair_down, swap_xl=True)
    pair_far = move(pair_down, dy=-1)
    pairs = jnp.concatenate([pair, pair_side, pair_up, pair_down], axis=0)
    other_pairs = move(pairs, swap_c=True)
    queries = project_queries(hidden, query_weight)
    pair_far, pair_side_up, pair_side_down, queries = lax.optimization_barrier(
        (pair_far, pair_side_up, pair_side_down, queries)
    )
    pair_side_far = move(pair_far, swap_xl=True)
    more_pairs = jnp.concatenate([pair_side_up, pair_side_down, pair_far, pair_side_far], axis=0)
    pairs = [pairs, more_pairs, other_pairs, move(more_pairs, swap_c=True)]

    send = attend(send_flags, [first_queries, queries], pairs)
    got = move(send, swap_xh=True)
    mine = attend(after(mine_flags, send), [first_queries, queries], pairs)

    totals = []
    for group in range(OUT_GROUPS):
        parts = output_partial(group, place, mine, got, weights)
        totals.append(reduce_over_z(*parts, 1 if group % 2 == 0 else -1))
    return jnp.concatenate(totals, axis=1)


def solution(mesh):
    in_specs = (P("span", None), P(), P("span", "uly"), P("span", None, "uly"), P("uly", "span"))
    out_specs = P(("span", "uly"), None)
    return jax.shard_map(
        per_device, mesh=mesh, in_specs=in_specs, out_specs=out_specs, check_vma=False
    )
```

```python
import functools
import math

import jax
import jax.numpy as jnp
from jax import lax
from jax.experimental import pallas as pl
from jax.experimental.pallas import tpu as pltpu
from jax.sharding import PartitionSpec as P

HEADS = 48
HEAD = 128
D = 6144
SPANS = 16
TOK = 512
SHARD = D // SPANS
GROUP = 3
GCOLS = GROUP * HEAD
FIRST = HEAD
SCALE2 = math.log2(math.e) / math.sqrt(HEAD)
SAFE_EXPONENT = 90.0
NEG_LARGE = -1e30
VMEM_LIMIT = 60 * 2**20
BOTH = ("span", "uly")
F32 = jnp.float32
BF16 = jnp.bfloat16


def coords(index):
    span, uly = index // 8, index % 8
    return span // 8, (span // 2) % 4, span % 2, uly // 2, uly % 2


def index_of(xl, y, c, z, xh):
    return (xl * 8 + y * 2 + c) * 8 + z * 2 + xh


def move(array, dx=0, dy=0, dz=0, swap_xl=False, swap_xh=False, swap_c=False):
    pairs = []
    for source in range(128):
        xl, y, c, z, xh = coords(source)
        x = (xh * 2 + xl + dx) % 4
        xh, xl = x // 2, x % 2
        if swap_xl:
            xl = 1 - xl
        if swap_xh:
            xh = 1 - xh
        if swap_c:
            c = 1 - c
        pairs.append((source, index_of(xl, (y + dy) % 4, c, (z + dz) % 4, xh)))
    return lax.ppermute(array, BOTH, pairs)


def after(array, *results):
    return lax.optimization_barrier((array, *results))[0]


def pick_kernel(which, hidden_ref, out_ref, arrived):
    copies = []
    for at in range(8):
        columns = pl.ds(pl.multiple_of(which[at] * SHARD, 128), SHARD)
        to = out_ref.at[:, at * SHARD : (at + 1) * SHARD]
        copies.append(pltpu.make_async_copy(hidden_ref.at[:, columns], to, arrived.at[at]))
    for copy in copies:
        copy.start()
    for copy in copies:
        copy.wait()


def pick_columns(hidden, which):
    return pl.pallas_call(
        pick_kernel,
        in_specs=[pl.BlockSpec(memory_space=pltpu.SMEM), pl.BlockSpec(memory_space=pl.ANY)],
        out_specs=pl.BlockSpec(memory_space=pltpu.VMEM),
        out_shape=jax.ShapeDtypeStruct((TOK, 8 * SHARD), BF16),
        scratch_shapes=[pltpu.SemaphoreType.DMA((8,))],
        compiler_params=pltpu.CompilerParams(vmem_limit_bytes=VMEM_LIMIT),
        cost_estimate=pl.CostEstimate(flops=0, bytes_accessed=4 * TOK * 8 * SHARD, transcendentals=0),
    )(which, hidden)


def project_kernel(which, own_ref, other_ref, *refs):
    pieces, (own_out, other_out, own_rows, other_rows, weight, arrived) = refs[:8], refs[8:]
    copies = []
    for at in range(8):
        columns = pl.ds(pl.multiple_of(which[at] * SHARD, 128), SHARD)
        other = pl.ds(pl.multiple_of(which[8 + at] * SHARD, 128), SHARD)
        to = slice(at * SHARD, (at + 1) * SHARD)
        copies.append(
            [
                pltpu.make_async_copy(pieces[at], weight.at[to, :], arrived.at[at, 0]),
                pltpu.make_async_copy(own_ref.at[:, columns], own_rows.at[:, to], arrived.at[at, 1]),
                pltpu.make_async_copy(other_ref.at[:, other], other_rows.at[:, to], arrived.at[at, 2]),
            ]
        )
    for copy in copies:
        for one in copy:
            one.start()
    for at in range(4):
        for copy in copies[2 * at : 2 * at + 2]:
            for one in copy:
                one.wait()
        to = slice(2 * at * SHARD, (2 * at + 2) * SHARD)
        for rows, out in ((own_rows, own_out), (other_rows, other_out)):
            part = jnp.dot(rows[:, to], weight[to, :], preferred_element_type=F32)
            if at == 0:
                out[...] = part
            else:
                out[...] += part


def project(hidden, other, which, pieces):
    cols = pieces[0].shape[1]
    out = jax.ShapeDtypeStruct((TOK, cols), F32)
    return pl.pallas_call(
        project_kernel,
        in_specs=[pl.BlockSpec(memory_space=pltpu.SMEM)] + [pl.BlockSpec(memory_space=pl.ANY)] * 10,
        out_specs=[pl.BlockSpec(memory_space=pltpu.VMEM)] * 2,
        out_shape=[out, out],
        scratch_shapes=[
            pltpu.VMEM((TOK, 8 * SHARD), BF16),
            pltpu.VMEM((TOK, 8 * SHARD), BF16),
            pltpu.VMEM((8 * SHARD, cols), BF16),
            pltpu.SemaphoreType.DMA((8, 3)),
        ],
        compiler_params=pltpu.CompilerParams(vmem_limit_bytes=VMEM_LIMIT),
        cost_estimate=pl.CostEstimate(
            flops=4 * TOK * 8 * SHARD * cols, bytes_accessed=12 * 2**20, transcendentals=0
        ),
    )(which, hidden, other, *pieces)


QUERY_STEP = 768


def query_kernel(hidden_ref, weight_ref, out_ref, total):
    step = pl.program_id(0)
    part = jnp.dot(hidden_ref[...], weight_ref[...], preferred_element_type=F32)

    @pl.when(step == 0)
    def _():
        total[...] = part

    @pl.when(step > 0)
    def _():
        total[...] += part

    @pl.when(step == pl.num_programs(0) - 1)
    def _():
        out_ref[...] = total[...].astype(BF16)


def project_queries(hidden, weight):
    cols = weight.shape[1]
    return pl.pallas_call(
        query_kernel,
        grid=(D // QUERY_STEP,),
        in_specs=[
            pl.BlockSpec((TOK, QUERY_STEP), lambda i: (0, i)),
            pl.BlockSpec((QUERY_STEP, cols), lambda i: (i, 0)),
        ],
        out_specs=pl.BlockSpec((TOK, cols), lambda i: (0, 0)),
        out_shape=jax.ShapeDtypeStruct((TOK, cols), BF16),
        scratch_shapes=[pltpu.VMEM((TOK, cols), F32)],
        compiler_params=pltpu.CompilerParams(vmem_limit_bytes=VMEM_LIMIT),
        cost_estimate=pl.CostEstimate(
            flops=2 * TOK * D * cols, bytes_accessed=16 * 2**20, transcendentals=0
        ),
    )(hidden, weight)


def attend_kernel(flags, first_ref, query_ref, *refs):
    pair_refs, refs = refs[:4], refs[4:]
    out_ref, query, keys, value, accum, best, largest, ready, arrived = refs
    side = flags[SPANS]
    heads = HEADS // 8
    loads = []
    for at in range(4):
        rows = pl.ds(pl.multiple_of(at * 128 + side * 64, 64), 64)
        to = query.at[at * 64 : at * 64 + 64, :FIRST]
        loads.append(pltpu.make_async_copy(first_ref.at[rows, :], to, ready.at[at, 0]))
        to = query.at[at * 64 : at * 64 + 64, FIRST:]
        loads.append(pltpu.make_async_copy(query_ref.at[rows, :], to, ready.at[at, 1]))
    pairs = []
    for ref in pair_refs:
        for at in range(SPANS // 4):
            block, rows = len(pairs), slice(at * TOK, (at + 1) * TOK)
            pairs.append(
                (
                    pltpu.make_async_copy(ref.at[rows, :HEAD], keys.at[block], arrived.at[block, 0]),
                    pltpu.make_async_copy(ref.at[rows, HEAD:], value.at[block, :, :HEAD], arrived.at[block, 1]),
                )
            )
    for load in loads:
        load.start()
    for key, mixed in pairs:
        key.start()
        mixed.start()
    value[:, :, HEAD:] = jnp.ones((SPANS, TOK, HEAD), BF16)
    accum[...] = jnp.zeros_like(accum)
    largest[...] = jnp.zeros_like(largest)
    for load in loads:
        load.wait()
    ones = jnp.ones((HEAD, HEAD), BF16)

    def squares(rows):
        sums = jnp.dot(rows * rows, ones, preferred_element_type=F32)
        return jnp.max(sums.reshape(rows.shape[0] // 8, 8, HEAD), axis=0)

    for head in range(heads):
        largest[0] = jnp.maximum(largest[0], squares(query[:, head * HEAD : (head + 1) * HEAD]))

    def step_small(block):
        key, extended = keys[block], value[block]
        largest[1] = jnp.maximum(largest[1], squares(key))
        for head in range(heads):
            scores = lax.dot_general(
                query[:, head * HEAD : (head + 1) * HEAD],
                key,
                (((1,), (1,)), ((), ())),
                preferred_element_type=F32,
            )
            probs = jnp.exp2(scores * SCALE2).astype(BF16)
            accum[head] += jnp.dot(probs, extended, preferred_element_type=F32)

    def step_any(block):
        def one(head, carry):
            scores = lax.dot_general(
                query[:, pl.ds(pl.multiple_of(head * HEAD, HEAD), HEAD)],
                keys[block],
                (((1,), (1,)), ((), ())),
                preferred_element_type=F32,
            )
            old = best[head]
            new = jnp.maximum(old, jnp.max(scores, axis=1, keepdims=True))
            best[head] = new
            probs = jnp.exp2((scores - new[:, :1]) * SCALE2).astype(BF16)
            factor = jnp.exp2((old - new) * SCALE2)
            accum[head] = accum[head] * factor[:, :1] + jnp.dot(
                probs, value[block], preferred_element_type=F32
            )
            return carry

        lax.fori_loop(0, heads, one, 0)

    def step(block, carry):
        for at, to in enumerate((keys.at[block], value.at[block, :, :HEAD])):
            pltpu.make_async_copy(pair_refs[0].at[:TOK, :HEAD], to, arrived.at[block, at]).wait()

        @pl.when(flags[block] > 0)
        def _():
            step_small(block)

        return carry

    lax.fori_loop(0, SPANS, step, 0)
    bound = jnp.max(largest[0]) * jnp.max(largest[1]) * (1.03 * SCALE2 * SCALE2)

    @pl.when(jnp.logical_not(bound <= SAFE_EXPONENT * SAFE_EXPONENT))
    def _():
        accum[...] = jnp.zeros_like(accum)
        best[...] = jnp.full_like(best, NEG_LARGE)

        def again(block, carry):
            @pl.when(flags[block] > 0)
            def _():
                step_any(block)

            return carry

        lax.fori_loop(0, SPANS, again, 0)

    for head in range(heads):
        mixed = accum[head]
        out_ref[:, head * HEAD : (head + 1) * HEAD] = (mixed[:, :HEAD] / mixed[:, HEAD:]).astype(BF16)


def attend(flags, queries, pairs):
    half, heads = TOK // 2, HEADS // 8
    return pl.pallas_call(
        attend_kernel,
        in_specs=[pl.BlockSpec(memory_space=pltpu.SMEM)] + [pl.BlockSpec(memory_space=pl.ANY)] * 6,
        out_specs=pl.BlockSpec(memory_space=pltpu.VMEM),
        out_shape=jax.ShapeDtypeStruct((half, 2 * GCOLS), BF16),
        scratch_shapes=[
            pltpu.VMEM((half, 2 * GCOLS), BF16),
            pltpu.VMEM((SPANS, TOK, HEAD), BF16),
            pltpu.VMEM((SPANS, TOK, 2 * HEAD), BF16),
            pltpu.VMEM((heads, half, 2 * HEAD), F32),
            pltpu.VMEM((heads, half, HEAD), F32),
            pltpu.VMEM((2, 8, HEAD), F32),
            pltpu.SemaphoreType.DMA((4, 2)),
            pltpu.SemaphoreType.DMA((SPANS, 2)),
        ],
        compiler_params=pltpu.CompilerParams(vmem_limit_bytes=VMEM_LIMIT),
        cost_estimate=pl.CostEstimate(
            flops=heads * 6 * half * SPANS * TOK * HEAD, bytes_accessed=6 * 2**20, transcendentals=0
        ),
    )(flags, *queries, *pairs)


OUT_GROUPS = 2
OUT_PARTS = 8 // OUT_GROUPS
OUT_COLS = D // OUT_GROUPS
Z_ORDER = (2, 1, 3, 0)


def output_kernel(group, place, mine_ref, got_ref, weight_ref, *refs):
    outs, (mine, got, rows_of, wide, result, loaded, arrived, stored) = refs[:4], refs[4:]
    z, side = place[0], place[1]
    loads = [
        pltpu.make_async_copy(mine_ref, mine, loaded.at[0]),
        pltpu.make_async_copy(got_ref, got, loaded.at[1]),
    ]
    copies = []
    for at in range(SPANS // OUT_GROUPS):
        for which, chosen in enumerate((side, 1 - side)):
            start = (chosen * SPANS + group * (SPANS // OUT_GROUPS) + at) * 2 * SHARD
            source = weight_ref.at[pl.ds(pl.multiple_of(start, 2 * SHARD), 2 * SHARD), :]
            to = wide.at[which * 2 * SHARD : (which + 1) * 2 * SHARD, at * SHARD : (at + 1) * SHARD]
            copies.append(pltpu.make_async_copy(source, to, arrived.at[at, which]))
    for copy in loads + copies[:4]:
        copy.start()
    for copy in loads:
        copy.wait()
    for at, step in enumerate(Z_ORDER):
        rows = pl.ds(pl.multiple_of(((z + step) % 4) * 64, 64), 64)
        rows_of[at * 64 : at * 64 + 64, : 2 * GCOLS] = mine[rows, :]
        rows_of[at * 64 : at * 64 + 64, 2 * GCOLS :] = got[rows, :]
    stores = []
    for part in range(OUT_PARTS):
        for copy in copies[part * 4 : part * 4 + 4]:
            copy.wait()
        for copy in copies[4:12] if part == 0 else copies[part * 4 + 8 : part * 4 + 12]:
            copy.start()
        columns = slice(part * 2 * SHARD, (part + 1) * 2 * SHARD)
        result[part] = jnp.dot(rows_of[...], wide[:, columns], preferred_element_type=F32).astype(BF16)
        for index, out in enumerate(outs):
            source = result.at[part, index * 64 : index * 64 + 64, :]
            stores.append(pltpu.make_async_copy(source, out.at[:, columns], stored.at[part, index]))
            stores[-1].start()
    for store in stores:
        store.wait()


def output_partial(group, place, mine, got, weights):
    anywhere = pl.BlockSpec(memory_space=pl.ANY)
    half = TOK // 2
    return pl.pallas_call(
        functools.partial(output_kernel, group),
        in_specs=[pl.BlockSpec(memory_space=pltpu.SMEM)] + [anywhere] * 3,
        out_specs=[anywhere] * 4,
        out_shape=[jax.ShapeDtypeStruct((64, OUT_COLS), BF16)] * 4,
        scratch_shapes=[
            pltpu.VMEM((half, 2 * GCOLS), BF16),
            pltpu.VMEM((half, 2 * GCOLS), BF16),
            pltpu.VMEM((half, 4 * GCOLS), BF16),
            pltpu.VMEM((4 * SHARD, OUT_COLS), BF16),
            pltpu.VMEM((OUT_PARTS, half, 2 * SHARD), BF16),
            pltpu.SemaphoreType.DMA((2,)),
            pltpu.SemaphoreType.DMA((SPANS // OUT_GROUPS, 2)),
            pltpu.SemaphoreType.DMA((OUT_PARTS, 4)),
        ],
        compiler_params=pltpu.CompilerParams(vmem_limit_bytes=VMEM_LIMIT),
        cost_estimate=pl.CostEstimate(
            flops=2 * TOK // 2 * OUT_COLS * 4 * GCOLS, bytes_accessed=6 * 2**20, transcendentals=0
        ),
    )(place, mine, got, weights)


def reduce_over_z(far, up, down, stay, sign):
    near, back = (up, down) if sign > 0 else (down, up)
    passed = move(far, dz=sign)
    behind = move(back, dz=-sign)
    near = (near.astype(F32) + passed.astype(F32)).astype(BF16)
    ahead = move(near, dz=sign)
    return (stay.astype(F32) + ahead.astype(F32) + behind.astype(F32)).astype(BF16)


def per_device(hidden, span_ids, w_query, w_keyval, w_out):
    span, uly = lax.axis_index("span"), lax.axis_index("uly")
    xl, y, core = span // 8, (span // 2) % 4, span % 2
    z, xh = uly // 2, uly % 2
    as_int = lambda values: jnp.stack([jnp.asarray(v, jnp.int32) for v in values])

    chips = [x * 4 + (y + dy) % 4 for dy in (0, 3, 1, 2) for x in (xl, 1 - xl)]
    which = as_int([j * 2 + core for j in chips] + chips)
    place = as_int([z, xh])
    block_ids = span_ids.reshape(SPANS, TOK)[:, 0]
    seen = (block_ids <= block_ids[span]).astype(jnp.int32)
    order = [chips[at] * 2 + core for at in (0, 1, 2, 4, 3, 5, 6, 7)]
    seen = seen[as_int(order + [at + 1 - 2 * core for at in order])]
    send_flags = jnp.concatenate([seen, as_int([1 - xh])])
    mine_flags = jnp.concatenate([seen, as_int([xh])])

    query_weight = lax.all_gather(w_query[:, FIRST:], "span", axis=0, tiled=True)

    own = jnp.concatenate([w_keyval[:, 0], w_keyval[:, 1], w_query[:, :FIRST]], axis=1)
    side = move(own, swap_xl=True)
    up, down = move(own, dy=1), move(own, dy=-1)
    elsewhere = after(as_int([j * 2 + 1 - core for j in range(8)]), own)
    picked = pick_columns(hidden, elsewhere)
    side, up, down, picked = lax.optimization_barrier((side, up, down, picked))
    other_hidden = move(picked, swap_c=True)
    side_up, side_down = move(side, dy=1), move(side, dy=-1)
    up, side_up, side_down, other_hidden, which, place, send_flags, mine_flags = lax.optimization_barrier(
        (up, side_up, side_down, other_hidden, which, place, send_flags, mine_flags)
    )
    far, side_far = move(up, dy=1), move(side_down, dy=-1)

    planes = [
        [index_of(span // 8, span // 2 % 4, span % 2, at, side) for side in range(2) for span in range(SPANS)]
        for at in range(4)
    ]
    weights = lax.all_gather(
        after(w_out, far, side_far), BOTH, axis=0, tiled=True, axis_index_groups=planes
    )
    pieces = [own, side, up, side_up, down, side_down, far, side_far]
    joint_own, joint_other = project(hidden, other_hidden, which, pieces)
    joint_other = move(joint_other, swap_c=True)
    pair = (joint_own[:, : 2 * HEAD] + joint_other[:, : 2 * HEAD]).astype(BF16)
    first_queries = (joint_own[:, 2 * HEAD :] + joint_other[:, 2 * HEAD :]).astype(BF16)

    pair_side = move(pair, swap_xl=True)
    pair_up, pair_down = move(pair, dy=1), move(pair, dy=-1)
    pair_side, pair_up, pair_down, query_weight, first_queries = lax.optimization_barrier(
        (pair_side, pair_up, pair_down, query_weight, first_queries)
    )
    pair_side_up, pair_side_down = move(pair_up, swap_xl=True), move(pair_down, swap_xl=True)
    pair_far = move(pair_down, dy=-1)
    pairs = jnp.concatenate([pair, pair_side, pair_up, pair_down], axis=0)
    other_pairs = move(pairs, swap_c=True)
    queries = project_queries(hidden, query_weight)
    pair_far, pair_side_up, pair_side_down, queries = lax.optimization_barrier(
        (pair_far, pair_side_up, pair_side_down, queries)
    )
    pair_side_far = move(pair_far, swap_xl=True)
    more_pairs = jnp.concatenate([pair_side_up, pair_side_down, pair_far, pair_side_far], axis=0)
    pairs = [pairs, more_pairs, other_pairs, move(more_pairs, swap_c=True)]

    send = attend(send_flags, [first_queries, queries], pairs)
    got = move(send, swap_xh=True)
    mine = attend(after(mine_flags, send), [first_queries, queries], pairs)

    totals = []
    for group in range(OUT_GROUPS):
        parts = output_partial(group, place, mine, got, weights)
        totals.append(reduce_over_z(*parts, 1 if group % 2 == 0 else -1))
    return jnp.concatenate(totals, axis=1)


def solution(mesh):
    in_specs = (P("span", None), P(), P("span", "uly"), P("span", None, "uly"), P("uly", "span"))
    out_specs = P(("span", "uly"), None)
    return jax.shard_map(
        per_device, mesh=mesh, in_specs=in_specs, out_specs=out_specs, check_vma=False
    )
```
